32 devices in a mesh: seq: 16 (over z, y, x), res: 2 (over core).
Axes of the slice: x: 2, y: 2, z: 4, core: 2. Of those that a mesh axis runs over, the one named last changes fastest.
Arguments:
- alignment: bfloat16 [32, 128, 64], P('seq', 'res'), may hold values from -16 to 16
- cotangent: bfloat16 [32, 128, 64], P('seq', 'res'), may hold values from -6 to 6
- pair_bias: bfloat16 [8, 128, 128], P(None, 'res'), may hold values from -8 to 360
- norm_gains: float32 [2, 64], replicated, may hold values from 0.5 to 1.5
- row_project: float32 [64, 256], replicated, may hold values from -0.75 to 0.75
- row_output: float32 [64, 64], replicated, may hold values from -0.75 to 0.75
- column_project: float32 [64, 144], replicated, may hold values from -16 to 16
- column_output: float32 [64, 64], replicated, may hold values from -0.75 to 0.75
- residue_mask: int32 [128], P('res'), may hold values 0 or 1
- sequence_mask: int32 [32], P('seq'), may hold values from 0 to 1, as said below
Outputs:
- grad_alignment: bfloat16 [32, 128, 64], P('seq', 'res')
- grad_pair_bias: float32 [8, 128, 128], P(None, 'res', 'seq')
- grad_gains: float32 [2, 64], replicated
- grad_row_project: float32 [64, 256], replicated
- grad_row_output: float32 [64, 64], replicated
- grad_column_project: float32 [64, 144], replicated
- grad_column_output: float32 [64, 64], replicated
The draws below stay inside these ranges and needn't reach their ends.
Inputs may be any that keep to these rules, and one draw needn't show every extreme that they name: `sequence_mask`: at least one extra sequence is present.
All inputs are finite; a program needn't handle non-finite values. No bound on the sum of `residue_mask` on one device may be relied on, other than what follows from the above.
Results may differ from the reference program's by a relative error of at most 0.0027.
Values sent between devices are 32-bit elements; how exact they have to be, the bound alone decides.
No kernel may reach another device: no remote copies, remote signals or barrier semaphores. Data moves between devices by JAX's collectives and lax.ppermute only.
A program may use at most 128 MiB of HBM per device.

```python
import math
import jax
import jax.numpy as jnp
from jax import lax

C = 64
H = 8
DH = 8
SEQS = 32
RES = 128


def draw_alignment(key, part):
    key = jax.random.fold_in(key, 11)
    noise_part = jax.random.normal(jax.random.fold_in(key, 1), (SEQS, RES, C), jnp.float32)
    values = jnp.clip(noise_part, -8.0, 8.0)
    return values.astype(jnp.bfloat16)


def draw_pair_bias(key, part):
    key = jax.random.fold_in(key, 23)
    values = jnp.clip(1.5 * jax.random.normal(jax.random.fold_in(key, 1), (H, RES, RES), jnp.float32), -8.0, 8.0)
    return values.astype(jnp.bfloat16)


def draw_column_project(key, part):
    key = jax.random.fold_in(key, 37)
    values = jax.random.normal(jax.random.fold_in(key, 1), (C, 2 * C + 2 * DH), jnp.float32) / math.sqrt(C)
    return jnp.clip(values, -16.0, 16.0)


def draw_sequence_mask(key, part):
    key = jax.random.fold_in(key, 41)
    position = jnp.arange(SEQS, dtype=jnp.int32)
    threshold = 250 + 500 * position // SEQS
    rolled = jax.random.randint(key, (SEQS,), 0, 1000)
    present = (rolled < threshold).astype(jnp.int32)
    return jnp.where(position == SEQS - 1, 1, present)


def set_ends(array, stream_key, smallest, high):
    longest = array.shape.index(max(array.shape))
    spots = []
    for shift in (0, 1):
        where = [jax.random.randint(jax.random.fold_in(stream_key, axis), (), 0, length) for axis, length in enumerate(array.shape)]
        where[longest] = (where[longest] + shift) % array.shape[longest]
        spots.append(tuple(where))
    return array.at[spots[0]].set(smallest).at[spots[1]].set(high)


def levels(rng, shape, split, low, high):
    def one(axis_at, blocks):
        draws = jax.random.uniform(jax.random.fold_in(jax.random.fold_in(rng, 6), axis_at), (blocks,), jnp.float32, low / len(split), high / len(split))
        return jnp.repeat(jnp.exp(draws), shape[axis_at] // blocks).reshape((-1,) + (1,) * (len(shape) - axis_at - 1))

    level = one(*split[0])
    for cut in split[1:]:
        level = level * one(*cut)
    return level


def noise(stream_key, shape, deviation, bound, split=(), kind=jnp.bfloat16):
    loudness = levels(stream_key, shape, split, -0.22, 0.18) if split else 1.0
    entries = jax.random.normal(stream_key, shape, jnp.float32) * deviation * loudness
    return jnp.minimum(jnp.maximum(entries, -bound), bound).astype(kind)


def setup_inputs(seed: int = 0) -> dict:
    key_list = jax.random.split(jax.random.key(seed), 11)
    alignment = draw_alignment(jax.random.fold_in(key_list[10], 71), 0)
    cotangent = noise(key_list[1], (SEQS, RES, C), 1.0, 6.0, ((0, 16), (1, 2)))
    pair_bias = draw_pair_bias(jax.random.fold_in(key_list[10], 71), 0)
    norm_gains = jnp.clip(1.0 + 0.1 * jax.random.normal(key_list[3], (2, C), jnp.float32), 0.5, 1.5)
    row_project = noise(key_list[4], (C, 4 * C), C ** -0.5, 0.75, (), jnp.float32)
    row_output = noise(key_list[5], (C, C), C ** -0.5, 0.75, (), jnp.float32)
    column_project = draw_column_project(jax.random.fold_in(key_list[10], 71), 0)
    column_output = noise(key_list[7], (C, C), C ** -0.5, 0.75, (), jnp.float32)
    residue_mask = set_ends((jax.random.randint(key_list[8], (RES,), 0, 8) < 7).astype(jnp.int32), jax.random.fold_in(key_list[8], 1), 0, 1)
    sequence_mask = draw_sequence_mask(jax.random.fold_in(key_list[10], 71), 0)
    return {"alignment": alignment, "cotangent": cotangent, "pair_bias": pair_bias, "norm_gains": norm_gains, "row_project": row_project, "row_output": row_output, "column_project": column_project, "column_output": column_output, "residue_mask": residue_mask, "sequence_mask": sequence_mask}


PRECISE = lax.Precision.HIGHEST
EPSILON = 1e-05
MASKED = 1000000000.0

def layer_norm(values, gain_vector):
    centre = lax.optimization_barrier(jnp.mean(values, axis=-1, keepdims=True))
    centred = values - centre
    spread = lax.optimization_barrier(jnp.mean(centred * centred, axis=-1, keepdims=True))
    return centred * lax.rsqrt(spread + EPSILON) * gain_vector

def row_single(normed, row_project, row_output, bias_values, key_bias):
    projected = jnp.dot(normed, row_project, precision=PRECISE)
    queries = projected[:, :C].reshape(-1, H, DH) * DH ** (-0.5)
    key_rows = projected[:, C:2 * C].reshape(-1, H, DH)
    value_rows = projected[:, 2 * C:3 * C].reshape(-1, H, DH)
    gating = jax.nn.sigmoid(projected[:, 3 * C:])
    scores = jnp.einsum('qhd,khd->hqk', queries, key_rows, precision=PRECISE) + bias_values + key_bias[None, None, :]
    weights = jax.nn.softmax(scores, axis=-1)
    mixture = jnp.einsum('hqk,khd->qhd', weights, value_rows, precision=PRECISE).reshape(-1, C)
    return jnp.dot(gating * mixture, row_output, precision=PRECISE)

def column_global(normed, present, column_project, column_output):
    counted = jnp.sum(present)
    mean_normed = jnp.einsum('s,src->rc', present, normed, precision=PRECISE) / counted
    queries = jnp.dot(mean_normed, column_project[:, :C], precision=PRECISE).reshape(-1, H, DH) * DH ** (-0.5)
    key_rows = jnp.einsum('src,cd->srd', normed, column_project[:, C:C + DH], precision=PRECISE)
    value_rows = jnp.einsum('src,cd->srd', normed, column_project[:, C + DH:C + 2 * DH], precision=PRECISE)
    gating = jax.nn.sigmoid(jnp.einsum('src,cd->srd', normed, column_project[:, C + 2 * DH:], precision=PRECISE))
    scores = jnp.einsum('rhd,srd->srh', queries, key_rows, precision=PRECISE) + MASKED * (present - 1.0)[:, None, None]
    weights = jax.nn.softmax(scores, axis=0)
    mixture = jnp.einsum('srh,srd->rhd', weights, value_rows, precision=PRECISE).reshape(-1, C)
    return jnp.einsum('src,cd->srd', gating * mixture[None], column_output, precision=PRECISE)

def reference(alignment, cotangent, pair_bias, norm_gains, row_project, row_output, column_project, column_output, residue_mask, sequence_mask):
    key_bias = MASKED * (residue_mask.astype(jnp.float32) - 1.0)
    present = sequence_mask.astype(jnp.float32)
    row_step = jax.checkpoint(row_single)

    def forward(initial, bias_values, gains, row_weights, row_out_weights, column_weights, column_out_weights):
        normed = layer_norm(initial, gains[0])
        row_result = lax.map(lambda normed_row: row_step(normed_row, row_weights, row_out_weights, bias_values, key_bias), normed)
        middle = initial + row_result
        return middle + column_global(layer_norm(middle, gains[1]), present, column_weights, column_out_weights)
    primals = (alignment.astype(jnp.float32), pair_bias.astype(jnp.float32), norm_gains, row_project, row_output, column_project, column_output)
    outcome, backward = jax.vjp(forward, *primals)
    gradients = backward(cotangent.astype(jnp.float32))
    return (gradients[0].astype(jnp.bfloat16), gradients[1], gradients[2], gradients[3], gradients[4], gradients[5], gradients[6])
```

```python
import functools

import jax
import jax.numpy as jnp
from jax import lax
from jax.experimental import pallas as pl
from jax.experimental.pallas import tpu as pltpu
from jax.sharding import PartitionSpec as P

C = 64
H = 8
DH = 8
LANES = 128
TILE = 8
SLABS = 5

PRECISE = lax.Precision.HIGHEST
EPSILON = 1e-05
MASKED = 1000000000.0
SCALE = DH ** (-0.5)
F32 = jnp.float32


def dot(a, b, over=((1,), (0,))):
    return lax.dot_general(a, b, (over, ((), ())), precision=PRECISE, preferred_element_type=F32)


def dot_rows(a, b):
    return dot(a, b, ((0,), (0,)))


def dot_t(a, b):
    return dot(a, b, ((1,), (1,)))


def normalise(values):
    centred = values - jnp.mean(values, axis=-1, keepdims=True)
    inverse = lax.rsqrt(jnp.mean(centred * centred, axis=-1, keepdims=True) + EPSILON)
    return centred * inverse, inverse


def normalise_back(grad_normed, gain, unit, inverse):
    grad_unit = grad_normed * gain
    along = jnp.mean(grad_unit * unit, axis=-1, keepdims=True)
    return inverse * (grad_unit - jnp.mean(grad_unit, axis=-1, keepdims=True) - unit * along)


def head_mask(rows):
    row = lax.broadcasted_iota(jnp.int32, (H, rows, C), 0)
    channel = lax.broadcasted_iota(jnp.int32, (H, rows, C), 2)
    return (row == channel // DH).astype(F32).reshape(H * rows, C)


def spread_heads(values, mask):
    return jnp.concatenate([values] * H, axis=0) * mask


def join_heads(values, mask):
    masked = values * mask
    return jnp.sum(masked.reshape(H, -1, C), axis=0)


def row_forward(n_res, me, seq_mask, *refs):
    sent = refs[:n_res]
    own, cotangent, bias, gains, w_row, w_out = refs[n_res : n_res + 6]
    payload, weights_out, unit_out, memory_out, query_gate_out, mixture_out, gathered = refs[n_res + 6 :]
    n_seq, n_rows, _ = own.shape
    for away in range(n_res):
        gathered[lax.rem(me[0] + away, n_res)] = sent[away][...]
    n_keys = n_res * n_rows
    n_blocks = payload.shape[0]
    block = n_rows // n_blocks
    data_rows = n_seq * block
    gain = gains[0:1, :]
    w_all = w_row[...]
    residue = gathered[:, n_seq].reshape(n_keys, C)
    key_bias = MASKED * (jnp.transpose(residue)[0:1, :] - 1.0)
    bias_rows = bias[...].reshape(H * n_rows, n_keys).astype(F32)
    mask = head_mask(n_rows)
    for s in range(n_seq):
        unit, _ = normalise(gathered[:, s].reshape(n_keys, C))
        unit_out[s] = unit
        memory = dot(unit * gain, w_all[:, C : 3 * C])
        memory_out[s] = memory
        initial = own[s].astype(F32)
        own_unit, _ = normalise(initial)
        projected = dot(own_unit * gain, w_all)
        query = projected[:, :C] * SCALE
        gate = jax.nn.sigmoid(projected[:, 3 * C :])
        query_gate_out[s] = jnp.concatenate([query, gate], axis=1)
        scores = dot_t(spread_heads(query, mask), memory[:, :C]) + bias_rows + key_bias
        exponent = jnp.exp(scores - jnp.max(scores, axis=-1, keepdims=True))
        weights = exponent / jnp.sum(exponent, axis=-1, keepdims=True)
        weights_out[s] = weights
        mixture = join_heads(dot(weights, memory[:, C:]), mask)
        mixture_out[s] = mixture
        middle = initial + dot(gate * mixture, w_out[...])
        both = jnp.concatenate([middle, cotangent[s].astype(F32)], axis=1)
        for b in range(n_blocks):
            payload[b, s * block : (s + 1) * block, :] = both[b * block : (b + 1) * block, :]
        for b in range(n_blocks):
            payload[b, data_rows + s * block : data_rows + (s + 1) * block, :] = jnp.full(
                (block, 2 * C), seq_mask[s].astype(F32)
            )


def column_step(arrived, gains, w_col, w_out, returned, col_slab, rest_slab, out_grad, n_seq):
    n_src, both_rows, _ = arrived.shape
    group = both_rows // 2
    block = group // n_seq
    rows = n_src * group
    arrived_rows = arrived[...]
    data = arrived_rows[:, :group, :].reshape(rows, 2 * C)
    present = arrived_rows[:, group:, :C]
    middle = data[:, :C]
    cot = data[:, C:]
    gain = gains[1:2, :]

    def over_sequences(values, combine, reduce):
        total = reduce(values.reshape(n_src, group, C), axis=0)
        result = total
        for shift in range(1, n_seq):
            result = combine(result, pltpu.roll(total, shift * block, 0))
        return result

    def total_of(values):
        return over_sequences(values, jnp.add, jnp.sum)

    def spread(values):
        return jnp.broadcast_to(values[None], (n_src, group, C)).reshape(rows, C)

    lane = lax.broadcasted_iota(jnp.int32, (C, C), 1)
    row = lax.broadcasted_iota(jnp.int32, (C, C), 0)
    same_head = (row // DH == lane // DH).astype(F32)
    repeat = (lax.broadcasted_iota(jnp.int32, (DH, C), 0) == lax.broadcasted_iota(jnp.int32, (DH, C), 1) % DH).astype(F32)
    w_all = w_col[...]
    w_query = w_all[:, :C]
    w_key = dot(w_all[:, C : C + DH], repeat)
    w_value = dot(w_all[:, C + DH : C + 2 * DH], repeat)
    w_gate = w_all[:, C + 2 * DH :]
    w_rest = jnp.concatenate([w_key, w_value, w_gate], axis=1)

    unit, inverse = normalise(middle)
    normed = unit * gain
    present_rows = present.reshape(rows, C)
    counted = total_of(present_rows)
    mean_normed = total_of(present_rows * normed) / counted
    query = dot(mean_normed, w_query) * SCALE
    query_rows = spread(query)
    rest = dot(normed, w_rest)
    key, value = rest[:, :C], rest[:, C : 2 * C]
    gate = jax.nn.sigmoid(rest[:, 2 * C :])
    scores = dot(query_rows * key, same_head) + MASKED * (present_rows - 1.0)
    peak = over_sequences(scores, jnp.maximum, jnp.max)
    exponent = jnp.exp(scores - spread(peak))
    weights = exponent / spread(total_of(exponent))
    mixture = total_of(weights * value)
    mixture_rows = spread(mixture)

    grad_gated = dot_t(cot, w_out[...])
    out_grad[...] = dot_rows(gate * mixture_rows, cot)
    grad_mixture = total_of(gate * grad_gated)
    grad_mixture_rows = spread(grad_mixture)
    grad_gate = grad_gated * mixture_rows * gate * (1.0 - gate)
    grad_weights = dot(grad_mixture_rows * value, same_head)
    inner = spread(dot(grad_mixture * mixture, same_head))
    grad_scores = weights * (grad_weights - inner)
    grad_rest = jnp.concatenate([grad_scores * query_rows, weights * grad_mixture_rows, grad_gate], axis=1)
    grad_query = total_of(grad_scores * key) * SCALE
    grad_mean = dot_t(grad_query, w_query)
    grad_normed = present_rows * spread(grad_mean / counted) + dot_t(grad_rest, w_rest)
    grad_query_weights = dot_rows(mean_normed, grad_query) * (1.0 / n_seq)
    grad_rest_weights = dot_rows(normed, grad_rest)
    fold_row = lax.broadcasted_iota(jnp.int32, (2 * C, 2 * DH), 0)
    fold_lane = lax.broadcasted_iota(jnp.int32, (2 * C, 2 * DH), 1)
    fold = ((fold_row // C == fold_lane // DH) & (fold_row % DH == fold_lane % DH)).astype(F32)
    grad_key_value = dot(grad_rest_weights[:, : 2 * C], fold)
    col_slab[...] = jnp.concatenate([grad_query_weights, grad_rest_weights[:, 2 * C :]], axis=1)
    rest_slab[...] = jnp.zeros(rest_slab.shape, F32)
    rest_slab[:, : 2 * DH] = grad_key_value
    rest_slab[1:2, C:] = jnp.sum(grad_normed * unit, axis=0, keepdims=True)
    grad_middle = cot + normalise_back(grad_normed, gain, unit, inverse)
    returned[:, :, :C] = grad_middle.reshape(n_src, group, C)
    returned[:, :, C:] = jnp.zeros((n_src, group, C), F32)


def row_backward(n_res, me, returned, own, weights_in, unit_in, memory_in, query_gate_in, mixture_in, gains, w_row,
                 w_out, col_slab, rest_slab, col_out_grad, payload, middle_grad, *refs):
    grads_out, normed_grad, slab = refs[:n_res], refs[n_res], refs[n_res + 1]
    n_seq, n_rows, _ = own.shape
    n_keys = memory_in.shape[1]
    n_blocks, group, _ = returned.shape
    block = group // n_seq
    gain = gains[0:1, :]
    w_all = w_row[...]
    w_memory = w_all[:, C : 3 * C]
    w_query_gate = jnp.concatenate([w_all[:, :C], w_all[:, 3 * C :]], axis=1)
    mask = head_mask(n_rows)
    for b in range(n_blocks):
        for s in range(n_seq):
            middle_grad[s, b * block : (b + 1) * block, :] = returned[b, s * block : (s + 1) * block, :C]
    slab[...] = jnp.zeros(slab.shape, F32)
    grad_out = jnp.zeros((C, C), F32)
    grad_query_gate_weights = jnp.zeros((C, 2 * C), F32)
    grad_memory_weights = jnp.zeros((C, 2 * C), F32)
    grad_gain = jnp.zeros((1, C), F32)
    bias_grad = jnp.zeros((H * n_rows, n_keys), F32)
    for s in range(n_seq):
        grad_middle = middle_grad[s]
        query = query_gate_in[s, :, :C]
        gate = query_gate_in[s, :, C:]
        mixture = mixture_in[s]
        memory = memory_in[s]
        weights = weights_in[s]
        grad_gated = dot_t(grad_middle, w_out[...])
        grad_out = grad_out + dot_rows(gate * mixture, grad_middle)
        grad_gate = grad_gated * mixture * gate * (1.0 - gate)
        grad_heads = spread_heads(grad_gated * gate, mask)
        query_heads = spread_heads(query, mask)
        inner = grad_heads * jnp.concatenate([mixture] * H, axis=0)
        left = jnp.concatenate([grad_heads, inner], axis=1)
        right = jnp.concatenate([memory[:, C:], jnp.full((n_keys, C), -1.0, F32)], axis=1)
        grad_scores = weights * dot_t(left, right)
        bias_grad = bias_grad + grad_scores
        grad_query = join_heads(dot(grad_scores, memory[:, :C]), mask) * SCALE
        grad_key = dot_rows(grad_scores, query_heads)
        grad_value = dot_rows(weights, grad_heads)
        grad_memory = jnp.concatenate([grad_key, grad_value], axis=1)
        grad_query_gate = jnp.concatenate([grad_query, grad_gate], axis=1)
        own_unit, _ = normalise(own[s].astype(F32))
        unit = unit_in[s]
        grad_query_gate_weights = grad_query_gate_weights + dot_rows(own_unit * gain, grad_query_gate)
        grad_memory_weights = grad_memory_weights + dot_rows(unit * gain, grad_memory)
        from_memory = dot_t(grad_memory, w_memory)
        from_own = dot_t(grad_query_gate, w_query_gate)
        grad_gain = grad_gain + jnp.sum(from_memory * unit, axis=0, keepdims=True)
        grad_gain = grad_gain + jnp.sum(from_own * own_unit, axis=0, keepdims=True)
        normed_grad[:, s] = from_memory.reshape(-1, n_rows, C)
        grads_out[0][s] = from_own
    grads_out[0][...] += normed_grad[me[0]]
    for away in range(1, n_res):
        grads_out[away][...] = normed_grad[lax.rem(me[0] + away, n_res)]
    slab[0:C, :] = grad_query_gate_weights
    slab[C : 2 * C, :] = grad_memory_weights
    slab[2 * C : 3 * C, :] = col_slab[...]
    slab[3 * C : 4 * C, :] = jnp.concatenate([grad_out, col_out_grad[...]], axis=1)
    slab[4 * C : 5 * C, :] = rest_slab[...]
    slab[4 * C : 4 * C + 1, C:] = grad_gain
    bias_t = jnp.transpose(bias_grad)
    keys_each = n_keys // n_blocks
    tiles = H * n_rows // LANES
    piece = slab.shape[0] // n_blocks
    for b in range(n_blocks):
        for t in range(tiles):
            payload[b, t * keys_each : (t + 1) * keys_each, :] = bias_t[
                b * keys_each : (b + 1) * keys_each, t * LANES : (t + 1) * LANES
            ]
        payload[b, tiles * keys_each :, :] = slab[b * piece : (b + 1) * piece, :]


def finish_alignment(own, middle_grad, gains, *refs):
    parts, out = refs[:-1], refs[-1]
    n_seq = own.shape[0]
    for s in range(n_seq):
        unit, inverse = normalise(own[s].astype(F32))
        grad_normed = parts[0][s]
        for part in parts[1:]:
            grad_normed = grad_normed + part[s]
        out[s] = (middle_grad[s] + normalise_back(grad_normed, gains[0:1, :], unit, inverse)).astype(out.dtype)


def add_arrivals(arrived, bias_out, piece_out):
    total = jnp.sum(arrived[...], axis=0)
    _, keys_each, n_rows = bias_out.shape
    each = LANES // n_rows
    tiles = H // each
    for t in range(tiles):
        for u in range(each):
            bias_out[t * each + u] = total[t * keys_each : (t + 1) * keys_each, u * n_rows : (u + 1) * n_rows]
    piece_out[...] = total[tiles * keys_each :, :]


def unpack(slab, gains_out, row_project_out, row_out_out, col_project_out, col_out_out):
    values = slab[...].reshape(-1, LANES)
    query_gate = values[0:C]
    row_project_out[:, :C] = query_gate[:, :C]
    row_project_out[:, C : 3 * C] = values[C : 2 * C]
    row_project_out[:, 3 * C :] = query_gate[:, C:]
    col_query_gate = values[2 * C : 3 * C]
    rest = values[4 * C : 5 * C]
    col_project_out[:, :C] = col_query_gate[:, :C]
    col_project_out[:, C : C + 2 * DH] = rest[:, : 2 * DH]
    col_project_out[:, C + 2 * DH :] = col_query_gate[:, C:]
    outs = values[3 * C : 4 * C]
    row_out_out[...] = outs[:, :C]
    col_out_out[...] = outs[:, C:]
    gains_out[...] = rest[0:2, C:]


def call(body, outs, *operands, smem=0, scratch=(), name):
    vmem = pl.BlockSpec(memory_space=pltpu.VMEM)
    scalar = pl.BlockSpec(memory_space=pltpu.SMEM)
    return pl.pallas_call(
        body,
        out_shape=[jax.ShapeDtypeStruct(shape, kind) for shape, kind in outs],
        in_specs=[scalar] * smem + [vmem] * (len(operands) - smem),
        out_specs=[vmem] * len(outs),
        scratch_shapes=list(scratch),
        compiler_params=pltpu.CompilerParams(vmem_limit_bytes=48 * 1024 * 1024),
        name=name,
    )(*operands)


def shift_residues(values, away, count):
    return lax.ppermute(values, "res", [((i + away) % count, i) for i in range(count)])


def swap_blocks(values):
    return lax.all_to_all(values, "seq", 0, 0, tiled=True)


def local(
    alignment,
    cotangent,
    pair_bias,
    norm_gains,
    row_project,
    row_output,
    column_project,
    column_output,
    residue_mask,
    sequence_mask,
    seq_count,
    res_count,
):
    n_seq, n_rows, _ = alignment.shape
    n_keys = pair_bias.shape[2]
    block = n_rows // seq_count
    group = n_seq * block
    present_keys = jnp.broadcast_to(residue_mask.astype(F32)[None, :, None], (1, n_rows, C))
    sent = jnp.concatenate([alignment.astype(F32), present_keys], axis=0)
    sent = [sent] + [shift_residues(sent, away, res_count) for away in range(1, res_count)]
    me = jnp.reshape(lax.axis_index("res"), (1,))
    payload, weights, unit, memory, query_gate, mixture = call(
        functools.partial(row_forward, res_count),
        [
            ((seq_count, 2 * group, 2 * C), F32),
            ((n_seq, H * n_rows, n_keys), F32),
            ((n_seq, n_keys, C), F32),
            ((n_seq, n_keys, 2 * C), F32),
            ((n_seq, n_rows, 2 * C), F32),
            ((n_seq, n_rows, C), F32),
        ],
        me, sequence_mask, *sent, alignment, cotangent, pair_bias, norm_gains, row_project, row_output,
        smem=2,
        scratch=[pltpu.VMEM((res_count, n_seq + 1, n_rows, C), F32)],
        name="row_forward",
    )
    arrived = swap_blocks(payload)
    returned, col_slab, rest_slab, col_out_grad = call(
        functools.partial(column_step, n_seq=n_seq),
        [((seq_count, group, 2 * C), F32), ((C, 2 * C), F32), ((C, 2 * C), F32), ((C, C), F32)],
        arrived, norm_gains, column_project, column_output,
        name="column_step",
    )
    returned = swap_blocks(returned)
    bias_rows = H * n_rows // LANES * (n_keys // seq_count)
    piece = -(-SLABS * C // (TILE * seq_count)) * TILE
    payload, middle_grad, *parts = call(
        functools.partial(row_backward, res_count),
        [((seq_count, bias_rows + piece, LANES), F32)] + [((n_seq, n_rows, C), F32)] * (res_count + 1),
        me, returned, alignment, weights, unit, memory, query_gate, mixture, norm_gains,
        row_project, row_output, col_slab, rest_slab, col_out_grad,
        smem=1,
        scratch=[pltpu.VMEM((res_count, n_seq, n_rows, C), F32), pltpu.VMEM((piece * seq_count, LANES), F32)],
        name="row_backward",
    )
    parts = parts[:1] + [shift_residues(parts[away], -away, res_count) for away in range(1, res_count)]
    arrived = swap_blocks(payload)
    (grad_alignment,) = call(
        finish_alignment,
        [(alignment.shape, alignment.dtype)],
        alignment, middle_grad, norm_gains, *parts,
        name="finish_alignment",
    )
    bias_grad, summed = call(
        add_arrivals,
        [((H, n_keys // seq_count, n_rows), F32), ((piece, LANES), F32)],
        arrived,
        name="add_arrivals",
    )
    others = [shift_residues(summed, away, res_count) for away in range(1, res_count)]
    summed = functools.reduce(jnp.add, others, summed)
    slab = swap_blocks(jnp.broadcast_to(summed[None], (seq_count, piece, LANES)))
    grads = call(
        unpack,
        [((2, C), F32), ((C, 4 * C), F32), ((C, C), F32), ((C, 2 * C + 2 * DH), F32), ((C, C), F32)],
        slab,
        name="unpack",
    )
    return (grad_alignment, jnp.transpose(bias_grad, (0, 2, 1)), *grads)


def solution(mesh):
    placed = (
        P("seq", "res", None),
        P("seq", "res", None),
        P(None, "res", None),
        P(),
        P(),
        P(),
        P(),
        P(),
        P("res"),
        P("seq"),
    )
    return jax.shard_map(
        functools.partial(local, seq_count=mesh.shape["seq"], res_count=mesh.shape["res"]),
        mesh=mesh,
        in_specs=placed,
        out_specs=(P("seq", "res", None), P(None, "res", "seq"), P(), P(), P(), P(), P()),
        check_vma=False,
    )
```

```python
import functools

import jax
import jax.numpy as jnp
from jax import lax
from jax.experimental import pallas as pl
from jax.experimental.pallas import tpu as pltpu
from jax.sharding import PartitionSpec as P

C = 64
H = 8
DH = 8
LANES = 128
ROWS = 8
FOUR = 4
WIDE = FOUR * LANES
SLABS = 5

EXACT = lax.Precision.HIGHEST
THREE = lax.Precision.HIGH
EPSILON = 1e-05
MASKED = 1000000000.0
SCALE = DH ** (-0.5)
F32 = jnp.float32


def dot(a, b, over=((1,), (0,)), precision=THREE):
    return lax.dot_general(a, b, (over, ((), ())), precision=precision, preferred_element_type=F32)


def dot_rows(a, b):
    return dot(a, b, ((0,), (0,)))


def dot_t(a, b, precision=THREE):
    return dot(a, b, ((1,), (1,)), precision)


def tile(blocks, at):
    return blocks[at // FOUR, :, at % FOUR * LANES : (at % FOUR + 1) * LANES]


def put_tiles(blocks, first, values):
    for i in range(values.shape[0] // ROWS):
        at = first + i
        blocks[at // FOUR, :, at % FOUR * LANES : (at % FOUR + 1) * LANES] = values[i * ROWS : (i + 1) * ROWS, :]


def take_tiles(blocks, first, count):
    return jnp.concatenate([tile(blocks, first + i) for i in range(count)], axis=0)


def to_column(row):
    eye = lax.broadcasted_iota(jnp.int32, (C, C), 0) == lax.broadcasted_iota(jnp.int32, (C, C), 1)
    return jnp.sum(jnp.where(eye, row, 0.0), axis=1, keepdims=True)


def to_row(column):
    eye = lax.broadcasted_iota(jnp.int32, (C, C), 0) == lax.broadcasted_iota(jnp.int32, (C, C), 1)
    return jnp.sum(jnp.where(eye, column, 0.0), axis=0, keepdims=True)


def normalise(values):
    centred = values - jnp.mean(values, axis=-1, keepdims=True)
    inverse = lax.rsqrt(jnp.mean(centred * centred, axis=-1, keepdims=True) + EPSILON)
    return centred * inverse, inverse


def normalise_back(grad_normed, gain, unit, inverse):
    grad_unit = grad_normed * gain
    along = jnp.mean(grad_unit * unit, axis=-1, keepdims=True)
    return inverse * (grad_unit - jnp.mean(grad_unit, axis=-1, keepdims=True) - unit * along)


def head_mask(rows):
    row = lax.broadcasted_iota(jnp.int32, (H, rows, C), 0)
    channel = lax.broadcasted_iota(jnp.int32, (H, rows, C), 2)
    return (row == channel // DH).astype(F32).reshape(H * rows, C)


def spread_heads(values, mask):
    return jnp.concatenate([values] * H, axis=0) * mask


def join_heads(values, mask):
    masked = values * mask
    return jnp.sum(masked.reshape(H, -1, C), axis=0)


def near_size(count):
    return 1 << (count.bit_length() // 2)


def row_forward(n_res, seq_mask, *refs):
    sent = refs[:n_res]
    own, cotangent, bias, gains, w_row, w_out = refs[n_res : n_res + 6]
    payload, weights_out, unit_out, own_unit_out, memory_out, query_gate_out, mixture_out, gathered = refs[n_res + 6 :]
    n_seq, n_rows, _ = own.shape
    me = lax.axis_index("res")
    for away in range(n_res):
        gathered[lax.rem(me + away, n_res)] = sent[away][...]
    n_keys = n_res * n_rows
    n_blocks = payload.shape[0]
    block = n_rows // n_blocks
    near = near_size(n_blocks)
    gain = gains[0:1, :]
    w_all = w_row[...]
    w_query_gate = jnp.concatenate([w_all[:, :C], w_all[:, 3 * C :]], axis=1)
    residue = gathered[:, n_seq].reshape(n_keys, C)
    key_bias = MASKED * (jnp.transpose(residue)[0:1, :] - 1.0)
    bias_rows = bias[...].reshape(H * n_rows, n_keys).astype(F32)
    mask = head_mask(n_rows)
    for s in range(n_seq):
        unit, _ = normalise(gathered[:, s].reshape(n_keys, C))
        unit_out[s] = unit
        memory = dot(unit * gain, w_all[:, C : 3 * C], precision=EXACT)
        memory_out[s] = memory
        initial = own[s].astype(F32)
        own_unit, _ = normalise(initial)
        own_unit_out[s] = own_unit
        projected = dot(own_unit * gain, w_query_gate, precision=EXACT)
        query = projected[:, :C] * SCALE
        gate = jax.nn.sigmoid(projected[:, C:])
        query_gate_out[s] = jnp.concatenate([query, gate], axis=1)
        scores = dot_t(spread_heads(query, mask), memory[:, :C], EXACT) + bias_rows + key_bias
        exponent = jnp.exp(scores - jnp.max(scores, axis=-1, keepdims=True))
        weights = exponent / jnp.sum(exponent, axis=-1, keepdims=True)
        weights_out[s] = weights
        mixture = join_heads(dot(weights, memory[:, C:]), mask)
        mixture_out[s] = mixture
        middle = initial + dot(gate * mixture, w_out[...])
        both = jnp.concatenate([middle, cotangent[s].astype(F32)], axis=1)
        for b in range(n_blocks):
            payload[b % near * (n_blocks // near) + b // near, s] = both[b * block : (b + 1) * block, :]
    lane = lax.broadcasted_iota(jnp.int32, (block, 2 * C), 1) // (2 * C // n_seq)
    present = jnp.zeros((block, 2 * C), F32)
    for s in range(n_seq):
        present = jnp.where(lane == s, seq_mask[s].astype(F32), present)
    for b in range(n_blocks):
        payload[b, n_seq] = present


def column_step(arrived, gains, w_col, w_out, returned, col_slab, rest_slab, out_grad, gathered, mask_rows, n_seq):
    n_src, _, block, _ = arrived.shape
    group = n_seq * block
    rows = n_src * group
    wide = 2 * C // n_seq
    for src in range(n_src):
        for s in range(n_seq):
            gathered[src, s * block : (s + 1) * block, :] = arrived[src, s]
            mask_rows[src, s * block : (s + 1) * block, :] = jnp.broadcast_to(
                arrived[src, n_seq, :, s * wide : s * wide + 1], (block, C)
            )
    data = gathered[...].reshape(rows, 2 * C)
    present = mask_rows[...]
    middle = data[:, :C]
    cot = data[:, C:]
    gain = gains[1:2, :]

    def over_sequences(values, combine, reduce):
        total = reduce(values.reshape(n_src, group, C), axis=0)
        result = total
        for shift in range(1, n_seq):
            result = combine(result, pltpu.roll(total, shift * block, 0))
        return result

    def total_of(values):
        return over_sequences(values, jnp.add, jnp.sum)

    def spread(values):
        return jnp.broadcast_to(values[None], (n_src, group, C)).reshape(rows, C)

    lane = lax.broadcasted_iota(jnp.int32, (C, C), 1)
    row = lax.broadcasted_iota(jnp.int32, (C, C), 0)
    same_head = (row // DH == lane // DH).astype(F32)
    repeat = (lax.broadcasted_iota(jnp.int32, (DH, C), 0) == lax.broadcasted_iota(jnp.int32, (DH, C), 1) % DH).astype(F32)
    w_all = w_col[...]
    w_query = w_all[:, :C]
    w_key = dot(w_all[:, C : C + DH], repeat, precision=EXACT)
    w_value = dot(w_all[:, C + DH : C + 2 * DH], repeat)
    w_gate = w_all[:, C + 2 * DH :]
    w_rest = jnp.concatenate([w_key, w_value, w_gate], axis=1)

    unit, inverse = normalise(middle)
    normed = unit * gain
    present_rows = present.reshape(rows, C)
    counted = total_of(present_rows)
    mean_unit = total_of(present_rows * unit) / counted
    mean_normed = mean_unit * gain
    query = dot(mean_normed, w_query, precision=EXACT) * SCALE
    query_rows = spread(query)
    rest = dot(normed, w_rest, precision=EXACT)
    key, value = rest[:, :C], rest[:, C : 2 * C]
    gate = jax.nn.sigmoid(rest[:, 2 * C :])
    scores = dot(query_rows * key, same_head, precision=EXACT) + MASKED * (present_rows - 1.0)
    peak = over_sequences(scores, jnp.maximum, jnp.max)
    exponent = jnp.exp(scores - spread(peak))
    weights = exponent / spread(total_of(exponent))
    mixture = total_of(weights * value)
    mixture_rows = spread(mixture)

    grad_gated = dot_t(cot, w_out[...])
    out_grad[...] = dot_rows(gate * mixture_rows, cot)
    grad_mixture = total_of(gate * grad_gated)
    grad_mixture_rows = spread(grad_mixture)
    grad_gate = grad_gated * mixture_rows * gate * (1.0 - gate)
    grad_weights = dot(grad_mixture_rows * value, same_head)
    inner = spread(dot(grad_mixture * mixture, same_head))
    grad_scores = weights * (grad_weights - inner)
    grad_rest = jnp.concatenate([grad_scores * query_rows, weights * grad_mixture_rows, grad_gate], axis=1)
    grad_query = total_of(grad_scores * key) * SCALE
    grad_mean = dot_t(grad_query, w_query)
    grad_normed = present_rows * spread(grad_mean / counted) + dot_t(grad_rest, w_rest)
    grad_query_weights = dot_rows(mean_unit, grad_query) * (1.0 / n_seq)
    grad_rest_weights = dot_rows(unit, grad_rest)
    fold_row = lax.broadcasted_iota(jnp.int32, (2 * C, 2 * DH), 0)
    fold_lane = lax.broadcasted_iota(jnp.int32, (2 * C, 2 * DH), 1)
    fold = ((fold_row // C == fold_lane // DH) & (fold_row % DH == fold_lane % DH)).astype(F32)
    grad_key_value = dot(grad_rest_weights[:, : 2 * C], fold)
    col_slab[...] = jnp.concatenate([grad_query_weights, grad_rest_weights[:, 2 * C :]], axis=1)
    rest_slab[...] = jnp.zeros(rest_slab.shape, F32)
    rest_slab[:, : 2 * DH] = grad_key_value
    grad_middle = (cot + normalise_back(grad_normed, gain, unit, inverse)).reshape(n_src, group, C)
    for src in range(n_src):
        for s in range(n_seq):
            returned[src, :, s * C : (s + 1) * C] = grad_middle[src, s * block : (s + 1) * block, :]


def row_backward(n_res, returned, weights_in, unit_in, memory_in, query_gate_in, mixture_in, own_unit_in, gains,
                 w_row, w_out, col_slab, rest_slab, col_out_grad, bias_out, middle_grad, *refs):
    sums_out, shares = refs[:n_res], refs[n_res]
    me = lax.axis_index("res")
    n_seq, n_rows, _ = middle_grad.shape
    n_keys = memory_in.shape[1]
    n_blocks, block, _ = returned.shape
    near = near_size(n_blocks)
    gain = gains[0:1, :]
    w_all = w_row[...]
    w_memory = w_all[:, C : 3 * C]
    w_query_gate = jnp.concatenate([w_all[:, :C], w_all[:, 3 * C :]], axis=1)
    mask = head_mask(n_rows)
    for b in range(n_blocks):
        for s in range(n_seq):
            at = b % near * (n_blocks // near) + b // near
            middle_grad[s, b * block : (b + 1) * block, :] = returned[at, :, s * C : (s + 1) * C]
    grad_out = jnp.zeros((C, C), F32)
    grad_query_gate_weights = jnp.zeros((C, 2 * C), F32)
    grad_memory_weights = jnp.zeros((C, 2 * C), F32)
    bias_grad = jnp.zeros((H * n_rows, n_keys), F32)
    from_own = []
    from_memory = []
    for s in range(n_seq):
        grad_middle = middle_grad[s]
        query = query_gate_in[s, :, :C]
        gate = query_gate_in[s, :, C:]
        mixture = mixture_in[s]
        memory = memory_in[s]
        weights = weights_in[s]
        grad_gated = dot_t(grad_middle, w_out[...])
        grad_out = grad_out + dot_rows(gate * mixture, grad_middle)
        grad_gate = grad_gated * mixture * gate * (1.0 - gate)
        grad_heads = spread_heads(grad_gated * gate, mask)
        query_heads = spread_heads(query, mask)
        inner = grad_heads * jnp.concatenate([mixture] * H, axis=0)
        left = jnp.concatenate([grad_heads, inner], axis=1)
        right = jnp.concatenate([memory[:, C:], jnp.full((n_keys, C), -1.0, F32)], axis=1)
        grad_scores = weights * dot_t(left, right)
        bias_grad = bias_grad + grad_scores
        grad_query = join_heads(dot(grad_scores, memory[:, :C]), mask) * SCALE
        grad_key = dot_rows(grad_scores, query_heads)
        grad_value = dot_rows(weights, grad_heads)
        grad_memory = jnp.concatenate([grad_key, grad_value], axis=1)
        grad_query_gate = jnp.concatenate([grad_query, grad_gate], axis=1)
        grad_query_gate_weights = grad_query_gate_weights + dot_rows(own_unit_in[s], grad_query_gate)
        grad_memory_weights = grad_memory_weights + dot_rows(unit_in[s], grad_memory)
        from_memory.append(dot_t(grad_memory, w_memory))
        from_own.append(dot_t(grad_query_gate, w_query_gate))
    bias_out[...] = jnp.transpose(bias_grad)
    slabs = (
        grad_query_gate_weights,
        grad_memory_weights,
        col_slab[...],
        jnp.concatenate([grad_out, col_out_grad[...]], axis=1),
        rest_slab[...],
    )
    normed_tiles = n_rows // ROWS
    part = shares.shape[1] * FOUR - normed_tiles
    shares[...] = jnp.zeros(shares.shape, F32)
    for i, values in enumerate(slabs):
        for k in range(C // ROWS):
            at = i * (C // ROWS) + k
            put_tiles(shares.at[at // part], at % part, values[k * ROWS : (k + 1) * ROWS, :])
    normed = jnp.concatenate(from_memory, axis=1)
    for i in range(n_res):
        put_tiles(shares.at[i], part, normed[i * n_rows : (i + 1) * n_rows, :])
    for away in range(n_res):
        sums_out[away][...] = shares[lax.rem(me + away, n_res)]
    own_normed = take_tiles(sums_out[0], part, normed_tiles) + jnp.concatenate(from_own, axis=1)
    put_tiles(sums_out[0], part, own_normed)


def step_bits(n_seq_devices, odd):
    bits = list(range(n_seq_devices.bit_length() - 1))
    if odd:
        for i in range(0, len(bits) - 1, 2):
            bits[i], bits[i + 1] = bits[i + 1], bits[i]
    return bits


def slot_mask(slot, bits):
    last = len(bits) - 1
    return sum(1 << bit for step, bit in enumerate(bits) if slot >> (last - step) & 1)


def combine(n_blocks, own, middle_grad, bias_grad, gains, *refs):
    sums, state, send, out = refs[:-3], refs[-3], refs[-2], refs[-1]
    n_seq, n_rows, _ = own.shape
    total = sums[0][...]
    for more in sums[1:]:
        total = total + more[...]
    shared = state.shape[0] - n_blocks
    part = shared * FOUR
    normed = take_tiles(total, part, n_rows // ROWS)
    for s in range(n_seq):
        unit, inverse = normalise(own[s].astype(F32))
        grad_normed = normed[:, s * C : (s + 1) * C]
        out[s] = (middle_grad[s] + normalise_back(grad_normed, gains[0:1, :], unit, inverse)).astype(out.dtype)
    place = lax.axis_index("seq")
    odd = lax.rem(lax.axis_index("res"), 2)
    even_bits, odd_bits = step_bits(n_blocks, False), step_bits(n_blocks, True)
    half = n_blocks // 2
    for slot in range(n_blocks):
        even_mask, odd_mask = slot_mask(slot, even_bits), slot_mask(slot, odd_bits)
        block = place ^ (even_mask + odd * (odd_mask - even_mask))
        values = bias_grad[pl.ds(pl.multiple_of(block * ROWS, ROWS), ROWS), :]
        if slot < half:
            state[slot] = values
        else:
            send[slot - half] = values
    state[n_blocks:] = total[:shared]
    send[half:] = total[:shared]


def step(left, state, arrived, state_out, send_out):
    half = left // 2
    blocks = state[:left] + arrived[:left]
    shared = state[state.shape[0] - (arrived.shape[0] - left) :] + arrived[left:]
    state_out[:left] = blocks
    state_out[left:] = shared
    send_out[:half] = blocks[half:]
    send_out[half:] = shared


def last_step(state, arrived, bias_out, shared_out):
    total = state[0] + arrived[0]
    shared_out[...] = state[state.shape[0] - shared_out.shape[0] :] + arrived[1:]
    heads, _, n_rows = bias_out.shape
    for h in range(heads):
        bias_out[h] = total[:, h * n_rows : (h + 1) * n_rows]


def unpack(n_res, *refs):
    parts = refs[:n_res]
    gains, w_row, w_col, gains_out, row_project_out, row_out_out, col_project_out, col_out_out, shares = refs[n_res:]
    me = lax.axis_index("res")
    for away in range(n_res):
        shares[lax.rem(me + away, n_res)] = parts[away][...]
    part = shares.shape[1] * FOUR
    each = C // ROWS
    slabs = [
        jnp.concatenate([tile(shares.at[at // part], at % part) for at in range(i * each, (i + 1) * each)], axis=0)
        for i in range(SLABS)
    ]
    gain_row = to_column(gains[0:1, :])
    gain_col = to_column(gains[1:2, :])
    w_all = w_row[...]
    w_column = w_col[...]
    query_gate, memory, col_query_gate, outs, rest = slabs
    rest = rest[:, : 2 * DH]
    row_gain_grad = (
        jnp.sum(query_gate[:, :C] * w_all[:, :C], axis=1, keepdims=True)
        + jnp.sum(memory * w_all[:, C : 3 * C], axis=1, keepdims=True)
        + jnp.sum(query_gate[:, C:] * w_all[:, 3 * C :], axis=1, keepdims=True)
    )
    col_gain_grad = (
        jnp.sum(col_query_gate[:, :C] * w_column[:, :C], axis=1, keepdims=True)
        + jnp.sum(rest * w_column[:, C : C + 2 * DH], axis=1, keepdims=True)
        + jnp.sum(col_query_gate[:, C:] * w_column[:, C + 2 * DH :], axis=1, keepdims=True)
    )
    gains_out[0:1, :] = to_row(row_gain_grad)
    gains_out[1:2, :] = to_row(col_gain_grad)
    row_project_out[:, :C] = query_gate[:, :C] * gain_row
    row_project_out[:, C : 3 * C] = memory * gain_row
    row_project_out[:, 3 * C :] = query_gate[:, C:] * gain_row
    col_project_out[:, :C] = col_query_gate[:, :C] * gain_col
    col_project_out[:, C : C + 2 * DH] = rest * gain_col
    col_project_out[:, C + 2 * DH :] = col_query_gate[:, C:] * gain_col
    row_out_out[...] = outs[:, :C]
    col_out_out[...] = outs[:, C:]


def call(body, outs, *operands, smem=0, scratch=(), name):
    vmem = pl.BlockSpec(memory_space=pltpu.VMEM)
    scalar = pl.BlockSpec(memory_space=pltpu.SMEM)
    return pl.pallas_call(
        body,
        out_shape=[jax.ShapeDtypeStruct(shape, kind) for shape, kind in outs],
        in_specs=[scalar] * smem + [vmem] * (len(operands) - smem),
        out_specs=[vmem] * len(outs),
        scratch_shapes=list(scratch),
        compiler_params=pltpu.CompilerParams(vmem_limit_bytes=32 * 1024 * 1024),
        name=name,
    )(*operands)


def shift_residues(values, away, count):
    return lax.ppermute(values, "res", [((i + away) % count, i) for i in range(count)])


def cross(values, at, seq_count, res_count):
    pairs = []
    for r in range(res_count):
        bit = 1 << step_bits(seq_count, r % 2)[at]
        pairs += [(i * res_count + r, (i ^ bit) * res_count + r) for i in range(seq_count)]
    return lax.ppermute(values, ("seq", "res"), pairs)


def regroup(source, out):
    for i in range(source.shape[0]):
        for j in range(source.shape[1]):
            out[j, i] = source[i, j]


def swap_groups(values, groups):
    return lax.all_to_all(values, "seq", 0, 0, axis_index_groups=groups, tiled=True)


def swap_blocks(values, near_first):
    count = values.shape[0]
    near = near_size(count)
    far = count // near
    near_groups = [[f * near + n for n in range(near)] for f in range(far)]
    far_groups = [[f * near + n for f in range(far)] for n in range(near)]
    shape = values.shape[1:]
    if near_first:
        first, second, sizes = near_groups, far_groups, (near, far)
    else:
        first, second, sizes = far_groups, near_groups, (far, near)
    values = swap_groups(values.reshape(sizes + shape), first)
    (values,) = call(regroup, [(sizes[::-1] + shape, values.dtype)], values, name="regroup")
    return swap_groups(values, second)


def local(
    alignment,
    cotangent,
    pair_bias,
    norm_gains,
    row_project,
    row_output,
    column_project,
    column_output,
    residue_mask,
    sequence_mask,
    seq_count,
    res_count,
):
    n_seq, n_rows, _ = alignment.shape
    n_keys = pair_bias.shape[2]
    block = n_rows // seq_count
    group = n_seq * block
    away_range = range(1, res_count)
    present_keys = jnp.broadcast_to(residue_mask.astype(F32)[None, :, None], (1, n_rows, C))
    sent = jnp.concatenate([alignment.astype(F32), present_keys], axis=0)
    payload, weights, unit, own_unit, memory, query_gate, mixture = call(
        functools.partial(row_forward, res_count),
        [
            ((seq_count, n_seq + 1, block, 2 * C), F32),
            ((n_seq, H * n_rows, n_keys), F32),
            ((n_seq, n_keys, C), F32),
            ((n_seq, n_rows, C), F32),
            ((n_seq, n_keys, 2 * C), F32),
            ((n_seq, n_rows, 2 * C), F32),
            ((n_seq, n_rows, C), F32),
        ],
        sequence_mask, sent, *[shift_residues(sent, away, res_count) for away in away_range],
        alignment, cotangent, pair_bias, norm_gains, row_project, row_output,
        smem=1,
        scratch=[pltpu.VMEM((res_count, n_seq + 1, n_rows, C), F32)],
        name="row_forward",
    )
    arrived = swap_blocks(payload, True).reshape(payload.shape)
    returned, col_slab, rest_slab, col_out_grad = call(
        functools.partial(column_step, n_seq=n_seq),
        [((seq_count, block, n_seq * C), F32), ((C, 2 * C), F32), ((C, 2 * C), F32), ((C, C), F32)],
        arrived, norm_gains, column_project, column_output,
        scratch=[pltpu.VMEM((seq_count, group, 2 * C), F32), pltpu.VMEM((seq_count, group, C), F32)],
        name="column_step",
    )
    returned = swap_blocks(returned, False).reshape(returned.shape)
    shared = -(-SLABS * C // (ROWS * FOUR * res_count))
    normed = n_rows // ROWS // FOUR
    bias_grad, middle_grad, *sums = call(
        functools.partial(row_backward, res_count),
        [((n_keys, H * n_rows), F32), ((n_seq, n_rows, C), F32)]
        + [((shared + normed, ROWS, WIDE), F32)] * res_count,
        returned, weights, unit, memory, query_gate, mixture, own_unit, norm_gains, row_project, row_output,
        col_slab, rest_slab, col_out_grad,
        scratch=[pltpu.VMEM((res_count, shared + normed, ROWS, WIDE), F32)],
        name="row_backward",
    )
    sums = sums[:1] + [shift_residues(sums[away], -away, res_count) for away in away_range]
    left = seq_count // 2
    state, send, grad_alignment = call(
        functools.partial(combine, seq_count),
        [
            ((seq_count + shared, ROWS, WIDE), F32),
            ((left + shared, ROWS, WIDE), F32),
            (alignment.shape, alignment.dtype),
        ],
        alignment, middle_grad, bias_grad, norm_gains, *sums,
        name="combine",
    )
    at = 0
    while left > 1:
        arrived = cross(send, at, seq_count, res_count)
        state, send = call(
            functools.partial(step, left),
            [((left + shared, ROWS, WIDE), F32), ((left // 2 + shared, ROWS, WIDE), F32)],
            state, arrived,
            name="step",
        )
        left, at = left // 2, at + 1
    arrived = cross(send, at, seq_count, res_count)
    bias_grad, summed = call(
        last_step,
        [((H, n_keys // seq_count, n_rows), F32), ((shared, ROWS, WIDE), F32)],
        state, arrived,
        name="last_step",
    )
    grads = call(
        functools.partial(unpack, res_count),
        [((2, C), F32), ((C, 4 * C), F32), ((C, C), F32), ((C, 2 * C + 2 * DH), F32), ((C, C), F32)],
        summed, *[shift_residues(summed, away, res_count) for away in away_range],
        norm_gains, row_project, column_project,
        scratch=[pltpu.VMEM((res_count, shared, ROWS, WIDE), F32)],
        name="unpack",
    )
    return (grad_alignment, jnp.transpose(bias_grad, (0, 2, 1)), *grads)


def solution(mesh):
    placed = (
        P("seq", "res", None),
        P("seq", "res", None),
        P(None, "res", None),
        P(),
        P(),
        P(),
        P(),
        P(),
        P("res"),
        P("seq"),
    )
    return jax.shard_map(
        functools.partial(local, seq_count=mesh.shape["seq"], res_count=mesh.shape["res"]),
        mesh=mesh,
        in_specs=placed,
        out_specs=(P("seq", "res", None), P(None, "res", "seq"), P(), P(), P(), P(), P()),
        check_vma=False,
    )
```

```python
import functools

import jax
import jax.numpy as jnp
from jax import lax
from jax.experimental import pallas as pl
from jax.experimental.pallas import tpu as pltpu
from jax.sharding import PartitionSpec as P

C = 64
H = 8
DH = 8
LANES = 128
ROWS = 8

EXACT = lax.Precision.HIGHEST
THREE = lax.Precision.HIGH
EPSILON = 1e-05
MASKED = 1000000000.0
SCALE = DH ** (-0.5)
F32 = jnp.float32


def dot(a, b, over=((1,), (0,)), precision=THREE):
    return lax.dot_general(a, b, (over, ((), ())), precision=precision, preferred_element_type=F32)


def dot_rows(a, b):
    return dot(a, b, ((0,), (0,)))


def dot_t(a, b, precision=THREE):
    return dot(a, b, ((1,), (1,)), precision)


def to_column(row):
    eye = lax.broadcasted_iota(jnp.int32, (C, C), 0) == lax.broadcasted_iota(jnp.int32, (C, C), 1)
    return jnp.sum(jnp.where(eye, row, 0.0), axis=1, keepdims=True)


def to_row(column):
    eye = lax.broadcasted_iota(jnp.int32, (C, C), 0) == lax.broadcasted_iota(jnp.int32, (C, C), 1)
    return jnp.sum(jnp.where(eye, column, 0.0), axis=0, keepdims=True)


def normalise(values):
    centred = values - jnp.mean(values, axis=-1, keepdims=True)
    inverse = lax.rsqrt(jnp.mean(centred * centred, axis=-1, keepdims=True) + EPSILON)
    return centred * inverse, inverse


def normalise_back(grad_normed, gain, unit, inverse):
    grad_unit = grad_normed * gain
    along = jnp.mean(grad_unit * unit, axis=-1, keepdims=True)
    return inverse * (grad_unit - jnp.mean(grad_unit, axis=-1, keepdims=True) - unit * along)


def head_mask(rows):
    row = lax.broadcasted_iota(jnp.int32, (H, rows, C), 0)
    channel = lax.broadcasted_iota(jnp.int32, (H, rows, C), 2)
    return (row == channel // DH).astype(F32).reshape(H * rows, C)


def spread_heads(values, mask):
    return jnp.concatenate([values] * H, axis=0) * mask


def join_heads(values, mask):
    masked = values * mask
    return jnp.sum(masked.reshape(H, -1, C), axis=0)


def row_forward(n_res, seq_mask, *refs):
    sent = refs[:n_res]
    own, cotangent, bias, gains, w_row, w_out = refs[n_res : n_res + 6]
    payload, weights_out, unit_out, own_unit_out, memory_out, query_gate_out, mixture_out, gathered = refs[n_res + 6 :]
    n_seq, n_rows, _ = own.shape
    me = lax.axis_index("res")
    for away in range(n_res):
        gathered[lax.rem(me + away, n_res)] = sent[away][...]
    n_keys = n_res * n_rows
    n_blocks = payload.shape[0]
    block = n_rows // n_blocks
    gain = gains[0:1, :]
    w_all = w_row[...]
    w_query_gate = jnp.concatenate([w_all[:, :C], w_all[:, 3 * C :]], axis=1)
    residue = gathered[:, n_seq].reshape(n_keys, C)
    key_bias = MASKED * (jnp.transpose(residue)[0:1, :] - 1.0)
    bias_rows = bias[...].reshape(H * n_rows, n_keys).astype(F32)
    mask = head_mask(n_rows)
    for s in range(n_seq):
        unit, _ = normalise(gathered[:, s].reshape(n_keys, C))
        unit_out[s] = unit
        memory = dot(unit * gain, w_all[:, C : 3 * C], precision=EXACT)
        memory_out[s] = memory
        initial = own[s].astype(F32)
        own_unit, _ = normalise(initial)
        own_unit_out[s] = own_unit
        projected = dot(own_unit * gain, w_query_gate, precision=EXACT)
        query = projected[:, :C] * SCALE
        gate = jax.nn.sigmoid(projected[:, C:])
        query_gate_out[s] = jnp.concatenate([query, gate], axis=1)
        scores = dot_t(spread_heads(query, mask), memory[:, :C], EXACT) + bias_rows + key_bias
        exponent = jnp.exp(scores - jnp.max(scores, axis=-1, keepdims=True))
        weights = exponent / jnp.sum(exponent, axis=-1, keepdims=True)
        weights_out[s] = weights
        mixture = join_heads(dot(weights, memory[:, C:]), mask)
        mixture_out[s] = mixture
        middle = initial + dot(gate * mixture, w_out[...])
        both = jnp.concatenate([middle, cotangent[s].astype(F32)], axis=1)
        for b in range(n_blocks):
            payload[b, s] = both[b * block : (b + 1) * block, :]
    lane = lax.broadcasted_iota(jnp.int32, (block, 2 * C), 1) // (2 * C // n_seq)
    present = jnp.zeros((block, 2 * C), F32)
    for s in range(n_seq):
        present = jnp.where(lane == s, seq_mask[s].astype(F32), present)
    for b in range(n_blocks):
        payload[b, n_seq] = present


def column_step(arrived, gains, w_col, w_out, returned, gathered, mask_rows, n_seq):
    n_src, _, block, _ = arrived.shape
    group = n_seq * block
    rows = n_src * group
    wide = 2 * C // n_seq
    share = C // n_src
    for src in range(n_src):
        for s in range(n_seq):
            gathered[src, s * block : (s + 1) * block, :] = arrived[src, s]
            mask_rows[src, s * block : (s + 1) * block, :] = jnp.broadcast_to(
                arrived[src, n_seq, :, s * wide : s * wide + 1], (block, C)
            )
    data = gathered[...].reshape(rows, 2 * C)
    present = mask_rows[...]
    middle = data[:, :C]
    cot = data[:, C:]
    gain = gains[1:2, :]

    def over_sequences(values, combine, reduce):
        total = reduce(values.reshape(n_src, group, C), axis=0)
        result = total
        for shift in range(1, n_seq):
            result = combine(result, pltpu.roll(total, shift * block, 0))
        return result

    def total_of(values):
        return over_sequences(values, jnp.add, jnp.sum)

    def spread(values):
        return jnp.broadcast_to(values[None], (n_src, group, C)).reshape(rows, C)

    lane = lax.broadcasted_iota(jnp.int32, (C, C), 1)
    row = lax.broadcasted_iota(jnp.int32, (C, C), 0)
    same_head = (row // DH == lane // DH).astype(F32)
    repeat = (lax.broadcasted_iota(jnp.int32, (DH, C), 0) == lax.broadcasted_iota(jnp.int32, (DH, C), 1) % DH).astype(F32)
    w_all = w_col[...]
    w_query = w_all[:, :C]
    w_key = dot(w_all[:, C : C + DH], repeat, precision=EXACT)
    w_value = dot(w_all[:, C + DH : C + 2 * DH], repeat)
    w_gate = w_all[:, C + 2 * DH :]
    w_rest = jnp.concatenate([w_key, w_value, w_gate], axis=1)

    unit, inverse = normalise(middle)
    normed = unit * gain
    present_rows = present.reshape(rows, C)
    counted = total_of(present_rows)
    mean_unit = total_of(present_rows * unit) / counted
    mean_normed = mean_unit * gain
    query = dot(mean_normed, w_query, precision=EXACT) * SCALE
    query_rows = spread(query)
    rest = dot(normed, w_rest, precision=EXACT)
    key, value = rest[:, :C], rest[:, C : 2 * C]
    gate = jax.nn.sigmoid(rest[:, 2 * C :])
    scores = dot(query_rows * key, same_head, precision=EXACT) + MASKED * (present_rows - 1.0)
    peak = over_sequences(scores, jnp.maximum, jnp.max)
    exponent = jnp.exp(scores - spread(peak))
    weights = exponent / spread(total_of(exponent))
    mixture = total_of(weights * value)
    mixture_rows = spread(mixture)

    grad_gated = dot_t(cot, w_out[...])
    out_grad = dot_rows(gate * mixture_rows, cot)
    grad_mixture = total_of(gate * grad_gated)
    grad_mixture_rows = spread(grad_mixture)
    grad_gate = grad_gated * mixture_rows * gate * (1.0 - gate)
    grad_weights = dot(grad_mixture_rows * value, same_head)
    inner = spread(dot(grad_mixture * mixture, same_head))
    grad_scores = weights * (grad_weights - inner)
    grad_rest = jnp.concatenate([grad_scores * query_rows, weights * grad_mixture_rows, grad_gate], axis=1)
    grad_query = total_of(grad_scores * key) * SCALE
    grad_mean = dot_t(grad_query, w_query)
    grad_normed = present_rows * spread(grad_mean / counted) + dot_t(grad_rest, w_rest)
    grad_query_weights = dot_rows(mean_unit, grad_query) * (1.0 / n_seq)
    grad_rest_weights = dot_rows(unit, grad_rest)
    fold_row = lax.broadcasted_iota(jnp.int32, (2 * C, 2 * DH), 0)
    fold_lane = lax.broadcasted_iota(jnp.int32, (2 * C, 2 * DH), 1)
    fold = ((fold_row // C == fold_lane // DH) & (fold_row % DH == fold_lane % DH)).astype(F32)
    grad_key_value = dot(grad_rest_weights[:, : 2 * C], fold)
    first = jnp.concatenate([grad_query_weights, grad_rest_weights[:, 2 * C :]], axis=1)
    second = jnp.concatenate([out_grad, grad_key_value, jnp.zeros((C, C - 2 * DH), F32)], axis=1)
    grad_middle = (cot + normalise_back(grad_normed, gain, unit, inverse)).reshape(n_src, group, C)
    for src in range(n_src):
        for s in range(n_seq):
            returned[src, 0, :, s * C : (s + 1) * C] = grad_middle[src, s * block : (s + 1) * block, :]
        returned[src, 1] = first[src * share : (src + 1) * share, :]
        returned[src, 2] = second[src * share : (src + 1) * share, :]


def row_backward(n_res, returned, weights_in, unit_in, memory_in, query_gate_in, mixture_in, own_unit_in,
                 w_row, w_out, state, send, middle_grad, *refs):
    sums_out, shares, bias_t = refs[:n_res], refs[n_res], refs[n_res + 1]
    me = lax.axis_index("res")
    n_seq, n_rows, _ = middle_grad.shape
    n_keys = memory_in.shape[1]
    n_blocks, _, block, _ = returned.shape
    w_all = w_row[...]
    w_memory = w_all[:, C : 3 * C]
    w_query_gate = jnp.concatenate([w_all[:, :C], w_all[:, 3 * C :]], axis=1)
    mask = head_mask(n_rows)
    for b in range(n_blocks):
        for s in range(n_seq):
            middle_grad[s, b * block : (b + 1) * block, :] = returned[b, 0, :, s * C : (s + 1) * C]
    grad_out = jnp.zeros((C, C), F32)
    grad_query_gate_weights = jnp.zeros((C, 2 * C), F32)
    grad_memory_weights = jnp.zeros((C, 2 * C), F32)
    bias_grad = jnp.zeros((H * n_rows, n_keys), F32)
    from_own = []
    from_memory = []
    for s in range(n_seq):
        grad_middle = middle_grad[s]
        query = query_gate_in[s, :, :C]
        gate = query_gate_in[s, :, C:]
        mixture = mixture_in[s]
        memory = memory_in[s]
        weights = weights_in[s]
        grad_gated = dot_t(grad_middle, w_out[...])
        grad_out = grad_out + dot_rows(gate * mixture, grad_middle)
        grad_gate = grad_gated * mixture * gate * (1.0 - gate)
        grad_heads = spread_heads(grad_gated * gate, mask)
        query_heads = spread_heads(query, mask)
        inner = grad_heads * jnp.concatenate([mixture] * H, axis=0)
        left = jnp.concatenate([grad_heads, inner], axis=1)
        right = jnp.concatenate([memory[:, C:], jnp.full((n_keys, C), -1.0, F32)], axis=1)
        grad_scores = weights * dot_t(left, right)
        bias_grad = bias_grad + grad_scores
        grad_query = join_heads(dot(grad_scores, memory[:, :C]), mask) * SCALE
        grad_key = dot_rows(grad_scores, query_heads)
        grad_value = dot_rows(weights, grad_heads)
        grad_memory = jnp.concatenate([grad_key, grad_value], axis=1)
        grad_query_gate = jnp.concatenate([grad_query, grad_gate], axis=1)
        grad_query_gate_weights = grad_query_gate_weights + dot_rows(own_unit_in[s], grad_query_gate)
        grad_memory_weights = grad_memory_weights + dot_rows(unit_in[s], grad_memory)
        from_memory.append(dot_t(grad_memory, w_memory))
        from_own.append(dot_t(grad_query_gate, w_query_gate))
    bias_t[...] = jnp.transpose(bias_grad)
    split_blocks(bias_t, state, send)

    half = C // 2
    weight_grads = jnp.concatenate(
        [grad_query_gate_weights, grad_memory_weights, jnp.concatenate([grad_out[:half], grad_out[half:]], axis=1)],
        axis=0,
    )
    part = shares.shape[1] - ROWS - n_rows
    shares[...] = jnp.zeros(shares.shape, F32)
    share = C // n_blocks
    column = jnp.sum(returned[:, 1:, :, :], axis=0)
    normed = jnp.concatenate(from_memory, axis=1)
    for i in range(n_res):
        rows = min(part, max(0, weight_grads.shape[0] - i * part))
        if rows:
            shares[i, :rows, :] = weight_grads[i * part : i * part + rows, :]
        shares[i, part : part + share, :] = column[0]
        shares[i, part + share : part + 2 * share, :] = column[1]
        shares[i, part + ROWS :, :] = normed[i * n_rows : (i + 1) * n_rows, :]
    for away in range(n_res):
        sums_out[away][...] = shares[lax.rem(me + away, n_res)]
    sums_out[0][part + ROWS :, :] += jnp.concatenate(from_own, axis=1)


def step_bits(n_seq_devices, odd, late_first=False):
    bits = list(range(n_seq_devices.bit_length() - 1))
    if odd:
        for i in range(0, len(bits) - 1, 2):
            bits[i], bits[i + 1] = bits[i + 1], bits[i]
    if late_first:
        middle = len(bits) // 2
        bits = bits[middle:] + bits[:middle]
    return bits


def relative_block(mask_of_bits, n_blocks, late_first=False):
    odd = lax.rem(lax.axis_index("res"), 2)
    even_mask = mask_of_bits(step_bits(n_blocks, False, late_first))
    odd_mask = mask_of_bits(step_bits(n_blocks, True, late_first))
    return lax.axis_index("seq") ^ (even_mask + odd * (odd_mask - even_mask))


def split_blocks(bias_t, state, send):
    n_blocks = state.shape[0] + send.shape[0]
    keys_each = bias_t.shape[0] // n_blocks
    half = n_blocks // 2

    for slot in range(n_blocks):

        def mask_of_bits(bits):
            last = len(bits) - 1
            return sum(1 << bit for at, bit in enumerate(bits) if slot >> (last - at) & 1)

        block = relative_block(mask_of_bits, n_blocks)
        values = bias_t[pl.ds(pl.multiple_of(block * keys_each, keys_each), keys_each), :]
        if slot < half:
            state[slot] = values
        else:
            send[slot - half] = values


def bias_step(state, arrived, state_out, send_out):
    total = state[...] + arrived[...]
    half = state_out.shape[0]
    state_out[...] = total[:half]
    send_out[...] = total[half:]


def bias_last(state, arrived, bias_out):
    total = state[0] + arrived[0]
    heads, _, n_rows = bias_out.shape
    for h in range(heads):
        bias_out[h] = total[:, h * n_rows : (h + 1) * n_rows]


def add_shares(*refs):
    sums, shared, normed = refs[:-2], refs[-2], refs[-1]
    total = sums[0][...]
    for more in sums[1:]:
        total = total + more[...]
    rows = shared.shape[0]
    shared[...] = total[:rows]
    normed[...] = total[rows:]


def shared_step(part, shared, arrived, *outs):
    total = shared[:part] + arrived[:part]
    pieces = shared.shape[0] - part
    if len(outs) == 2:
        outs[0][...] = total
        joined, at = outs[1], 0
    else:
        outs[0][:part] = total
        joined, at = outs[0], part
    joined[at : at + pieces] = shared[part:]
    joined[at + pieces :] = arrived[part:]


def finish_alignment(own, middle_grad, gains, normed, out):
    n_seq = own.shape[0]
    for s in range(n_seq):
        unit, inverse = normalise(own[s].astype(F32))
        grad_normed = normed[:, s * C : (s + 1) * C]
        out[s] = (middle_grad[s] + normalise_back(grad_normed, gains[0:1, :], unit, inverse)).astype(out.dtype)


def unpack(n_res, joined, *refs):
    parts = refs[:n_res]
    gains, w_row, w_col, gains_out, row_project_out, row_out_out, col_project_out, col_out_out = refs[n_res : n_res + 8]
    shares, column = refs[n_res + 8 :]
    me = lax.axis_index("res")
    part = shares.shape[1]
    for away in range(n_res):
        shares[lax.rem(me + away, n_res)] = parts[away][...]
    n_blocks, _, share, _ = column.shape
    for slot in range(n_blocks):
        block = relative_block(
            lambda bits: sum(1 << bit for at, bit in enumerate(bits) if slot >> at & 1), n_blocks, True
        )
        piece = joined[slot * ROWS : (slot + 1) * ROWS, :]
        column[block, 0] = piece[:share]
        column[block, 1] = piece[share : 2 * share]
    flat = jnp.concatenate([shares[i] for i in range(n_res)], axis=0)
    query_gate, memory, outs = flat[:C], flat[C : 2 * C], flat[2 * C : 2 * C + C // 2]
    col_query_gate = jnp.concatenate([column[i, 0] for i in range(n_blocks)], axis=0)
    col_rest = jnp.concatenate([column[i, 1] for i in range(n_blocks)], axis=0)
    rest = col_rest[:, C : C + 2 * DH]
    gain_row = to_column(gains[0:1, :])
    gain_col = to_column(gains[1:2, :])
    w_all = w_row[...]
    w_column = w_col[...]
    row_gain_grad = (
        jnp.sum(query_gate[:, :C] * w_all[:, :C], axis=1, keepdims=True)
        + jnp.sum(memory * w_all[:, C : 3 * C], axis=1, keepdims=True)
        + jnp.sum(query_gate[:, C:] * w_all[:, 3 * C :], axis=1, keepdims=True)
    )
    col_gain_grad = (
        jnp.sum(col_query_gate[:, :C] * w_column[:, :C], axis=1, keepdims=True)
        + jnp.sum(rest * w_column[:, C : C + 2 * DH], axis=1, keepdims=True)
        + jnp.sum(col_query_gate[:, C:] * w_column[:, C + 2 * DH :], axis=1, keepdims=True)
    )
    gains_out[0:1, :] = to_row(row_gain_grad)
    gains_out[1:2, :] = to_row(col_gain_grad)
    row_project_out[:, :C] = query_gate[:, :C] * gain_row
    row_project_out[:, C : 3 * C] = memory * gain_row
    row_project_out[:, 3 * C :] = query_gate[:, C:] * gain_row
    col_project_out[:, :C] = col_query_gate[:, :C] * gain_col
    col_project_out[:, C : C + 2 * DH] = rest * gain_col
    col_project_out[:, C + 2 * DH :] = col_query_gate[:, C:] * gain_col
    half = C // 2
    row_out_out[:half, :] = outs[:, :C]
    row_out_out[half:, :] = outs[:, C:]
    col_out_out[...] = col_rest[:, :C]


def call(body, outs, *operands, smem=0, scratch=(), name):
    vmem = pl.BlockSpec(memory_space=pltpu.VMEM)
    scalar = pl.BlockSpec(memory_space=pltpu.SMEM)
    return pl.pallas_call(
        body,
        out_shape=[jax.ShapeDtypeStruct(shape, kind) for shape, kind in outs],
        in_specs=[scalar] * smem + [vmem] * (len(operands) - smem),
        out_specs=[vmem] * len(outs),
        scratch_shapes=list(scratch),
        compiler_params=pltpu.CompilerParams(vmem_limit_bytes=32 * 1024 * 1024),
        name=name,
    )(*operands)


def shift_residues(values, away, count):
    return lax.ppermute(values, "res", [((i + away) % count, i) for i in range(count)])


def cross(values, at, seq_count, res_count, late_first=False):
    pairs = []
    for r in range(res_count):
        bit = 1 << step_bits(seq_count, r % 2, late_first)[at]
        pairs += [(i * res_count + r, (i ^ bit) * res_count + r) for i in range(seq_count)]
    return lax.ppermute(values, ("seq", "res"), pairs)


def swap_blocks(values):
    return lax.all_to_all(values, "seq", 0, 0, tiled=True)


def local(
    alignment,
    cotangent,
    pair_bias,
    norm_gains,
    row_project,
    row_output,
    column_project,
    column_output,
    residue_mask,
    sequence_mask,
    seq_count,
    res_count,
):
    n_seq, n_rows, _ = alignment.shape
    n_keys = pair_bias.shape[2]
    block = n_rows // seq_count
    group = n_seq * block
    away_range = range(1, res_count)
    present_keys = jnp.broadcast_to(residue_mask.astype(F32)[None, :, None], (1, n_rows, C))
    sent = jnp.concatenate([alignment.astype(F32), present_keys], axis=0)
    payload, weights, unit, own_unit, memory, query_gate, mixture = call(
        functools.partial(row_forward, res_count),
        [
            ((seq_count, n_seq + 1, block, 2 * C), F32),
            ((n_seq, H * n_rows, n_keys), F32),
            ((n_seq, n_keys, C), F32),
            ((n_seq, n_rows, C), F32),
            ((n_seq, n_keys, 2 * C), F32),
            ((n_seq, n_rows, 2 * C), F32),
            ((n_seq, n_rows, C), F32),
        ],
        sequence_mask, sent, *[shift_residues(sent, away, res_count) for away in away_range],
        alignment, cotangent, pair_bias, norm_gains, row_project, row_output,
        smem=1,
        scratch=[pltpu.VMEM((res_count, n_seq + 1, n_rows, C), F32)],
        name="row_forward",
    )
    arrived = swap_blocks(payload)
    (returned,) = call(
        functools.partial(column_step, n_seq=n_seq),
        [((seq_count, 3, block, 2 * C), F32)],
        arrived, norm_gains, column_project, column_output,
        scratch=[pltpu.VMEM((seq_count, group, 2 * C), F32), pltpu.VMEM((seq_count, group, C), F32)],
        name="column_step",
    )
    returned = swap_blocks(returned)
    part = -(-5 * C // (2 * ROWS * res_count)) * ROWS
    wide = H * n_rows
    keys_each = n_keys // seq_count
    left = seq_count // 2
    state, send, middle_grad, *sums = call(
        functools.partial(row_backward, res_count),
        [((left, keys_each, wide), F32)] * 2
        + [((n_seq, n_rows, C), F32)]
        + [((part + ROWS + n_rows, LANES), F32)] * res_count,
        returned, weights, unit, memory, query_gate, mixture, own_unit, row_project, row_output,
        scratch=[
            pltpu.VMEM((res_count, part + ROWS + n_rows, LANES), F32),
            pltpu.VMEM((n_keys, wide), F32),
        ],
        name="row_backward",
    )
    sums = sums[:1] + [shift_residues(sums[away], -away, res_count) for away in away_range]
    arrived = cross(send, 0, seq_count, res_count)
    shared, normed = call(
        add_shares,
        [((part + ROWS, LANES), F32), ((n_rows, LANES), F32)],
        *sums,
        name="add_shares",
    )
    steps = seq_count.bit_length() - 1
    for at in range(steps):
        arrived_shared = cross(shared, at, seq_count, res_count, True)
        if at < steps - 1:
            left //= 2
            state, send = call(
                bias_step, [((left, keys_each, wide), F32)] * 2, state, arrived, name="bias_step"
            )
            arrived = cross(send, at + 1, seq_count, res_count)
        else:
            (bias_grad,) = call(bias_last, [((H, keys_each, n_rows), F32)], state, arrived, name="bias_last")
        pieces = ROWS << (at + 1)
        shapes = [(part + pieces, LANES)] if at < steps - 1 else [(part, LANES), (pieces, LANES)]
        shared, *joined = call(
            functools.partial(shared_step, part),
            [(shape, F32) for shape in shapes],
            shared, arrived_shared,
            name="shared_step",
        )
    (grad_alignment,) = call(
        finish_alignment,
        [(alignment.shape, alignment.dtype)],
        alignment, middle_grad, norm_gains, normed,
        name="finish_alignment",
    )
    grads = call(
        functools.partial(unpack, res_count),
        [((2, C), F32), ((C, 4 * C), F32), ((C, C), F32), ((C, 2 * C + 2 * DH), F32), ((C, C), F32)],
        *joined, shared, *[shift_residues(shared, away, res_count) for away in away_range],
        norm_gains, row_project, column_project,
        scratch=[
            pltpu.VMEM((res_count, part, LANES), F32),
            pltpu.VMEM((seq_count, 2, C // seq_count, LANES), F32),
        ],
        name="unpack",
    )
    return (grad_alignment, jnp.transpose(bias_grad, (0, 2, 1)), *grads)


def solution(mesh):
    placed = (
        P("seq", "res", None),
        P("seq", "res", None),
        P(None, "res", None),
        P(),
        P(),
        P(),
        P(),
        P(),
        P("res"),
        P("seq"),
    )
    return jax.shard_map(
        functools.partial(local, seq_count=mesh.shape["seq"], res_count=mesh.shape["res"]),
        mesh=mesh,
        in_specs=placed,
        out_specs=(P("seq", "res", None), P(None, "res", "seq"), P(), P(), P(), P(), P()),
        check_vma=False,
    )
```

```python
import functools

import jax
import jax.numpy as jnp
from jax import lax
from jax.experimental import pallas as pl
from jax.experimental.pallas import tpu as pltpu
from jax.sharding import PartitionSpec as P

C = 64
H = 8
DH = 8
LANES = 128
ROWS = 8

EXACT = lax.Precision.HIGHEST
THREE = lax.Precision.HIGH
EPSILON = 1e-05
MASKED = 1000000000.0
SCALE = DH ** (-0.5)
F32 = jnp.float32


def dot(a, b, over=((1,), (0,)), precision=THREE):
    return lax.dot_general(a, b, (over, ((), ())), precision=precision, preferred_element_type=F32)


def dot_rows(a, b):
    return dot(a, b, ((0,), (0,)))


def dot_t(a, b, precision=THREE):
    return dot(a, b, ((1,), (1,)), precision)


def to_column(row):
    eye = lax.broadcasted_iota(jnp.int32, (C, C), 0) == lax.broadcasted_iota(jnp.int32, (C, C), 1)
    return jnp.sum(jnp.where(eye, row, 0.0), axis=1, keepdims=True)


def to_row(column):
    eye = lax.broadcasted_iota(jnp.int32, (C, C), 0) == lax.broadcasted_iota(jnp.int32, (C, C), 1)
    return jnp.sum(jnp.where(eye, column, 0.0), axis=0, keepdims=True)


def normalise(values):
    centred = values - jnp.mean(values, axis=-1, keepdims=True)
    inverse = lax.rsqrt(jnp.mean(centred * centred, axis=-1, keepdims=True) + EPSILON)
    return centred * inverse, inverse


def normalise_back(grad_normed, gain, unit, inverse):
    grad_unit = grad_normed * gain
    along = jnp.mean(grad_unit * unit, axis=-1, keepdims=True)
    return inverse * (grad_unit - jnp.mean(grad_unit, axis=-1, keepdims=True) - unit * along)


def head_mask(rows):
    row = lax.broadcasted_iota(jnp.int32, (H, rows, C), 0)
    channel = lax.broadcasted_iota(jnp.int32, (H, rows, C), 2)
    return (row == channel // DH).astype(F32).reshape(H * rows, C)


def spread_heads(values, mask):
    return jnp.concatenate([values] * H, axis=0) * mask


def join_heads(values, mask):
    masked = values * mask
    return jnp.sum(masked.reshape(H, -1, masked.shape[1]), axis=0)


def row_forward(n_res, seq_mask, *refs):
    sent = refs[:n_res]
    own, cotangent, bias, gains, w_row, w_out = refs[n_res : n_res + 6]
    payload, exponent_out, unit_out, own_unit_out, memory_out, query_gate_out, mixture_out, inverse_out, gathered = refs[n_res + 6 :]
    n_seq, n_rows, _ = own.shape
    me = lax.axis_index("res")
    for away in range(n_res):
        gathered[lax.rem(me + away, n_res)] = sent[away][...]
    n_keys = n_res * n_rows
    n_blocks = payload.shape[0]
    block = n_rows // n_blocks
    gain = gains[0:1, :]
    w_all = w_row[...]
    w_query_gate = jnp.concatenate([w_all[:, :C], w_all[:, 3 * C :]], axis=1)
    present_keys = jnp.concatenate([gathered[i, n_seq, 0:1, :n_rows] for i in range(n_res)], axis=1)
    key_bias = MASKED * (present_keys - 1.0)
    bias_rows = bias[...].reshape(H * n_rows, n_keys).astype(F32)
    mask = head_mask(n_rows)
    wide_mask = jnp.concatenate([mask, mask], axis=1)
    for s in range(n_seq):
        unit, _ = normalise(gathered[:, s].reshape(n_keys, C))
        unit_out[s] = unit
        memory = dot(unit * gain, w_all[:, C : 3 * C], precision=EXACT)
        memory_out[s] = memory
        initial = own[s].astype(F32)
        own_unit, _ = normalise(initial)
        own_unit_out[s] = own_unit
        projected = dot(own_unit * gain, w_query_gate, precision=EXACT)
        query = projected[:, :C] * SCALE
        gate = jax.nn.sigmoid(projected[:, C:])
        query_gate_out[s] = jnp.concatenate([query, gate], axis=1)
        scores = dot_t(spread_heads(query, mask), memory[:, :C], EXACT) + bias_rows + key_bias
        exponent = jnp.exp(scores - jnp.max(scores, axis=-1, keepdims=True))
        exponent_out[s] = exponent
        summed = dot(exponent, jnp.concatenate([memory[:, C:], jnp.ones((n_keys, C), F32)], axis=1))
        summed = join_heads(summed, wide_mask)
        inverse = 1.0 / summed[:, C:]
        inverse_out[s] = inverse
        mixture = summed[:, :C] * inverse
        mixture_out[s] = mixture
        middle = initial + dot(gate * mixture, w_out[...])
        both = jnp.concatenate([middle, cotangent[s].astype(F32)], axis=1)
        for b in range(n_blocks):
            payload[b, s] = both[b * block : (b + 1) * block, :]
    lane = lax.broadcasted_iota(jnp.int32, (block, 2 * C), 1) // (2 * C // n_seq)
    present = jnp.zeros((block, 2 * C), F32)
    for s in range(n_seq):
        present = jnp.where(lane == s, seq_mask[s].astype(F32), present)
    for b in range(n_blocks):
        payload[b, n_seq] = present


def column_step(arrived, gains, w_col, w_out, returned, gathered, mask_rows, n_seq):
    n_src, _, block, _ = arrived.shape
    group = n_seq * block
    rows = n_src * group
    wide = 2 * C // n_seq
    share = C // n_src
    for src in range(n_src):
        for s in range(n_seq):
            gathered[src, s * block : (s + 1) * block, :] = arrived[src, s]
            mask_rows[src, s * block : (s + 1) * block, :] = jnp.broadcast_to(
                arrived[src, n_seq, :, s * wide : s * wide + 1], (block, C)
            )
    data = gathered[...].reshape(rows, 2 * C)
    present = mask_rows[...]
    middle = data[:, :C]
    cot = data[:, C:]
    gain = gains[1:2, :]

    def over_sequences(values, combine, reduce):
        total = reduce(values.reshape(n_src, group, C), axis=0)
        result = total
        for shift in range(1, n_seq):
            result = combine(result, pltpu.roll(total, shift * block, 0))
        return result

    def total_of(values):
        return over_sequences(values, jnp.add, jnp.sum)

    def spread(values):
        return jnp.broadcast_to(values[None], (n_src, group, C)).reshape(rows, C)

    lane = lax.broadcasted_iota(jnp.int32, (C, C), 1)
    row = lax.broadcasted_iota(jnp.int32, (C, C), 0)
    same_head = (row // DH == lane // DH).astype(F32)
    repeat = (lax.broadcasted_iota(jnp.int32, (DH, C), 0) == lax.broadcasted_iota(jnp.int32, (DH, C), 1) % DH).astype(F32)
    w_all = w_col[...]
    w_query = w_all[:, :C]
    w_key = dot(w_all[:, C : C + DH], repeat, precision=EXACT)
    w_value = dot(w_all[:, C + DH : C + 2 * DH], repeat)
    w_gate = w_all[:, C + 2 * DH :]
    w_rest = jnp.concatenate([w_key, w_value, w_gate], axis=1)

    unit, inverse = normalise(middle)
    normed = unit * gain
    present_rows = present.reshape(rows, C)
    counted = total_of(present_rows)
    mean_unit = total_of(present_rows * unit) / counted
    mean_normed = mean_unit * gain
    query = dot(mean_normed, w_query, precision=EXACT) * SCALE
    query_rows = spread(query)
    rest = dot(normed, w_rest, precision=EXACT)
    key, value = rest[:, :C], rest[:, C : 2 * C]
    gate = jax.nn.sigmoid(rest[:, 2 * C :])
    scores = dot(query_rows * key, same_head, precision=EXACT) + MASKED * (present_rows - 1.0)
    peak = over_sequences(scores, jnp.maximum, jnp.max)
    exponent = jnp.exp(scores - spread(peak))
    weights = exponent / spread(total_of(exponent))
    mixture = total_of(weights * value)
    mixture_rows = spread(mixture)

    grad_gated = dot_t(cot, w_out[...])
    out_grad = dot_rows(gate * mixture_rows, cot)
    grad_mixture = total_of(gate * grad_gated)
    grad_mixture_rows = spread(grad_mixture)
    grad_gate = grad_gated * mixture_rows * gate * (1.0 - gate)
    grad_weights = dot(grad_mixture_rows * value, same_head)
    inner = spread(dot(grad_mixture * mixture, same_head))
    grad_scores = weights * (grad_weights - inner)
    grad_rest = jnp.concatenate([grad_scores * query_rows, weights * grad_mixture_rows, grad_gate], axis=1)
    grad_query = total_of(grad_scores * key) * SCALE
    grad_mean = dot_t(grad_query, w_query)
    grad_normed = present_rows * spread(grad_mean / counted) + dot_t(grad_rest, w_rest)
    grad_query_weights = dot_rows(mean_unit, grad_query) * (1.0 / n_seq)
    grad_rest_weights = dot_rows(unit, grad_rest)
    fold_row = lax.broadcasted_iota(jnp.int32, (2 * C, 2 * DH), 0)
    fold_lane = lax.broadcasted_iota(jnp.int32, (2 * C, 2 * DH), 1)
    fold = ((fold_row // C == fold_lane // DH) & (fold_row % DH == fold_lane % DH)).astype(F32)
    grad_key_value = dot(grad_rest_weights[:, : 2 * C], fold)
    first = jnp.concatenate([grad_query_weights, grad_rest_weights[:, 2 * C :]], axis=1)
    second = jnp.concatenate([out_grad, grad_key_value, jnp.zeros((C, C - 2 * DH), F32)], axis=1)
    grad_middle = (cot + normalise_back(grad_normed, gain, unit, inverse)).reshape(n_src, group, C)
    for src in range(n_src):
        for s in range(n_seq):
            returned[src, 0, :, s * C : (s + 1) * C] = grad_middle[src, s * block : (s + 1) * block, :]
        returned[src, 1] = first[src * share : (src + 1) * share, :]
        returned[src, 2] = second[src * share : (src + 1) * share, :]


def row_backward(n_res, returned, exponent_in, unit_in, memory_in, query_gate_in, mixture_in, inverse_in, own_unit_in,
                 w_row, w_out, state, send, middle_grad, *refs):
    sums_out, shares, bias_t = refs[:n_res], refs[n_res], refs[n_res + 1]
    me = lax.axis_index("res")
    n_seq, n_rows, _ = middle_grad.shape
    n_keys = memory_in.shape[1]
    n_blocks, _, block, _ = returned.shape
    w_all = w_row[...]
    w_memory = w_all[:, C : 3 * C]
    w_query_gate = jnp.concatenate([w_all[:, :C], w_all[:, 3 * C :]], axis=1)
    mask = head_mask(n_rows)
    for b in range(n_blocks):
        for s in range(n_seq):
            middle_grad[s, b * block : (b + 1) * block, :] = returned[b, 0, :, s * C : (s + 1) * C]
    grad_out = jnp.zeros((C, C), F32)
    grad_query_gate_weights = jnp.zeros((C, 2 * C), F32)
    grad_memory_weights = jnp.zeros((C, 2 * C), F32)
    bias_grad = jnp.zeros((H * n_rows, n_keys), F32)
    from_own = []
    from_memory = []
    for s in range(n_seq):
        grad_middle = middle_grad[s]
        query = query_gate_in[s, :, :C]
        gate = query_gate_in[s, :, C:]
        mixture = mixture_in[s]
        memory = memory_in[s]
        exponent = exponent_in[s]
        grad_gated = dot_t(grad_middle, w_out[...])
        grad_out = grad_out + dot_rows(gate * mixture, grad_middle)
        grad_gate = grad_gated * mixture * gate * (1.0 - gate)
        grad_heads = spread_heads(grad_gated * gate * inverse_in[s], mask)
        query_heads = spread_heads(query, mask)
        inner = grad_heads * jnp.concatenate([mixture] * H, axis=0)
        left = jnp.concatenate([grad_heads, inner], axis=1)
        right = jnp.concatenate([memory[:, C:], jnp.full((n_keys, C), -1.0, F32)], axis=1)
        grad_scores = exponent * dot_t(left, right)
        bias_grad = bias_grad + grad_scores
        grad_query = join_heads(dot(grad_scores, memory[:, :C]), mask) * SCALE
        grad_key = dot_rows(grad_scores, query_heads)
        grad_value = dot_rows(exponent, grad_heads)
        grad_memory = jnp.concatenate([grad_key, grad_value], axis=1)
        grad_query_gate = jnp.concatenate([grad_query, grad_gate], axis=1)
        grad_query_gate_weights = grad_query_gate_weights + dot_rows(own_unit_in[s], grad_query_gate)
        grad_memory_weights = grad_memory_weights + dot_rows(unit_in[s], grad_memory)
        from_memory.append(dot_t(grad_memory, w_memory))
        from_own.append(dot_t(grad_query_gate, w_query_gate))
    bias_t[...] = jnp.transpose(bias_grad)
    split_blocks(bias_t, state, send)

    half = C // 2
    weight_grads = jnp.concatenate(
        [grad_query_gate_weights, grad_memory_weights, jnp.concatenate([grad_out[:half], grad_out[half:]], axis=1)],
        axis=0,
    )
    part = shares.shape[1] - ROWS - n_rows
    shares[...] = jnp.zeros(shares.shape, F32)
    share = C // n_blocks
    column = jnp.sum(returned[:, 1:, :, :], axis=0)
    normed = jnp.concatenate(from_memory, axis=1)
    for i in range(n_res):
        rows = min(part, max(0, weight_grads.shape[0] - i * part))
        if rows:
            shares[i, :rows, :] = weight_grads[i * part : i * part + rows, :]
        shares[i, part : part + share, :] = column[0]
        shares[i, part + share : part + 2 * share, :] = column[1]
        shares[i, part + ROWS :, :] = normed[i * n_rows : (i + 1) * n_rows, :]
    for away in range(n_res):
        sums_out[away][...] = shares[lax.rem(me + away, n_res)]
    sums_out[0][part + ROWS :, :] += jnp.concatenate(from_own, axis=1)


def step_bits(n_seq_devices, odd, late_first=False):
    bits = list(range(n_seq_devices.bit_length() - 1))
    if odd:
        for i in range(0, len(bits) - 1, 2):
            bits[i], bits[i + 1] = bits[i + 1], bits[i]
    if late_first:
        middle = len(bits) // 2
        bits = bits[middle:] + bits[:middle]
    return bits


def relative_block(mask_of_bits, n_blocks, late_first=False):
    odd = lax.rem(lax.axis_index("res"), 2)
    even_mask = mask_of_bits(step_bits(n_blocks, False, late_first))
    odd_mask = mask_of_bits(step_bits(n_blocks, True, late_first))
    return lax.axis_index("seq") ^ (even_mask + odd * (odd_mask - even_mask))


def split_blocks(bias_t, state, send):
    n_blocks = state.shape[0] + send.shape[0]
    keys_each = bias_t.shape[0] // n_blocks
    half = n_blocks // 2

    for slot in range(n_blocks):

        def mask_of_bits(bits):
            last = len(bits) - 1
            return sum(1 << bit for at, bit in enumerate(bits) if slot >> (last - at) & 1)

        block = relative_block(mask_of_bits, n_blocks)
        values = bias_t[pl.ds(pl.multiple_of(block * keys_each, keys_each), keys_each), :]
        if slot < half:
            state[slot] = values
        else:
            send[slot - half] = values


def bias_step(state, arrived, state_out, send_out):
    total = state[...] + arrived[...]
    half = state_out.shape[0]
    state_out[...] = total[:half]
    send_out[...] = total[half:]


def bias_last(state, arrived, bias_out):
    total = state[0] + arrived[0]
    heads, _, n_rows = bias_out.shape
    for h in range(heads):
        bias_out[h] = total[:, h * n_rows : (h + 1) * n_rows]


def add_shares(*refs):
    sums, shared, normed = refs[:-2], refs[-2], refs[-1]
    total = sums[0][...]
    for more in sums[1:]:
        total = total + more[...]
    rows = shared.shape[0]
    shared[...] = total[:rows]
    normed[...] = total[rows:]


def shared_step(part, n_before, shared, arrived, *refs):
    outs = refs[n_before:]
    total = shared[:part] + arrived[:part]
    pieces = shared.shape[0] - part
    if len(outs) == 2:
        outs[0][...] = total
        joined, at = outs[1], 0
    else:
        outs[0][:part] = total
        joined, at = outs[0], part
    joined[at : at + pieces] = shared[part:]
    joined[at + pieces :] = arrived[part:]


def finish_alignment(own, middle_grad, gains, normed, out):
    n_seq = own.shape[0]
    for s in range(n_seq):
        unit, inverse = normalise(own[s].astype(F32))
        grad_normed = normed[:, s * C : (s + 1) * C]
        out[s] = (middle_grad[s] + normalise_back(grad_normed, gains[0:1, :], unit, inverse)).astype(out.dtype)


def unpack(n_res, joined, *refs):
    parts = refs[:n_res]
    gains, w_row, w_col, gains_out, row_project_out, row_out_out, col_project_out, col_out_out = refs[n_res : n_res + 8]
    shares, column = refs[n_res + 8 :]
    me = lax.axis_index("res")
    part = shares.shape[1]
    for away in range(n_res):
        shares[lax.rem(me + away, n_res)] = parts[away][...]
    n_blocks, _, share, _ = column.shape
    for slot in range(n_blocks):
        block = relative_block(
            lambda bits: sum(1 << bit for at, bit in enumerate(bits) if slot >> at & 1), n_blocks, True
        )
        piece = joined[slot * ROWS : (slot + 1) * ROWS, :]
        column[block, 0] = piece[:share]
        column[block, 1] = piece[share : 2 * share]
    flat = jnp.concatenate([shares[i] for i in range(n_res)], axis=0)
    query_gate, memory, outs = flat[:C], flat[C : 2 * C], flat[2 * C : 2 * C + C // 2]
    col_query_gate = jnp.concatenate([column[i, 0] for i in range(n_blocks)], axis=0)
    col_rest = jnp.concatenate([column[i, 1] for i in range(n_blocks)], axis=0)
    rest = col_rest[:, C : C + 2 * DH]
    gain_row = to_column(gains[0:1, :])
    gain_col = to_column(gains[1:2, :])
    w_all = w_row[...]
    w_column = w_col[...]
    row_gain_grad = (
        jnp.sum(query_gate[:, :C] * w_all[:, :C], axis=1, keepdims=True)
        + jnp.sum(memory * w_all[:, C : 3 * C], axis=1, keepdims=True)
        + jnp.sum(query_gate[:, C:] * w_all[:, 3 * C :], axis=1, keepdims=True)
    )
    col_gain_grad = (
        jnp.sum(col_query_gate[:, :C] * w_column[:, :C], axis=1, keepdims=True)
        + jnp.sum(rest * w_column[:, C : C + 2 * DH], axis=1, keepdims=True)
        + jnp.sum(col_query_gate[:, C:] * w_column[:, C + 2 * DH :], axis=1, keepdims=True)
    )
    gains_out[0:1, :] = to_row(row_gain_grad)
    gains_out[1:2, :] = to_row(col_gain_grad)
    row_project_out[:, :C] = query_gate[:, :C] * gain_row
    row_project_out[:, C : 3 * C] = memory * gain_row
    row_project_out[:, 3 * C :] = query_gate[:, C:] * gain_row
    col_project_out[:, :C] = col_query_gate[:, :C] * gain_col
    col_project_out[:, C : C + 2 * DH] = rest * gain_col
    col_project_out[:, C + 2 * DH :] = col_query_gate[:, C:] * gain_col
    half = C // 2
    row_out_out[:half, :] = outs[:, :C]
    row_out_out[half:, :] = outs[:, C:]
    col_out_out[...] = col_rest[:, :C]


def call(body, outs, *operands, smem=0, unread=0, scratch=(), name):
    vmem = pl.BlockSpec(memory_space=pltpu.VMEM)
    scalar = pl.BlockSpec(memory_space=pltpu.SMEM)
    return pl.pallas_call(
        body,
        out_shape=[jax.ShapeDtypeStruct(shape, kind) for shape, kind in outs],
        in_specs=[scalar] * smem + [vmem] * (len(operands) - smem - unread)
        + [pl.BlockSpec(memory_space=pl.ANY)] * unread,
        out_specs=[vmem] * len(outs),
        scratch_shapes=list(scratch),
        compiler_params=pltpu.CompilerParams(vmem_limit_bytes=32 * 1024 * 1024),
        name=name,
    )(*operands)


def shift_residues(values, away, count):
    return lax.ppermute(values, "res", [((i + away) % count, i) for i in range(count)])


def cross(values, at, seq_count, res_count, late_first=False):
    pairs = []
    for r in range(res_count):
        bit = 1 << step_bits(seq_count, r % 2, late_first)[at]
        pairs += [(i * res_count + r, (i ^ bit) * res_count + r) for i in range(seq_count)]
    return lax.ppermute(values, ("seq", "res"), pairs)


def swap_blocks(values):
    return lax.all_to_all(values, "seq", 0, 0, tiled=True)


def local(
    alignment,
    cotangent,
    pair_bias,
    norm_gains,
    row_project,
    row_output,
    column_project,
    column_output,
    residue_mask,
    sequence_mask,
    seq_count,
    res_count,
):
    n_seq, n_rows, _ = alignment.shape
    n_keys = pair_bias.shape[2]
    block = n_rows // seq_count
    group = n_seq * block
    away_range = range(1, res_count)
    present_keys = jnp.pad(residue_mask.astype(F32), (0, C - n_rows))
    present_keys = jnp.broadcast_to(present_keys[None, None, :], (1, n_rows, C))
    sent = jnp.concatenate([alignment.astype(F32), present_keys], axis=0)
    payload, exponent, unit, own_unit, memory, query_gate, mixture, inverse = call(
        functools.partial(row_forward, res_count),
        [
            ((seq_count, n_seq + 1, block, 2 * C), F32),
            ((n_seq, H * n_rows, n_keys), F32),
            ((n_seq, n_keys, C), F32),
            ((n_seq, n_rows, C), F32),
            ((n_seq, n_keys, 2 * C), F32),
            ((n_seq, n_rows, 2 * C), F32),
            ((n_seq, n_rows, C), F32),
            ((n_seq, n_rows, C), F32),
        ],
        sequence_mask, sent, *[shift_residues(sent, away, res_count) for away in away_range],
        alignment, cotangent, pair_bias, norm_gains, row_project, row_output,
        smem=1,
        scratch=[pltpu.VMEM((res_count, n_seq + 1, n_rows, C), F32)],
        name="row_forward",
    )
    arrived = swap_blocks(payload)
    (returned,) = call(
        functools.partial(column_step, n_seq=n_seq),
        [((seq_count, 3, block, 2 * C), F32)],
        arrived, norm_gains, column_project, column_output,
        scratch=[pltpu.VMEM((seq_count, group, 2 * C), F32), pltpu.VMEM((seq_count, group, C), F32)],
        name="column_step",
    )
    returned = swap_blocks(returned)
    part = -(-5 * C // (2 * ROWS * res_count)) * ROWS
    wide = H * n_rows
    keys_each = n_keys // seq_count
    left = seq_count // 2
    state, send, middle_grad, *sums = call(
        functools.partial(row_backward, res_count),
        [((left, keys_each, wide), F32)] * 2
        + [((n_seq, n_rows, C), F32)]
        + [((part + ROWS + n_rows, LANES), F32)] * res_count,
        returned, exponent, unit, memory, query_gate, mixture, inverse, own_unit, row_project, row_output,
        scratch=[
            pltpu.VMEM((res_count, part + ROWS + n_rows, LANES), F32),
            pltpu.VMEM((n_keys, wide), F32),
        ],
        name="row_backward",
    )
    sums = sums[:1] + [shift_residues(sums[away], -away, res_count) for away in away_range]
    arrived = cross(send, 0, seq_count, res_count)
    shared, normed = call(
        add_shares,
        [((part + ROWS, LANES), F32), ((n_rows, LANES), F32)],
        *sums,
        name="add_shares",
    )
    steps = seq_count.bit_length() - 1
    for at in range(steps):
        arrived_shared = cross(shared, at, seq_count, res_count, True)
        if at < steps - 1:
            left //= 2
            state, send = call(
                bias_step, [((left, keys_each, wide), F32)] * 2, state, arrived, name="bias_step"
            )
            arrived = cross(send, at + 1, seq_count, res_count)
            before = [send]
        else:
            (bias_grad,) = call(bias_last, [((H, keys_each, n_rows), F32)], state, arrived, name="bias_last")
            before = [bias_grad]
        pieces = ROWS << (at + 1)
        shapes = [(part + pieces, LANES)] if at < steps - 1 else [(part, LANES), (pieces, LANES)]
        shared, *joined = call(
            functools.partial(shared_step, part, len(before)),
            [(shape, F32) for shape in shapes],
            shared, arrived_shared, *before,
            unread=len(before),
            name="shared_step",
        )
    (grad_alignment,) = call(
        finish_alignment,
        [(alignment.shape, alignment.dtype)],
        alignment, middle_grad, norm_gains, normed,
        name="finish_alignment",
    )
    grads = call(
        functools.partial(unpack, res_count),
        [((2, C), F32), ((C, 4 * C), F32), ((C, C), F32), ((C, 2 * C + 2 * DH), F32), ((C, C), F32)],
        *joined, shared, *[shift_residues(shared, away, res_count) for away in away_range],
        norm_gains, row_project, column_project,
        scratch=[
            pltpu.VMEM((res_count, part, LANES), F32),
            pltpu.VMEM((seq_count, 2, C // seq_count, LANES), F32),
        ],
        name="unpack",
    )
    return (grad_alignment, jnp.transpose(bias_grad, (0, 2, 1)), *grads)


def solution(mesh):
    placed = (
        P("seq", "res", None),
        P("seq", "res", None),
        P(None, "res", None),
        P(),
        P(),
        P(),
        P(),
        P(),
        P("res"),
        P("seq"),
    )
    return jax.shard_map(
        functools.partial(local, seq_count=mesh.shape["seq"], res_count=mesh.shape["res"]),
        mesh=mesh,
        in_specs=placed,
        out_specs=(P("seq", "res", None), P(None, "res", "seq"), P(), P(), P(), P(), P()),
        check_vma=False,
    )
```

```python
import functools

import jax
import jax.numpy as jnp
from jax import lax
from jax.experimental import pallas as pl
from jax.experimental.pallas import tpu as pltpu
from jax.sharding import PartitionSpec as P

C = 64
H = 8
DH = 8
LANES = 128
ROWS = 8

EXACT = lax.Precision.HIGHEST
THREE = lax.Precision.HIGH
EPSILON = 1e-05
MASKED = 1000000000.0
SCALE = DH ** (-0.5)
F32 = jnp.float32


def dot(a, b, over=((1,), (0,)), precision=THREE):
    return lax.dot_general(a, b, (over, ((), ())), precision=precision, preferred_element_type=F32)


def dot_rows(a, b):
    return dot(a, b, ((0,), (0,)))


def dot_t(a, b, precision=THREE):
    return dot(a, b, ((1,), (1,)), precision)


def to_column(row):
    eye = lax.broadcasted_iota(jnp.int32, (C, C), 0) == lax.broadcasted_iota(jnp.int32, (C, C), 1)
    return jnp.sum(jnp.where(eye, row, 0.0), axis=1, keepdims=True)


def to_row(column):
    eye = lax.broadcasted_iota(jnp.int32, (C, C), 0) == lax.broadcasted_iota(jnp.int32, (C, C), 1)
    return jnp.sum(jnp.where(eye, column, 0.0), axis=0, keepdims=True)


def normalise(values):
    centred = values - jnp.mean(values, axis=-1, keepdims=True)
    inverse = lax.rsqrt(jnp.mean(centred * centred, axis=-1, keepdims=True) + EPSILON)
    return centred * inverse, inverse


def normalise_back(grad_normed, gain, unit, inverse):
    grad_unit = grad_normed * gain
    along = jnp.mean(grad_unit * unit, axis=-1, keepdims=True)
    return inverse * (grad_unit - jnp.mean(grad_unit, axis=-1, keepdims=True) - unit * along)


def head_mask(rows):
    row = lax.broadcasted_iota(jnp.int32, (H, rows, C), 0)
    channel = lax.broadcasted_iota(jnp.int32, (H, rows, C), 2)
    return (row == channel // DH).astype(F32).reshape(H * rows, C)


def spread_heads(values, mask):
    return jnp.concatenate([values] * H, axis=0) * mask


def join_heads(values, mask):
    masked = values * mask
    return jnp.sum(masked.reshape(H, -1, masked.shape[1]), axis=0)


def row_forward(n_res, seq_mask, *refs):
    sent = refs[:n_res]
    own, cotangent, bias, gains, w_row, w_out = refs[n_res : n_res + 6]
    payload, exponent_out, unit_out, own_unit_out, memory_out, query_gate_out, mixture_out, inverse_out, gathered = refs[n_res + 6 :]
    n_seq, n_rows, _ = own.shape
    me = lax.axis_index("res")
    for away in range(n_res):
        gathered[lax.rem(me + away, n_res)] = sent[away][...]
    n_keys = n_res * n_rows
    n_blocks = payload.shape[0]
    block = n_rows // n_blocks
    gain = gains[0:1, :]
    w_all = w_row[...]
    w_query_gate = jnp.concatenate([w_all[:, :C], w_all[:, 3 * C :]], axis=1)
    present_keys = jnp.concatenate([gathered[i, n_seq, 0:1, :n_rows] for i in range(n_res)], axis=1)
    key_bias = MASKED * (present_keys - 1.0)
    bias_rows = bias[...].reshape(H * n_rows, n_keys).astype(F32)
    mask = head_mask(n_rows)
    wide_mask = jnp.concatenate([mask, mask], axis=1)
    units = jnp.concatenate([gathered[:, s].reshape(n_keys, C) for s in range(n_seq)], axis=0)
    units, _ = normalise(units)
    memories = dot(units * gain, w_all[:, C : 3 * C], precision=EXACT)
    initial = own[...].reshape(n_seq * n_rows, C).astype(F32)
    own_units, _ = normalise(initial)
    projected = dot(own_units * gain, w_query_gate, precision=EXACT)
    queries = projected[:, :C] * SCALE
    gates = jax.nn.sigmoid(projected[:, C:])
    unit_out[...] = units.reshape(n_seq, n_keys, C)
    memory_out[...] = memories.reshape(n_seq, n_keys, 2 * C)
    own_unit_out[...] = own_units.reshape(n_seq, n_rows, C)
    query_gate_out[...] = jnp.concatenate([queries, gates], axis=1).reshape(n_seq, n_rows, 2 * C)
    sums = []
    for s in range(n_seq):
        memory = memories[s * n_keys : (s + 1) * n_keys]
        query = queries[s * n_rows : (s + 1) * n_rows]
        scores = dot_t(spread_heads(query, mask), memory[:, :C], EXACT) + bias_rows + key_bias
        exponent = jnp.exp(scores - jnp.max(scores, axis=-1, keepdims=True))
        exponent_out[s] = exponent
        summed = dot(exponent, jnp.concatenate([memory[:, C:], jnp.ones((n_keys, C), F32)], axis=1))
        sums.append(join_heads(summed, wide_mask))
    summed = jnp.concatenate(sums, axis=0)
    inverse = 1.0 / summed[:, C:]
    mixture = summed[:, :C] * inverse
    inverse_out[...] = inverse.reshape(n_seq, n_rows, C)
    mixture_out[...] = mixture.reshape(n_seq, n_rows, C)
    middle = initial + dot(gates * mixture, w_out[...])
    both = jnp.concatenate([middle, cotangent[...].reshape(n_seq * n_rows, C).astype(F32)], axis=1)
    for s in range(n_seq):
        for b in range(n_blocks):
            row = s * n_rows + b * block
            payload[b, s] = both[row : row + block, :]
    lane = lax.broadcasted_iota(jnp.int32, (block, 2 * C), 1) // (2 * C // n_seq)
    present = jnp.zeros((block, 2 * C), F32)
    for s in range(n_seq):
        present = jnp.where(lane == s, seq_mask[s].astype(F32), present)
    for b in range(n_blocks):
        payload[b, n_seq] = present


def column_step(arrived, gains, w_col, w_out, returned, gathered, mask_rows, n_seq):
    n_src, _, block, _ = arrived.shape
    group = n_seq * block
    rows = n_src * group
    wide = 2 * C // n_seq
    share = C // n_src
    for src in range(n_src):
        for s in range(n_seq):
            gathered[src, s * block : (s + 1) * block, :] = arrived[src, s]
            mask_rows[src, s * block : (s + 1) * block, :] = jnp.broadcast_to(
                arrived[src, n_seq, :, s * wide : s * wide + 1], (block, C)
            )
    data = gathered[...].reshape(rows, 2 * C)
    present = mask_rows[...]
    middle = data[:, :C]
    cot = data[:, C:]
    gain = gains[1:2, :]

    def over_sequences(values, combine, reduce):
        total = reduce(values.reshape(n_src, group, C), axis=0)
        result = total
        for shift in range(1, n_seq):
            result = combine(result, pltpu.roll(total, shift * block, 0))
        return result

    def total_of(values):
        return over_sequences(values, jnp.add, jnp.sum)

    def spread(values):
        return jnp.broadcast_to(values[None], (n_src, group, C)).reshape(rows, C)

    lane = lax.broadcasted_iota(jnp.int32, (C, C), 1)
    row = lax.broadcasted_iota(jnp.int32, (C, C), 0)
    same_head = (row // DH == lane // DH).astype(F32)
    repeat = (lax.broadcasted_iota(jnp.int32, (DH, C), 0) == lax.broadcasted_iota(jnp.int32, (DH, C), 1) % DH).astype(F32)
    w_all = w_col[...]
    w_query = w_all[:, :C]
    w_key = dot(w_all[:, C : C + DH], repeat, precision=EXACT)
    w_value = dot(w_all[:, C + DH : C + 2 * DH], repeat)
    w_gate = w_all[:, C + 2 * DH :]
    w_rest = jnp.concatenate([w_key, w_value, w_gate], axis=1)

    unit, inverse = normalise(middle)
    normed = unit * gain
    present_rows = present.reshape(rows, C)
    counted = total_of(present_rows)
    mean_unit = total_of(present_rows * unit) / counted
    mean_normed = mean_unit * gain
    query = dot(mean_normed, w_query, precision=EXACT) * SCALE
    query_rows = spread(query)
    rest = dot(normed, w_rest, precision=EXACT)
    key, value = rest[:, :C], rest[:, C : 2 * C]
    gate = jax.nn.sigmoid(rest[:, 2 * C :])
    scores = dot(query_rows * key, same_head, precision=EXACT) + MASKED * (present_rows - 1.0)
    peak = over_sequences(scores, jnp.maximum, jnp.max)
    exponent = jnp.exp(scores - spread(peak))
    weights = exponent / spread(total_of(exponent))
    mixture = total_of(weights * value)
    mixture_rows = spread(mixture)

    grad_gated = dot_t(cot, w_out[...])
    out_grad = dot_rows(gate * mixture_rows, cot)
    grad_mixture = total_of(gate * grad_gated)
    grad_mixture_rows = spread(grad_mixture)
    grad_gate = grad_gated * mixture_rows * gate * (1.0 - gate)
    grad_weights = dot(grad_mixture_rows * value, same_head)
    inner = spread(dot(grad_mixture * mixture, same_head))
    grad_scores = weights * (grad_weights - inner)
    grad_rest = jnp.concatenate([grad_scores * query_rows, weights * grad_mixture_rows, grad_gate], axis=1)
    grad_query = total_of(grad_scores * key) * SCALE
    grad_mean = dot_t(grad_query, w_query)
    grad_normed = present_rows * spread(grad_mean / counted) + dot_t(grad_rest, w_rest)
    grad_query_weights = dot_rows(mean_unit, grad_query) * (1.0 / n_seq)
    grad_rest_weights = dot_rows(unit, grad_rest)
    fold_row = lax.broadcasted_iota(jnp.int32, (2 * C, 2 * DH), 0)
    fold_lane = lax.broadcasted_iota(jnp.int32, (2 * C, 2 * DH), 1)
    fold = ((fold_row // C == fold_lane // DH) & (fold_row % DH == fold_lane % DH)).astype(F32)
    grad_key_value = dot(grad_rest_weights[:, : 2 * C], fold)
    first = jnp.concatenate([grad_query_weights, grad_rest_weights[:, 2 * C :]], axis=1)
    second = jnp.concatenate([out_grad, grad_key_value, jnp.zeros((C, C - 2 * DH), F32)], axis=1)
    grad_middle = (cot + normalise_back(grad_normed, gain, unit, inverse)).reshape(n_src, group, C)
    for src in range(n_src):
        for s in range(n_seq):
            returned[src, 0, :, s * C : (s + 1) * C] = grad_middle[src, s * block : (s + 1) * block, :]
        returned[src, 1] = first[src * share : (src + 1) * share, :]
        returned[src, 2] = second[src * share : (src + 1) * share, :]


def row_backward(n_res, returned, exponent_in, unit_in, memory_in, query_gate_in, mixture_in, inverse_in, own_unit_in,
                 w_row, w_out, state, send, middle_grad, *refs):
    sums_out, shares, bias_t = refs[:n_res], refs[n_res], refs[n_res + 1]
    me = lax.axis_index("res")
    n_seq, n_rows, _ = middle_grad.shape
    n_keys = memory_in.shape[1]
    n_blocks, _, block, _ = returned.shape
    w_all = w_row[...]
    w_memory = w_all[:, C : 3 * C]
    w_query_gate = jnp.concatenate([w_all[:, :C], w_all[:, 3 * C :]], axis=1)
    mask = head_mask(n_rows)
    for b in range(n_blocks):
        for s in range(n_seq):
            middle_grad[s, b * block : (b + 1) * block, :] = returned[b, 0, :, s * C : (s + 1) * C]
    grad_middle = middle_grad[...].reshape(n_seq * n_rows, C)
    queries_gates = query_gate_in[...].reshape(n_seq * n_rows, 2 * C)
    gates = queries_gates[:, C:]
    mixtures = mixture_in[...].reshape(n_seq * n_rows, C)
    grad_gated = dot_t(grad_middle, w_out[...])
    grad_out = dot_rows(gates * mixtures, grad_middle)
    grad_gates = grad_gated * mixtures * gates * (1.0 - gates)
    grad_mixtures = grad_gated * gates * inverse_in[...].reshape(n_seq * n_rows, C)
    inners = grad_mixtures * mixtures
    bias_grad = jnp.zeros((H * n_rows, n_keys), F32)
    grad_queries = []
    grad_memories = []
    for s in range(n_seq):
        rows = slice(s * n_rows, (s + 1) * n_rows)
        memory = memory_in[s]
        exponent = exponent_in[s]
        grad_heads = spread_heads(grad_mixtures[rows], mask)
        query_heads = spread_heads(queries_gates[rows, :C], mask)
        left = jnp.concatenate([grad_heads, spread_heads(inners[rows], mask)], axis=1)
        right = jnp.concatenate([memory[:, C:], jnp.full((n_keys, C), -1.0, F32)], axis=1)
        grad_scores = exponent * dot_t(left, right)
        bias_grad = bias_grad + grad_scores
        grad_queries.append(join_heads(dot(grad_scores, memory[:, :C]), mask) * SCALE)
        grad_key = dot_rows(grad_scores, query_heads)
        grad_value = dot_rows(exponent, grad_heads)
        grad_memories.append(jnp.concatenate([grad_key, grad_value], axis=1))
    grad_query_gate = jnp.concatenate([jnp.concatenate(grad_queries, axis=0), grad_gates], axis=1)
    grad_memory = jnp.concatenate(grad_memories, axis=0)
    grad_query_gate_weights = dot_rows(own_unit_in[...].reshape(n_seq * n_rows, C), grad_query_gate)
    grad_memory_weights = dot_rows(unit_in[...].reshape(n_seq * n_keys, C), grad_memory)
    from_memory = dot_t(grad_memory, w_memory)
    from_own = dot_t(grad_query_gate, w_query_gate)
    from_memory = [from_memory[s * n_keys : (s + 1) * n_keys] for s in range(n_seq)]
    from_own = [from_own[s * n_rows : (s + 1) * n_rows] for s in range(n_seq)]
    bias_t[...] = jnp.transpose(bias_grad)
    split_blocks(bias_t, state, send)

    half = C // 2
    weight_grads = jnp.concatenate(
        [grad_query_gate_weights, grad_memory_weights, jnp.concatenate([grad_out[:half], grad_out[half:]], axis=1)],
        axis=0,
    )
    part = shares.shape[1] - ROWS - n_rows
    shares[...] = jnp.zeros(shares.shape, F32)
    share = C // n_blocks
    column = jnp.sum(returned[:, 1:, :, :], axis=0)
    normed = jnp.concatenate(from_memory, axis=1)
    for i in range(n_res):
        rows = min(part, max(0, weight_grads.shape[0] - i * part))
        if rows:
            shares[i, :rows, :] = weight_grads[i * part : i * part + rows, :]
        shares[i, part : part + share, :] = column[0]
        shares[i, part + share : part + 2 * share, :] = column[1]
        shares[i, part + ROWS :, :] = normed[i * n_rows : (i + 1) * n_rows, :]
    for away in range(n_res):
        sums_out[away][...] = shares[lax.rem(me + away, n_res)]
    sums_out[0][part + ROWS :, :] += jnp.concatenate(from_own, axis=1)


def step_bits(n_seq_devices, odd, late_first=False):
    bits = list(range(n_seq_devices.bit_length() - 1))
    if odd:
        for i in range(0, len(bits) - 1, 2):
            bits[i], bits[i + 1] = bits[i + 1], bits[i]
    if late_first:
        middle = len(bits) // 2
        bits = bits[middle:] + bits[:middle]
    return bits


def relative_block(mask_of_bits, n_blocks, late_first=False):
    odd = lax.rem(lax.axis_index("res"), 2)
    even_mask = mask_of_bits(step_bits(n_blocks, False, late_first))
    odd_mask = mask_of_bits(step_bits(n_blocks, True, late_first))
    return lax.axis_index("seq") ^ (even_mask + odd * (odd_mask - even_mask))


def split_blocks(bias_t, state, send):
    n_blocks = state.shape[0] + send.shape[0]
    keys_each = bias_t.shape[0] // n_blocks
    half = n_blocks // 2

    for slot in range(n_blocks):

        def mask_of_bits(bits):
            last = len(bits) - 1
            return sum(1 << bit for at, bit in enumerate(bits) if slot >> (last - at) & 1)

        block = relative_block(mask_of_bits, n_blocks)
        values = bias_t[pl.ds(pl.multiple_of(block * keys_each, keys_each), keys_each), :]
        if slot < half:
            state[slot] = values
        else:
            send[slot - half] = values


def bias_step(state, arrived, state_out, send_out):
    total = state[...] + arrived[...]
    half = state_out.shape[0]
    state_out[...] = total[:half]
    send_out[...] = total[half:]


def bias_last(state, arrived, bias_out):
    total = state[0] + arrived[0]
    heads, _, n_rows = bias_out.shape
    for h in range(heads):
        bias_out[h] = total[:, h * n_rows : (h + 1) * n_rows]


def add_shares(*refs):
    sums, shared, normed = refs[:-2], refs[-2], refs[-1]
    total = sums[0][...]
    for more in sums[1:]:
        total = total + more[...]
    rows = shared.shape[0]
    shared[...] = total[:rows]
    normed[...] = total[rows:]


def shared_step(part, n_before, shared, arrived, *refs):
    outs = refs[n_before:]
    total = shared[:part] + arrived[:part]
    pieces = shared.shape[0] - part
    if len(outs) == 2:
        outs[0][...] = total
        joined, at = outs[1], 0
    else:
        outs[0][:part] = total
        joined, at = outs[0], part
    joined[at : at + pieces] = shared[part:]
    joined[at + pieces :] = arrived[part:]


def finish_alignment(own, middle_grad, gains, normed, out):
    n_seq = own.shape[0]
    for s in range(n_seq):
        unit, inverse = normalise(own[s].astype(F32))
        grad_normed = normed[:, s * C : (s + 1) * C]
        out[s] = (middle_grad[s] + normalise_back(grad_normed, gains[0:1, :], unit, inverse)).astype(out.dtype)


def unpack(n_res, joined, *refs):
    parts = refs[:n_res]
    gains, w_row, w_col, gains_out, row_project_out, row_out_out, col_project_out, col_out_out = refs[n_res : n_res + 8]
    shares, column = refs[n_res + 8 :]
    me = lax.axis_index("res")
    part = shares.shape[1]
    for away in range(n_res):
        shares[lax.rem(me + away, n_res)] = parts[away][...]
    n_blocks, _, share, _ = column.shape
    for slot in range(n_blocks):
        block = relative_block(
            lambda bits: sum(1 << bit for at, bit in enumerate(bits) if slot >> at & 1), n_blocks, True
        )
        piece = joined[slot * ROWS : (slot + 1) * ROWS, :]
        column[block, 0] = piece[:share]
        column[block, 1] = piece[share : 2 * share]
    flat = jnp.concatenate([shares[i] for i in range(n_res)], axis=0)
    query_gate, memory, outs = flat[:C], flat[C : 2 * C], flat[2 * C : 2 * C + C // 2]
    col_query_gate = jnp.concatenate([column[i, 0] for i in range(n_blocks)], axis=0)
    col_rest = jnp.concatenate([column[i, 1] for i in range(n_blocks)], axis=0)
    rest = col_rest[:, C : C + 2 * DH]
    gain_row = to_column(gains[0:1, :])
    gain_col = to_column(gains[1:2, :])
    w_all = w_row[...]
    w_column = w_col[...]
    row_gain_grad = (
        jnp.sum(query_gate[:, :C] * w_all[:, :C], axis=1, keepdims=True)
        + jnp.sum(memory * w_all[:, C : 3 * C], axis=1, keepdims=True)
        + jnp.sum(query_gate[:, C:] * w_all[:, 3 * C :], axis=1, keepdims=True)
    )
    col_gain_grad = (
        jnp.sum(col_query_gate[:, :C] * w_column[:, :C], axis=1, keepdims=True)
        + jnp.sum(rest * w_column[:, C : C + 2 * DH], axis=1, keepdims=True)
        + jnp.sum(col_query_gate[:, C:] * w_column[:, C + 2 * DH :], axis=1, keepdims=True)
    )
    gains_out[0:1, :] = to_row(row_gain_grad)
    gains_out[1:2, :] = to_row(col_gain_grad)
    row_project_out[:, :C] = query_gate[:, :C] * gain_row
    row_project_out[:, C : 3 * C] = memory * gain_row
    row_project_out[:, 3 * C :] = query_gate[:, C:] * gain_row
    col_project_out[:, :C] = col_query_gate[:, :C] * gain_col
    col_project_out[:, C : C + 2 * DH] = rest * gain_col
    col_project_out[:, C + 2 * DH :] = col_query_gate[:, C:] * gain_col
    half = C // 2
    row_out_out[:half, :] = outs[:, :C]
    row_out_out[half:, :] = outs[:, C:]
    col_out_out[...] = col_rest[:, :C]


def call(body, outs, *operands, smem=0, unread=0, scratch=(), name):
    vmem = pl.BlockSpec(memory_space=pltpu.VMEM)
    scalar = pl.BlockSpec(memory_space=pltpu.SMEM)
    return pl.pallas_call(
        body,
        out_shape=[jax.ShapeDtypeStruct(shape, kind) for shape, kind in outs],
        in_specs=[scalar] * smem + [vmem] * (len(operands) - smem - unread)
        + [pl.BlockSpec(memory_space=pl.ANY)] * unread,
        out_specs=[vmem] * len(outs),
        scratch_shapes=list(scratch),
        compiler_params=pltpu.CompilerParams(vmem_limit_bytes=32 * 1024 * 1024),
        name=name,
    )(*operands)


def shift_residues(values, away, count):
    return lax.ppermute(values, "res", [((i + away) % count, i) for i in range(count)])


def cross(values, at, seq_count, res_count, late_first=False):
    pairs = []
    for r in range(res_count):
        bit = 1 << step_bits(seq_count, r % 2, late_first)[at]
        pairs += [(i * res_count + r, (i ^ bit) * res_count + r) for i in range(seq_count)]
    return lax.ppermute(values, ("seq", "res"), pairs)


def swap_blocks(values):
    return lax.all_to_all(values, "seq", 0, 0, tiled=True)


def local(
    alignment,
    cotangent,
    pair_bias,
    norm_gains,
    row_project,
    row_output,
    column_project,
    column_output,
    residue_mask,
    sequence_mask,
    seq_count,
    res_count,
):
    n_seq, n_rows, _ = alignment.shape
    n_keys = pair_bias.shape[2]
    block = n_rows // seq_count
    group = n_seq * block
    away_range = range(1, res_count)
    present_keys = jnp.pad(residue_mask.astype(F32), (0, C - n_rows))
    present_keys = jnp.broadcast_to(present_keys[None, None, :], (1, n_rows, C))
    sent = jnp.concatenate([alignment.astype(F32), present_keys], axis=0)
    payload, exponent, unit, own_unit, memory, query_gate, mixture, inverse = call(
        functools.partial(row_forward, res_count),
        [
            ((seq_count, n_seq + 1, block, 2 * C), F32),
            ((n_seq, H * n_rows, n_keys), F32),
            ((n_seq, n_keys, C), F32),
            ((n_seq, n_rows, C), F32),
            ((n_seq, n_keys, 2 * C), F32),
            ((n_seq, n_rows, 2 * C), F32),
            ((n_seq, n_rows, C), F32),
            ((n_seq, n_rows, C), F32),
        ],
        sequence_mask, sent, *[shift_residues(sent, away, res_count) for away in away_range],
        alignment, cotangent, pair_bias, norm_gains, row_project, row_output,
        smem=1,
        scratch=[pltpu.VMEM((res_count, n_seq + 1, n_rows, C), F32)],
        name="row_forward",
    )
    arrived = swap_blocks(payload)
    (returned,) = call(
        functools.partial(column_step, n_seq=n_seq),
        [((seq_count, 3, block, 2 * C), F32)],
        arrived, norm_gains, column_project, column_output,
        scratch=[pltpu.VMEM((seq_count, group, 2 * C), F32), pltpu.VMEM((seq_count, group, C), F32)],
        name="column_step",
    )
    returned = swap_blocks(returned)
    part = -(-5 * C // (2 * ROWS * res_count)) * ROWS
    wide = H * n_rows
    keys_each = n_keys // seq_count
    left = seq_count // 2
    state, send, middle_grad, *sums = call(
        functools.partial(row_backward, res_count),
        [((left, keys_each, wide), F32)] * 2
        + [((n_seq, n_rows, C), F32)]
        + [((part + ROWS + n_rows, LANES), F32)] * res_count,
        returned, exponent, unit, memory, query_gate, mixture, inverse, own_unit, row_project, row_output,
        scratch=[
            pltpu.VMEM((res_count, part + ROWS + n_rows, LANES), F32),
            pltpu.VMEM((n_keys, wide), F32),
        ],
        name="row_backward",
    )
    sums = sums[:1] + [shift_residues(sums[away], -away, res_count) for away in away_range]
    steps = seq_count.bit_length() - 1
    arrivals = []
    before = []
    for at in range(steps):
        arrivals.append(cross(send, at, seq_count, res_count))
        if at < steps - 1:
            left //= 2
            state, send = call(
                bias_step, [((left, keys_each, wide), F32)] * 2, state, arrivals[at], name="bias_step"
            )
            before.append([send] if at == 0 else [])
    before = [before[0]] + [[arrived] for arrived in arrivals[2:]] + [[]]
    (bias_grad,) = call(bias_last, [((H, keys_each, n_rows), F32)], state, arrivals[-1], name="bias_last")
    shared, normed = call(
        add_shares,
        [((part + ROWS, LANES), F32), ((n_rows, LANES), F32)],
        *sums,
        name="add_shares",
    )
    for at in range(steps):
        arrived_shared = cross(shared, at, seq_count, res_count, True)
        pieces = ROWS << (at + 1)
        shapes = [(part + pieces, LANES)] if at < steps - 1 else [(part, LANES), (pieces, LANES)]
        shared, *joined = call(
            functools.partial(shared_step, part, len(before[at])),
            [(shape, F32) for shape in shapes],
            shared, arrived_shared, *before[at],
            unread=len(before[at]),
            name="shared_step",
        )
    (grad_alignment,) = call(
        finish_alignment,
        [(alignment.shape, alignment.dtype)],
        alignment, middle_grad, norm_gains, normed,
        name="finish_alignment",
    )
    grads = call(
        functools.partial(unpack, res_count),
        [((2, C), F32), ((C, 4 * C), F32), ((C, C), F32), ((C, 2 * C + 2 * DH), F32), ((C, C), F32)],
        *joined, shared, *[shift_residues(shared, away, res_count) for away in away_range],
        norm_gains, row_project, column_project,
        scratch=[
            pltpu.VMEM((res_count, part, LANES), F32),
            pltpu.VMEM((seq_count, 2, C // seq_count, LANES), F32),
        ],
        name="unpack",
    )
    return (grad_alignment, jnp.transpose(bias_grad, (0, 2, 1)), *grads)


def solution(mesh):
    placed = (
        P("seq", "res", None),
        P("seq", "res", None),
        P(None, "res", None),
        P(),
        P(),
        P(),
        P(),
        P(),
        P("res"),
        P("seq"),
    )
    return jax.shard_map(
        functools.partial(local, seq_count=mesh.shape["seq"], res_count=mesh.shape["res"]),
        mesh=mesh,
        in_specs=placed,
        out_specs=(P("seq", "res", None), P(None, "res", "seq"), P(), P(), P(), P(), P()),
        check_vma=False,
    )
```

```python
import functools

import jax
import jax.numpy as jnp
from jax import lax
from jax.experimental import pallas as pl
from jax.experimental.pallas import tpu as pltpu
from jax.sharding import PartitionSpec as P

C = 64
H = 8
DH = 8
LANES = 128
ROWS = 8

EXACT = lax.Precision.HIGHEST
THREE = lax.Precision.HIGH
EPSILON = 1e-05
MASKED = 1000000000.0
SCALE = DH ** (-0.5)
F32 = jnp.float32


def dot(a, b, over=((1,), (0,)), precision=THREE):
    return lax.dot_general(a, b, (over, ((), ())), precision=precision, preferred_element_type=F32)


def dot_rows(a, b):
    return dot(a, b, ((0,), (0,)))


def dot_t(a, b, precision=THREE):
    return dot(a, b, ((1,), (1,)), precision)


def to_column(row):
    eye = lax.broadcasted_iota(jnp.int32, (C, C), 0) == lax.broadcasted_iota(jnp.int32, (C, C), 1)
    return jnp.sum(jnp.where(eye, row, 0.0), axis=1, keepdims=True)


def to_row(column):
    eye = lax.broadcasted_iota(jnp.int32, (C, C), 0) == lax.broadcasted_iota(jnp.int32, (C, C), 1)
    return jnp.sum(jnp.where(eye, column, 0.0), axis=0, keepdims=True)


def normalise(values):
    centred = values - jnp.mean(values, axis=-1, keepdims=True)
    inverse = lax.rsqrt(jnp.mean(centred * centred, axis=-1, keepdims=True) + EPSILON)
    return centred * inverse, inverse


def normalise_back(grad_normed, gain, unit, inverse):
    grad_unit = grad_normed * gain
    along = jnp.mean(grad_unit * unit, axis=-1, keepdims=True)
    return inverse * (grad_unit - jnp.mean(grad_unit, axis=-1, keepdims=True) - unit * along)


def head_mask(rows):
    row = lax.broadcasted_iota(jnp.int32, (H, rows, C), 0)
    channel = lax.broadcasted_iota(jnp.int32, (H, rows, C), 2)
    return (row == channel // DH).astype(F32).reshape(H * rows, C)


def spread_heads(values, mask):
    return jnp.concatenate([values] * H, axis=0) * mask


def join_heads(values, mask):
    masked = values * mask
    return jnp.sum(masked.reshape(H, -1, masked.shape[1]), axis=0)


def row_forward(n_res, seq_mask, *refs):
    sent = refs[:n_res]
    own, cotangent, bias, gains, w_row, w_out = refs[n_res : n_res + 6]
    payload, exponent_out, unit_out, own_unit_out, memory_out, query_gate_out, mixture_out, inverse_out, gathered = refs[n_res + 6 :]
    n_seq, n_rows, _ = own.shape
    me = lax.axis_index("res")
    for away in range(n_res):
        gathered[lax.rem(me + away, n_res)] = sent[away][...]
    n_keys = n_res * n_rows
    n_blocks = payload.shape[0]
    block = n_rows // n_blocks
    gain = gains[0:1, :]
    w_all = w_row[...]
    w_query_gate = jnp.concatenate([w_all[:, :C], w_all[:, 3 * C :]], axis=1)
    present_keys = jnp.concatenate([gathered[i, n_seq, 0:1, :n_rows] for i in range(n_res)], axis=1)
    key_bias = MASKED * (present_keys - 1.0)
    bias_rows = bias[...].reshape(H * n_rows, n_keys).astype(F32)
    mask = head_mask(n_rows)
    wide_mask = jnp.concatenate([mask, mask], axis=1)
    units = jnp.concatenate([gathered[:, s].reshape(n_keys, C) for s in range(n_seq)], axis=0)
    units, _ = normalise(units)
    memories = dot(units * gain, w_all[:, C : 3 * C], precision=EXACT)
    initial = own[...].reshape(n_seq * n_rows, C).astype(F32)
    own_units, _ = normalise(initial)
    projected = dot(own_units * gain, w_query_gate, precision=EXACT)
    queries = projected[:, :C] * SCALE
    gates = jax.nn.sigmoid(projected[:, C:])
    unit_out[...] = units.reshape(n_seq, n_keys, C)
    memory_out[...] = memories.reshape(n_seq, n_keys, 2 * C)
    own_unit_out[...] = own_units.reshape(n_seq, n_rows, C)
    query_gate_out[...] = jnp.concatenate([queries, gates], axis=1).reshape(n_seq, n_rows, 2 * C)
    sums = []
    for s in range(n_seq):
        memory = memories[s * n_keys : (s + 1) * n_keys]
        query = queries[s * n_rows : (s + 1) * n_rows]
        scores = dot_t(spread_heads(query, mask), memory[:, :C], EXACT) + bias_rows + key_bias
        exponent = jnp.exp(scores - jnp.max(scores, axis=-1, keepdims=True))
        exponent_out[s] = exponent
        summed = dot(exponent, jnp.concatenate([memory[:, C:], jnp.ones((n_keys, C), F32)], axis=1))
        sums.append(join_heads(summed, wide_mask))
    summed = jnp.concatenate(sums, axis=0)
    inverse = 1.0 / summed[:, C:]
    mixture = summed[:, :C] * inverse
    inverse_out[...] = inverse.reshape(n_seq, n_rows, C)
    mixture_out[...] = mixture.reshape(n_seq, n_rows, C)
    middle = initial + dot(gates * mixture, w_out[...])
    both = jnp.concatenate([middle, cotangent[...].reshape(n_seq * n_rows, C).astype(F32)], axis=1)
    for s in range(n_seq):
        for b in range(n_blocks):
            row = s * n_rows + b * block
            payload[b, s] = both[row : row + block, :]
    lane = lax.broadcasted_iota(jnp.int32, (block, 2 * C), 1) // (2 * C // n_seq)
    present = jnp.zeros((block, 2 * C), F32)
    for s in range(n_seq):
        present = jnp.where(lane == s, seq_mask[s].astype(F32), present)
    for b in range(n_blocks):
        payload[b, n_seq] = present


def column_step(arrived, gains, w_col, w_out, returned, gathered, mask_rows, n_seq):
    n_src, _, block, _ = arrived.shape
    group = n_seq * block
    rows = n_src * group
    wide = 2 * C // n_seq
    share = C // n_src
    for src in range(n_src):
        for s in range(n_seq):
            gathered[src, s * block : (s + 1) * block, :] = arrived[src, s]
            mask_rows[src, s * block : (s + 1) * block, :] = jnp.broadcast_to(
                arrived[src, n_seq, :, s * wide : s * wide + 1], (block, C)
            )
    data = gathered[...].reshape(rows, 2 * C)
    present = mask_rows[...]
    middle = data[:, :C]
    cot = data[:, C:]
    gain = gains[1:2, :]

    def over_sequences(values, combine, reduce):
        total = reduce(values.reshape(n_src, group, C), axis=0)
        result = total
        for shift in range(1, n_seq):
            result = combine(result, pltpu.roll(total, shift * block, 0))
        return result

    def total_of(values):
        return over_sequences(values, jnp.add, jnp.sum)

    def spread(values):
        return jnp.broadcast_to(values[None], (n_src, group, C)).reshape(rows, C)

    lane = lax.broadcasted_iota(jnp.int32, (C, C), 1)
    row = lax.broadcasted_iota(jnp.int32, (C, C), 0)
    same_head = (row // DH == lane // DH).astype(F32)
    repeat = (lax.broadcasted_iota(jnp.int32, (DH, C), 0) == lax.broadcasted_iota(jnp.int32, (DH, C), 1) % DH).astype(F32)
    w_all = w_col[...]
    w_query = w_all[:, :C]
    w_key = dot(w_all[:, C : C + DH], repeat, precision=EXACT)
    w_value = dot(w_all[:, C + DH : C + 2 * DH], repeat)
    w_gate = w_all[:, C + 2 * DH :]
    w_rest = jnp.concatenate([w_key, w_value, w_gate], axis=1)

    unit, inverse = normalise(middle)
    normed = unit * gain
    present_rows = present.reshape(rows, C)
    counted = total_of(present_rows)
    mean_unit = total_of(present_rows * unit) / counted
    mean_normed = mean_unit * gain
    query = dot(mean_normed, w_query, precision=EXACT) * SCALE
    query_rows = spread(query)
    rest = dot(normed, w_rest, precision=EXACT)
    key, value = rest[:, :C], rest[:, C : 2 * C]
    gate = jax.nn.sigmoid(rest[:, 2 * C :])
    scores = dot(query_rows * key, same_head, precision=EXACT) + MASKED * (present_rows - 1.0)
    peak = over_sequences(scores, jnp.maximum, jnp.max)
    exponent = jnp.exp(scores - spread(peak))
    weights = exponent / spread(total_of(exponent))
    mixture = total_of(weights * value)
    mixture_rows = spread(mixture)

    grad_gated = dot_t(cot, w_out[...])
    out_grad = dot_rows(gate * mixture_rows, cot)
    grad_mixture = total_of(gate * grad_gated)
    grad_mixture_rows = spread(grad_mixture)
    grad_gate = grad_gated * mixture_rows * gate * (1.0 - gate)
    grad_weights = dot(grad_mixture_rows * value, same_head)
    inner = spread(dot(grad_mixture * mixture, same_head))
    grad_scores = weights * (grad_weights - inner)
    grad_rest = jnp.concatenate([grad_scores * query_rows, weights * grad_mixture_rows, grad_gate], axis=1)
    grad_query = total_of(grad_scores * key) * SCALE
    grad_mean = dot_t(grad_query, w_query)
    grad_normed = present_rows * spread(grad_mean / counted) + dot_t(grad_rest, w_rest)
    grad_query_weights = dot_rows(mean_unit, grad_query) * (1.0 / n_seq)
    grad_rest_weights = dot_rows(unit, grad_rest)
    fold_row = lax.broadcasted_iota(jnp.int32, (2 * C, 2 * DH), 0)
    fold_lane = lax.broadcasted_iota(jnp.int32, (2 * C, 2 * DH), 1)
    fold = ((fold_row // C == fold_lane // DH) & (fold_row % DH == fold_lane % DH)).astype(F32)
    grad_key_value = dot(grad_rest_weights[:, : 2 * C], fold)
    first = jnp.concatenate([grad_query_weights, grad_rest_weights[:, 2 * C :]], axis=1)
    second = jnp.concatenate([out_grad, grad_key_value, jnp.zeros((C, C - 2 * DH), F32)], axis=1)
    grad_middle = (cot + normalise_back(grad_normed, gain, unit, inverse)).reshape(n_src, group, C)
    for src in range(n_src):
        for s in range(n_seq):
            returned[src, 0, :, s * C : (s + 1) * C] = grad_middle[src, s * block : (s + 1) * block, :]
        returned[src, 1] = first[src * share : (src + 1) * share, :]
        returned[src, 2] = second[src * share : (src + 1) * share, :]


def row_backward(n_res, returned, exponent_in, unit_in, memory_in, query_gate_in, mixture_in, inverse_in, own_unit_in,
                 w_row, w_out, state, send, middle_grad, *refs):
    sums_out, shares, bias_t = refs[:n_res], refs[n_res], refs[n_res + 1]
    me = lax.axis_index("res")
    n_seq, n_rows, _ = middle_grad.shape
    n_keys = memory_in.shape[1]
    n_blocks, _, block, _ = returned.shape
    w_all = w_row[...]
    w_memory = w_all[:, C : 3 * C]
    w_query_gate = jnp.concatenate([w_all[:, :C], w_all[:, 3 * C :]], axis=1)
    mask = head_mask(n_rows)
    for b in range(n_blocks):
        for s in range(n_seq):
            middle_grad[s, b * block : (b + 1) * block, :] = returned[b, 0, :, s * C : (s + 1) * C]
    grad_middle = middle_grad[...].reshape(n_seq * n_rows, C)
    queries_gates = query_gate_in[...].reshape(n_seq * n_rows, 2 * C)
    gates = queries_gates[:, C:]
    mixtures = mixture_in[...].reshape(n_seq * n_rows, C)
    grad_gated = dot_t(grad_middle, w_out[...])
    grad_out = dot_rows(gates * mixtures, grad_middle)
    grad_gates = grad_gated * mixtures * gates * (1.0 - gates)
    grad_mixtures = grad_gated * gates * inverse_in[...].reshape(n_seq * n_rows, C)
    inners = grad_mixtures * mixtures
    bias_grad = jnp.zeros((H * n_rows, n_keys), F32)
    grad_queries = []
    grad_memories = []
    for s in range(n_seq):
        rows = slice(s * n_rows, (s + 1) * n_rows)
        memory = memory_in[s]
        exponent = exponent_in[s]
        grad_heads = spread_heads(grad_mixtures[rows], mask)
        query_heads = spread_heads(queries_gates[rows, :C], mask)
        left = jnp.concatenate([grad_heads, spread_heads(inners[rows], mask)], axis=1)
        right = jnp.concatenate([memory[:, C:], jnp.full((n_keys, C), -1.0, F32)], axis=1)
        grad_scores = exponent * dot_t(left, right)
        bias_grad = bias_grad + grad_scores
        grad_queries.append(join_heads(dot(grad_scores, memory[:, :C]), mask) * SCALE)
        grad_key = dot_rows(grad_scores, query_heads)
        grad_value = dot_rows(exponent, grad_heads)
        grad_memories.append(jnp.concatenate([grad_key, grad_value], axis=1))
    grad_query_gate = jnp.concatenate([jnp.concatenate(grad_queries, axis=0), grad_gates], axis=1)
    grad_memory = jnp.concatenate(grad_memories, axis=0)
    grad_query_gate_weights = dot_rows(own_unit_in[...].reshape(n_seq * n_rows, C), grad_query_gate)
    grad_memory_weights = dot_rows(unit_in[...].reshape(n_seq * n_keys, C), grad_memory)
    from_memory = dot_t(grad_memory, w_memory)
    from_own = dot_t(grad_query_gate, w_query_gate)
    from_memory = [from_memory[s * n_keys : (s + 1) * n_keys] for s in range(n_seq)]
    from_own = [from_own[s * n_rows : (s + 1) * n_rows] for s in range(n_seq)]
    bias_t[...] = jnp.transpose(bias_grad)
    split_blocks(bias_t, state, send)

    half = C // 2
    weight_grads = jnp.concatenate(
        [grad_query_gate_weights, grad_memory_weights, jnp.concatenate([grad_out[:half], grad_out[half:]], axis=1)],
        axis=0,
    )
    part = shares.shape[1] - ROWS - n_rows
    shares[...] = jnp.zeros(shares.shape, F32)
    share = C // n_blocks
    column = jnp.sum(returned[:, 1:, :, :], axis=0)
    normed = jnp.concatenate(from_memory, axis=1)
    for i in range(n_res):
        rows = min(part, max(0, weight_grads.shape[0] - i * part))
        if rows:
            shares[i, :rows, :] = weight_grads[i * part : i * part + rows, :]
        shares[i, part : part + share, :] = column[0]
        shares[i, part + share : part + 2 * share, :] = column[1]
        shares[i, part + ROWS :, :] = normed[i * n_rows : (i + 1) * n_rows, :]
    for away in range(n_res):
        sums_out[away][...] = shares[lax.rem(me + away, n_res)]
    sums_out[0][part + ROWS :, :] += jnp.concatenate(from_own, axis=1)


def step_bits(n_seq_devices, odd):
    bits = list(range(n_seq_devices.bit_length() - 1))
    if odd:
        for i in range(0, len(bits) - 1, 2):
            bits[i], bits[i + 1] = bits[i + 1], bits[i]
    return bits


def relative_block(mask_of_bits, n_blocks):
    odd = lax.rem(lax.axis_index("res"), 2)
    even_mask = mask_of_bits(step_bits(n_blocks, False))
    odd_mask = mask_of_bits(step_bits(n_blocks, True))
    return lax.axis_index("seq") ^ (even_mask + odd * (odd_mask - even_mask))


def split_blocks(bias_t, state, send):
    tiles = bias_t.shape[1] // LANES
    n_blocks = (state.shape[0] + send.shape[0]) // tiles
    keys_each = bias_t.shape[0] // n_blocks
    half = n_blocks // 2

    for slot in range(n_blocks):

        def mask_of_bits(bits):
            last = len(bits) - 1
            return sum(1 << bit for at, bit in enumerate(bits) if slot >> (last - at) & 1)

        block = relative_block(mask_of_bits, n_blocks)
        values = bias_t[pl.ds(pl.multiple_of(block * keys_each, keys_each), keys_each), :]
        for i in range(tiles):
            out, at = (state, slot) if slot < half else (send, slot - half)
            out[at * tiles + i] = values[:, i * LANES : (i + 1) * LANES]


def bias_last(state, arrived, bias_out):
    heads, _, n_rows = bias_out.shape
    each = LANES // n_rows
    for i in range(state.shape[0]):
        total = state[i] + arrived[i]
        for e in range(each):
            bias_out[i * each + e] = total[:, e * n_rows : (e + 1) * n_rows]


def add_shares(bias_send, *refs):
    sums, send, normed = refs[:-2], refs[-2], refs[-1]
    total = sums[0][...]
    for more in sums[1:]:
        total = total + more[...]
    left = bias_send.shape[0]
    rows = total.shape[0] - normed.shape[0]
    send[:left] = bias_send[...]
    send[left:] = total[:rows].reshape(rows // ROWS, ROWS, LANES)
    normed[...] = total[rows:]


def step(part, state, sent, arrived, state_out, send):
    left = state.shape[0]
    half = left // 2
    total = state[...] + arrived[:left]
    state_out[...] = total[:half]
    send[:half] = total[half:]
    send[half : half + part] = sent[left : left + part] + arrived[left : left + part]
    pieces = sent.shape[0] - left - part
    send[half + part : half + part + pieces] = sent[left + part :]
    send[half + part + pieces :] = arrived[left + part :]


def last_step(sent, arrived, _, shared, joined):
    part = shared.shape[0]
    pieces = joined.shape[0] // 2
    left = sent.shape[0] - part - pieces
    shared[...] = sent[left : left + part] + arrived[left : left + part]
    joined[:pieces] = sent[left + part :]
    joined[pieces:] = arrived[left + part :]


def finish_alignment(own, middle_grad, gains, normed, out, done):
    n_seq = own.shape[0]
    done[...] = jnp.zeros(done.shape, F32)
    for s in range(n_seq):
        unit, inverse = normalise(own[s].astype(F32))
        grad_normed = normed[:, s * C : (s + 1) * C]
        out[s] = (middle_grad[s] + normalise_back(grad_normed, gains[0:1, :], unit, inverse)).astype(out.dtype)


def unpack(n_res, joined, *refs):
    parts = refs[:n_res]
    gains, w_row, w_col, gains_out, row_project_out, row_out_out, col_project_out, col_out_out = refs[n_res : n_res + 8]
    shares, column = refs[n_res + 8 :]
    me = lax.axis_index("res")
    part = shares.shape[1]
    for away in range(n_res):
        shares[lax.rem(me + away, n_res)] = parts[away][...].reshape(part, LANES)
    n_blocks, _, share, _ = column.shape
    for slot in range(n_blocks):
        block = relative_block(
            lambda bits: sum(1 << bit for at, bit in enumerate(bits) if slot >> at & 1), n_blocks
        )
        piece = joined[slot]
        column[block, 0] = piece[:share]
        column[block, 1] = piece[share : 2 * share]
    flat = jnp.concatenate([shares[i] for i in range(n_res)], axis=0)
    query_gate, memory, outs = flat[:C], flat[C : 2 * C], flat[2 * C : 2 * C + C // 2]
    col_query_gate = jnp.concatenate([column[i, 0] for i in range(n_blocks)], axis=0)
    col_rest = jnp.concatenate([column[i, 1] for i in range(n_blocks)], axis=0)
    rest = col_rest[:, C : C + 2 * DH]
    gain_row = to_column(gains[0:1, :])
    gain_col = to_column(gains[1:2, :])
    w_all = w_row[...]
    w_column = w_col[...]
    row_gain_grad = (
        jnp.sum(query_gate[:, :C] * w_all[:, :C], axis=1, keepdims=True)
        + jnp.sum(memory * w_all[:, C : 3 * C], axis=1, keepdims=True)
        + jnp.sum(query_gate[:, C:] * w_all[:, 3 * C :], axis=1, keepdims=True)
    )
    col_gain_grad = (
        jnp.sum(col_query_gate[:, :C] * w_column[:, :C], axis=1, keepdims=True)
        + jnp.sum(rest * w_column[:, C : C + 2 * DH], axis=1, keepdims=True)
        + jnp.sum(col_query_gate[:, C:] * w_column[:, C + 2 * DH :], axis=1, keepdims=True)
    )
    gains_out[0:1, :] = to_row(row_gain_grad)
    gains_out[1:2, :] = to_row(col_gain_grad)
    row_project_out[:, :C] = query_gate[:, :C] * gain_row
    row_project_out[:, C : 3 * C] = memory * gain_row
    row_project_out[:, 3 * C :] = query_gate[:, C:] * gain_row
    col_project_out[:, :C] = col_query_gate[:, :C] * gain_col
    col_project_out[:, C : C + 2 * DH] = rest * gain_col
    col_project_out[:, C + 2 * DH :] = col_query_gate[:, C:] * gain_col
    half = C // 2
    row_out_out[:half, :] = outs[:, :C]
    row_out_out[half:, :] = outs[:, C:]
    col_out_out[...] = col_rest[:, :C]


def call(body, outs, *operands, smem=0, unread=0, scratch=(), name):
    vmem = pl.BlockSpec(memory_space=pltpu.VMEM)
    scalar = pl.BlockSpec(memory_space=pltpu.SMEM)
    return pl.pallas_call(
        body,
        out_shape=[jax.ShapeDtypeStruct(shape, kind) for shape, kind in outs],
        in_specs=[scalar] * smem + [vmem] * (len(operands) - smem - unread)
        + [pl.BlockSpec(memory_space=pl.ANY)] * unread,
        out_specs=[vmem] * len(outs),
        scratch_shapes=list(scratch),
        compiler_params=pltpu.CompilerParams(vmem_limit_bytes=32 * 1024 * 1024),
        name=name,
    )(*operands)


def shift_residues(values, away, count):
    return lax.ppermute(values, "res", [((i + away) % count, i) for i in range(count)])


def cross(values, at, seq_count, res_count):
    pairs = []
    for r in range(res_count):
        bit = 1 << step_bits(seq_count, r % 2)[at]
        pairs += [(i * res_count + r, (i ^ bit) * res_count + r) for i in range(seq_count)]
    return lax.ppermute(values, ("seq", "res"), pairs)


def swap_blocks(values):
    return lax.all_to_all(values, "seq", 0, 0, tiled=True)


def local(
    alignment,
    cotangent,
    pair_bias,
    norm_gains,
    row_project,
    row_output,
    column_project,
    column_output,
    residue_mask,
    sequence_mask,
    seq_count,
    res_count,
):
    n_seq, n_rows, _ = alignment.shape
    n_keys = pair_bias.shape[2]
    block = n_rows // seq_count
    group = n_seq * block
    away_range = range(1, res_count)
    present_keys = jnp.pad(residue_mask.astype(F32), (0, C - n_rows))
    present_keys = jnp.broadcast_to(present_keys[None, None, :], (1, n_rows, C))
    sent = jnp.concatenate([alignment.astype(F32), present_keys], axis=0)
    payload, exponent, unit, own_unit, memory, query_gate, mixture, inverse = call(
        functools.partial(row_forward, res_count),
        [
            ((seq_count, n_seq + 1, block, 2 * C), F32),
            ((n_seq, H * n_rows, n_keys), F32),
            ((n_seq, n_keys, C), F32),
            ((n_seq, n_rows, C), F32),
            ((n_seq, n_keys, 2 * C), F32),
            ((n_seq, n_rows, 2 * C), F32),
            ((n_seq, n_rows, C), F32),
            ((n_seq, n_rows, C), F32),
        ],
        sequence_mask, sent, *[shift_residues(sent, away, res_count) for away in away_range],
        alignment, cotangent, pair_bias, norm_gains, row_project, row_output,
        smem=1,
        scratch=[pltpu.VMEM((res_count, n_seq + 1, n_rows, C), F32)],
        name="row_forward",
    )
    arrived = swap_blocks(payload)
    (returned,) = call(
        functools.partial(column_step, n_seq=n_seq),
        [((seq_count, 3, block, 2 * C), F32)],
        arrived, norm_gains, column_project, column_output,
        scratch=[pltpu.VMEM((seq_count, group, 2 * C), F32), pltpu.VMEM((seq_count, group, C), F32)],
        name="column_step",
    )
    returned = swap_blocks(returned)
    part = -(-5 * C // (2 * ROWS * res_count)) * ROWS
    keys_each = n_keys // seq_count
    tiles = H * n_rows // LANES
    left = seq_count // 2 * tiles
    state, send, middle_grad, *sums = call(
        functools.partial(row_backward, res_count),
        [((left, keys_each, LANES), F32)] * 2
        + [((n_seq, n_rows, C), F32)]
        + [((part + ROWS + n_rows, LANES), F32)] * res_count,
        returned, exponent, unit, memory, query_gate, mixture, inverse, own_unit, row_project, row_output,
        scratch=[
            pltpu.VMEM((res_count, part + ROWS + n_rows, LANES), F32),
            pltpu.VMEM((n_keys, H * n_rows), F32),
        ],
        name="row_backward",
    )
    sums = sums[:1] + [shift_residues(sums[away], -away, res_count) for away in away_range]
    part_tiles = part // ROWS
    send, normed = call(
        add_shares,
        [((left + part_tiles + 1, ROWS, LANES), F32), ((n_rows, LANES), F32)],
        send, *sums,
        name="add_shares",
    )
    grad_alignment, done = call(
        finish_alignment,
        [(alignment.shape, alignment.dtype), ((ROWS, LANES), F32)],
        alignment, middle_grad, norm_gains, normed,
        name="finish_alignment",
    )
    steps = seq_count.bit_length() - 1
    for at in range(steps):
        arrived = cross(send, at, seq_count, res_count)
        if at < steps - 1:
            left //= 2
            state, send = call(
                functools.partial(step, part_tiles),
                [((left, ROWS, LANES), F32), ((left + part_tiles + (2 << at), ROWS, LANES), F32)],
                state, send, arrived,
                name="step",
            )
    shared, joined = call(
        last_step,
        [((part_tiles, ROWS, LANES), F32), ((seq_count, ROWS, LANES), F32)],
        send, arrived, done,
        unread=1,
        name="last_step",
    )
    (bias_grad,) = call(bias_last, [((H, keys_each, n_rows), F32)], state, arrived, name="bias_last")
    grads = call(
        functools.partial(unpack, res_count),
        [((2, C), F32), ((C, 4 * C), F32), ((C, C), F32), ((C, 2 * C + 2 * DH), F32), ((C, C), F32)],
        joined, shared, *[shift_residues(shared, away, res_count) for away in away_range],
        norm_gains, row_project, column_project,
        scratch=[
            pltpu.VMEM((res_count, part, LANES), F32),
            pltpu.VMEM((seq_count, 2, C // seq_count, LANES), F32),
        ],
        name="unpack",
    )
    return (grad_alignment, jnp.transpose(bias_grad, (0, 2, 1)), *grads)


def solution(mesh):
    placed = (
        P("seq", "res", None),
        P("seq", "res", None),
        P(None, "res", None),
        P(),
        P(),
        P(),
        P(),
        P(),
        P("res"),
        P("seq"),
    )
    return jax.shard_map(
        functools.partial(local, seq_count=mesh.shape["seq"], res_count=mesh.shape["res"]),
        mesh=mesh,
        in_specs=placed,
        out_specs=(P("seq", "res", None), P(None, "res", "seq"), P(), P(), P(), P(), P()),
        check_vma=False,
    )
```

```python
import functools

import jax
import jax.numpy as jnp
from jax import lax
from jax.experimental import pallas as pl
from jax.experimental.pallas import tpu as pltpu
from jax.sharding import PartitionSpec as P

C = 64
H = 8
DH = 8
LANES = 128
ROWS = 8

EXACT = lax.Precision.HIGHEST
THREE = lax.Precision.HIGH
EPSILON = 1e-05
MASKED = 1000000000.0
SCALE = DH ** (-0.5)
F32 = jnp.float32


def dot(a, b, over=((1,), (0,)), precision=THREE):
    return lax.dot_general(a, b, (over, ((), ())), precision=precision, preferred_element_type=F32)


def dot_rows(a, b):
    return dot(a, b, ((0,), (0,)))


def dot_t(a, b, precision=THREE):
    return dot(a, b, ((1,), (1,)), precision)


def to_column(row):
    eye = lax.broadcasted_iota(jnp.int32, (C, C), 0) == lax.broadcasted_iota(jnp.int32, (C, C), 1)
    return jnp.sum(jnp.where(eye, row, 0.0), axis=1, keepdims=True)


def to_row(column):
    eye = lax.broadcasted_iota(jnp.int32, (C, C), 0) == lax.broadcasted_iota(jnp.int32, (C, C), 1)
    return jnp.sum(jnp.where(eye, column, 0.0), axis=0, keepdims=True)


def normalise(values):
    centred = values - jnp.mean(values, axis=-1, keepdims=True)
    inverse = lax.rsqrt(jnp.mean(centred * centred, axis=-1, keepdims=True) + EPSILON)
    return centred * inverse, inverse


def normalise_back(grad_normed, gain, unit, inverse):
    grad_unit = grad_normed * gain
    along = jnp.mean(grad_unit * unit, axis=-1, keepdims=True)
    return inverse * (grad_unit - jnp.mean(grad_unit, axis=-1, keepdims=True) - unit * along)


def head_mask(rows):
    channel = lax.broadcasted_iota(jnp.int32, (C, H * rows), 0)
    lane = lax.broadcasted_iota(jnp.int32, (C, H * rows), 1)
    return (lane // rows == channel // DH).astype(F32)


def spread_heads(values, mask):
    rows = values.shape[0]
    turned = jnp.transpose(values)
    turned = jnp.concatenate([turned] * (LANES // rows), axis=1)
    return jnp.concatenate([turned] * (H * rows // LANES), axis=1) * mask


def join_heads(values, mask):
    masked = values * mask
    rows = mask.shape[1] // H
    total = masked[:, :LANES]
    for i in range(1, H * rows // LANES):
        total = total + masked[:, i * LANES : (i + 1) * LANES]
    joined = total[:, :rows]
    for i in range(1, LANES // rows):
        joined = joined + total[:, i * rows : (i + 1) * rows]
    return jnp.transpose(joined)


def row_forward(n_res, seq_mask, *refs):
    sent = refs[:n_res]
    own, cotangent, bias, gains, w_row, w_out = refs[n_res : n_res + 6]
    (payload, exponent_out, unit_out, own_unit_out, memory_out, query_gate_out, mixture_out, inverse_out,
     gathered) = refs[n_res + 6 :]
    n_seq, n_rows, _ = own.shape
    me = lax.axis_index("res")
    for away in range(n_res):
        gathered[lax.rem(me + away, n_res)] = sent[away][...]
    n_keys = n_res * n_rows
    n_blocks = payload.shape[0]
    block = n_rows // n_blocks
    gain = gains[0:1, :]
    w_all = w_row[...]
    w_query_gate = jnp.concatenate([w_all[:, :C], w_all[:, 3 * C :]], axis=1)
    key_bias = MASKED * (gathered[:, n_seq].reshape(n_keys, C)[:, 0:1] - 1.0)
    bias_t = jnp.transpose(bias[...].reshape(H * n_rows, n_keys).astype(F32))
    mask = head_mask(n_rows)
    wide_mask = jnp.concatenate([mask, mask], axis=0)
    units = jnp.concatenate([gathered[:, s].reshape(n_keys, C) for s in range(n_seq)], axis=0)
    units, _ = normalise(units)
    memories = dot(units * gain, w_all[:, C : 3 * C], precision=EXACT)
    initial = own[...].reshape(n_seq * n_rows, C).astype(F32)
    own_units, _ = normalise(initial)
    projected = dot(own_units * gain, w_query_gate, precision=EXACT)
    queries = projected[:, :C] * SCALE
    gates = jax.nn.sigmoid(projected[:, C:])
    unit_out[...] = units.reshape(n_seq, n_keys, C)
    memory_out[...] = memories.reshape(n_seq, n_keys, 2 * C)
    own_unit_out[...] = own_units.reshape(n_seq, n_rows, C)
    query_gate_out[...] = jnp.concatenate([queries, gates], axis=1).reshape(n_seq, n_rows, 2 * C)
    sums = []
    for s in range(n_seq):
        memory = memories[s * n_keys : (s + 1) * n_keys]
        query = queries[s * n_rows : (s + 1) * n_rows]
        scores = dot(memory[:, :C], spread_heads(query, mask), precision=EXACT) + bias_t + key_bias
        exponent = jnp.exp(scores - jnp.max(scores, axis=0, keepdims=True))
        exponent_out[s] = exponent
        summed = dot_rows(jnp.concatenate([memory[:, C:], jnp.ones((n_keys, C), F32)], axis=1), exponent)
        sums.append(join_heads(summed, wide_mask))
    summed = jnp.concatenate(sums, axis=0)
    inverse = 1.0 / summed[:, C:]
    mixture = summed[:, :C] * inverse
    inverse_out[...] = inverse.reshape(n_seq, n_rows, C)
    mixture_out[...] = mixture.reshape(n_seq, n_rows, C)
    middle = initial + dot(gates * mixture, w_out[...])
    both = jnp.concatenate([middle, cotangent[...].reshape(n_seq * n_rows, C).astype(F32)], axis=1)
    for s in range(n_seq):
        for b in range(n_blocks):
            row = s * n_rows + b * block
            payload[b, s] = both[row : row + block, :]
    lane = lax.broadcasted_iota(jnp.int32, (block, 2 * C), 1) // (2 * C // n_seq)
    present = jnp.zeros((block, 2 * C), F32)
    for s in range(n_seq):
        present = jnp.where(lane == s, seq_mask[s].astype(F32), present)
    for b in range(n_blocks):
        payload[b, n_seq] = present


def column_step(arrived, gains, w_col, w_out, returned, gathered, mask_rows, n_seq):
    n_src, _, block, _ = arrived.shape
    group = n_seq * block
    rows = n_src * group
    wide = 2 * C // n_seq
    share = C // n_src
    for src in range(n_src):
        for s in range(n_seq):
            gathered[src, s * block : (s + 1) * block, :] = arrived[src, s]
            mask_rows[src, s * block : (s + 1) * block, :] = jnp.broadcast_to(
                arrived[src, n_seq, :, s * wide : s * wide + 1], (block, C)
            )
    data = gathered[...].reshape(rows, 2 * C)
    present = mask_rows[...]
    middle = data[:, :C]
    cot = data[:, C:]
    gain = gains[1:2, :]

    def over_sequences(values, combine, reduce):
        total = reduce(values.reshape(n_src, group, C), axis=0)
        result = total
        for shift in range(1, n_seq):
            result = combine(result, pltpu.roll(total, shift * block, 0))
        return result

    def total_of(values):
        return over_sequences(values, jnp.add, jnp.sum)

    def spread(values):
        return jnp.broadcast_to(values[None], (n_src, group, C)).reshape(rows, C)

    lane = lax.broadcasted_iota(jnp.int32, (C, C), 1)
    row = lax.broadcasted_iota(jnp.int32, (C, C), 0)
    same_head = (row // DH == lane // DH).astype(F32)
    repeat = (lax.broadcasted_iota(jnp.int32, (DH, C), 0) == lax.broadcasted_iota(jnp.int32, (DH, C), 1) % DH).astype(F32)
    w_all = w_col[...]
    w_query = w_all[:, :C]
    w_key = dot(w_all[:, C : C + DH], repeat, precision=EXACT)
    w_value = dot(w_all[:, C + DH : C + 2 * DH], repeat)
    w_gate = w_all[:, C + 2 * DH :]
    w_rest = jnp.concatenate([w_key, w_value, w_gate], axis=1)

    unit, inverse = normalise(middle)
    normed = unit * gain
    present_rows = present.reshape(rows, C)
    counted = total_of(present_rows)
    mean_unit = total_of(present_rows * unit) / counted
    mean_normed = mean_unit * gain
    query = dot(mean_normed, w_query, precision=EXACT) * SCALE
    query_rows = spread(query)
    rest = dot(normed, w_rest, precision=EXACT)
    key, value = rest[:, :C], rest[:, C : 2 * C]
    gate = jax.nn.sigmoid(rest[:, 2 * C :])
    scores = dot(query_rows * key, same_head, precision=EXACT) + MASKED * (present_rows - 1.0)
    peak = over_sequences(scores, jnp.maximum, jnp.max)
    exponent = jnp.exp(scores - spread(peak))
    weights = exponent / spread(total_of(exponent))
    mixture = total_of(weights * value)
    mixture_rows = spread(mixture)

    grad_gated = dot_t(cot, w_out[...])
    out_grad = dot_rows(gate * mixture_rows, cot)
    grad_mixture = total_of(gate * grad_gated)
    grad_mixture_rows = spread(grad_mixture)
    grad_gate = grad_gated * mixture_rows * gate * (1.0 - gate)
    grad_weights = dot(grad_mixture_rows * value, same_head)
    inner = spread(dot(grad_mixture * mixture, same_head))
    grad_scores = weights * (grad_weights - inner)
    grad_rest = jnp.concatenate([grad_scores * query_rows, weights * grad_mixture_rows, grad_gate], axis=1)
    grad_query = total_of(grad_scores * key) * SCALE
    grad_mean = dot_t(grad_query, w_query)
    grad_normed = present_rows * spread(grad_mean / counted) + dot_t(grad_rest, w_rest)
    grad_query_weights = dot_rows(mean_unit, grad_query) * (1.0 / n_seq)
    grad_rest_weights = dot_rows(unit, grad_rest)
    fold_row = lax.broadcasted_iota(jnp.int32, (2 * C, 2 * DH), 0)
    fold_lane = lax.broadcasted_iota(jnp.int32, (2 * C, 2 * DH), 1)
    fold = ((fold_row // C == fold_lane // DH) & (fold_row % DH == fold_lane % DH)).astype(F32)
    grad_key_value = dot(grad_rest_weights[:, : 2 * C], fold)
    first = jnp.concatenate([grad_query_weights, grad_rest_weights[:, 2 * C :]], axis=1)
    second = jnp.concatenate([out_grad, grad_key_value, jnp.zeros((C, C - 2 * DH), F32)], axis=1)
    grad_middle = (cot + normalise_back(grad_normed, gain, unit, inverse)).reshape(n_src, group, C)
    for src in range(n_src):
        for s in range(n_seq):
            returned[src, 0, :, s * C : (s + 1) * C] = grad_middle[src, s * block : (s + 1) * block, :]
        returned[src, 1] = first[src * share : (src + 1) * share, :]
        returned[src, 2] = second[src * share : (src + 1) * share, :]


def row_backward(n_res, returned, exponent_in, unit_in, memory_in, query_gate_in, mixture_in, inverse_in, own_unit_in,
                 w_row, w_out, state, send, middle_grad, *refs):
    sums_out, shares, bias_t = refs[:n_res], refs[n_res], refs[n_res + 1]
    me = lax.axis_index("res")
    n_seq, n_rows, _ = middle_grad.shape
    n_keys = memory_in.shape[1]
    n_blocks, _, block, _ = returned.shape
    w_all = w_row[...]
    w_memory = w_all[:, C : 3 * C]
    w_query_gate = jnp.concatenate([w_all[:, :C], w_all[:, 3 * C :]], axis=1)
    mask = head_mask(n_rows)
    for b in range(n_blocks):
        for s in range(n_seq):
            middle_grad[s, b * block : (b + 1) * block, :] = returned[b, 0, :, s * C : (s + 1) * C]
    grad_middle = middle_grad[...].reshape(n_seq * n_rows, C)
    queries_gates = query_gate_in[...].reshape(n_seq * n_rows, 2 * C)
    gates = queries_gates[:, C:]
    mixtures = mixture_in[...].reshape(n_seq * n_rows, C)
    grad_gated = dot_t(grad_middle, w_out[...])
    grad_out = dot_rows(gates * mixtures, grad_middle)
    grad_gates = grad_gated * mixtures * gates * (1.0 - gates)
    grad_mixtures = grad_gated * gates * inverse_in[...].reshape(n_seq * n_rows, C)
    inners = grad_mixtures * mixtures
    bias_grad = jnp.zeros((n_keys, H * n_rows), F32)
    grad_queries = []
    grad_memories = []
    for s in range(n_seq):
        rows = slice(s * n_rows, (s + 1) * n_rows)
        memory = memory_in[s]
        exponent = exponent_in[s]
        grad_heads = spread_heads(grad_mixtures[rows], mask)
        query_heads = spread_heads(queries_gates[rows, :C], mask)
        right = jnp.concatenate([grad_heads, spread_heads(inners[rows], mask)], axis=0)
        left = jnp.concatenate([memory[:, C:], jnp.full((n_keys, C), -1.0, F32)], axis=1)
        grad_scores = exponent * dot(left, right)
        bias_grad = bias_grad + grad_scores
        grad_queries.append(join_heads(dot_rows(memory[:, :C], grad_scores), mask) * SCALE)
        grad_key = dot_t(grad_scores, query_heads)
        grad_value = dot_t(exponent, grad_heads)
        grad_memories.append(jnp.concatenate([grad_key, grad_value], axis=1))
    grad_query_gate = jnp.concatenate([jnp.concatenate(grad_queries, axis=0), grad_gates], axis=1)
    grad_memory = jnp.concatenate(grad_memories, axis=0)
    grad_query_gate_weights = dot_rows(own_unit_in[...].reshape(n_seq * n_rows, C), grad_query_gate)
    grad_memory_weights = dot_rows(unit_in[...].reshape(n_seq * n_keys, C), grad_memory)
    from_memory = dot_t(grad_memory, w_memory)
    from_own = dot_t(grad_query_gate, w_query_gate)
    from_memory = [from_memory[s * n_keys : (s + 1) * n_keys] for s in range(n_seq)]
    from_own = [from_own[s * n_rows : (s + 1) * n_rows] for s in range(n_seq)]
    bias_t[...] = bias_grad
    split_blocks(bias_t, state, send)

    half = C // 2
    weight_grads = jnp.concatenate(
        [grad_query_gate_weights, grad_memory_weights, jnp.concatenate([grad_out[:half], grad_out[half:]], axis=1)],
        axis=0,
    )
    part = shares.shape[1] - ROWS - n_rows
    shares[...] = jnp.zeros(shares.shape, F32)
    share = C // n_blocks
    column = jnp.sum(returned[:, 1:, :, :], axis=0)
    normed = jnp.concatenate(from_memory, axis=1)
    for i in range(n_res):
        rows = min(part, max(0, weight_grads.shape[0] - i * part))
        if rows:
            shares[i, :rows, :] = weight_grads[i * part : i * part + rows, :]
        shares[i, part : part + share, :] = column[0]
        shares[i, part + share : part + 2 * share, :] = column[1]
        shares[i, part + ROWS :, :] = normed[i * n_rows : (i + 1) * n_rows, :]
    for away in range(n_res):
        sums_out[away][...] = shares[lax.rem(me + away, n_res)]
    sums_out[0][part + ROWS :, :] += jnp.concatenate(from_own, axis=1)


def step_bits(n_seq_devices, odd):
    bits = list(range(n_seq_devices.bit_length() - 1))
    if odd:
        for i in range(0, len(bits) - 1, 2):
            bits[i], bits[i + 1] = bits[i + 1], bits[i]
    return bits


def relative_block(mask_of_bits, n_blocks):
    odd = lax.rem(lax.axis_index("res"), 2)
    even_mask = mask_of_bits(step_bits(n_blocks, False))
    odd_mask = mask_of_bits(step_bits(n_blocks, True))
    return lax.axis_index("seq") ^ (even_mask + odd * (odd_mask - even_mask))


def split_blocks(bias_t, state, send):
    tiles = bias_t.shape[1] // LANES
    n_blocks = (state.shape[0] + send.shape[0]) // tiles
    keys_each = bias_t.shape[0] // n_blocks
    half = n_blocks // 2

    for slot in range(n_blocks):

        def mask_of_bits(bits):
            last = len(bits) - 1
            return sum(1 << bit for at, bit in enumerate(bits) if slot >> (last - at) & 1)

        block = relative_block(mask_of_bits, n_blocks)
        values = bias_t[pl.ds(pl.multiple_of(block * keys_each, keys_each), keys_each), :]
        for i in range(tiles):
            out, at = (state, slot) if slot < half else (send, slot - half)
            out[at * tiles + i] = values[:, i * LANES : (i + 1) * LANES]


def bias_last(state, arrived, bias_out):
    heads, _, n_rows = bias_out.shape
    each = LANES // n_rows
    for i in range(state.shape[0]):
        total = state[i] + arrived[i]
        for e in range(each):
            bias_out[i * each + e] = total[:, e * n_rows : (e + 1) * n_rows]


def add_shares(bias_send, *refs):
    sums, send, normed = refs[:-2], refs[-2], refs[-1]
    total = sums[0][...]
    for more in sums[1:]:
        total = total + more[...]
    left = bias_send.shape[0]
    rows = total.shape[0] - normed.shape[0]
    send[:left] = bias_send[...]
    send[left:] = total[:rows].reshape(rows // ROWS, ROWS, LANES)
    normed[...] = total[rows:]


def step(part, state, sent, arrived, state_out, send):
    left = state.shape[0]
    half = left // 2
    total = state[...] + arrived[:left]
    state_out[...] = total[:half]
    send[:half] = total[half:]
    send[half : half + part] = sent[left : left + part] + arrived[left : left + part]
    pieces = sent.shape[0] - left - part
    send[half + part : half + part + pieces] = sent[left + part :]
    send[half + part + pieces :] = arrived[left + part :]


def last_step(sent, arrived, _, shared, joined):
    part = shared.shape[0]
    pieces = joined.shape[0] // 2
    left = sent.shape[0] - part - pieces
    shared[...] = sent[left : left + part] + arrived[left : left + part]
    joined[:pieces] = sent[left + part :]
    joined[pieces:] = arrived[left + part :]


def finish_alignment(own, middle_grad, gains, normed, out, done):
    n_seq = own.shape[0]
    done[...] = jnp.zeros(done.shape, F32)
    for s in range(n_seq):
        unit, inverse = normalise(own[s].astype(F32))
        grad_normed = normed[:, s * C : (s + 1) * C]
        out[s] = (middle_grad[s] + normalise_back(grad_normed, gains[0:1, :], unit, inverse)).astype(out.dtype)


def unpack(n_res, joined, *refs):
    parts = refs[:n_res]
    gains, w_row, w_col, gains_out, row_project_out, row_out_out, col_project_out, col_out_out = refs[n_res : n_res + 8]
    shares, column = refs[n_res + 8 :]
    me = lax.axis_index("res")
    part = shares.shape[1]
    for away in range(n_res):
        shares[lax.rem(me + away, n_res)] = parts[away][...].reshape(part, LANES)
    n_blocks, _, share, _ = column.shape
    for slot in range(n_blocks):
        block = relative_block(
            lambda bits: sum(1 << bit for at, bit in enumerate(bits) if slot >> at & 1), n_blocks
        )
        piece = joined[slot]
        column[block, 0] = piece[:share]
        column[block, 1] = piece[share : 2 * share]
    flat = jnp.concatenate([shares[i] for i in range(n_res)], axis=0)
    query_gate, memory, outs = flat[:C], flat[C : 2 * C], flat[2 * C : 2 * C + C // 2]
    col_query_gate = jnp.concatenate([column[i, 0] for i in range(n_blocks)], axis=0)
    col_rest = jnp.concatenate([column[i, 1] for i in range(n_blocks)], axis=0)
    rest = col_rest[:, C : C + 2 * DH]
    gain_row = to_column(gains[0:1, :])
    gain_col = to_column(gains[1:2, :])
    w_all = w_row[...]
    w_column = w_col[...]
    row_gain_grad = (
        jnp.sum(query_gate[:, :C] * w_all[:, :C], axis=1, keepdims=True)
        + jnp.sum(memory * w_all[:, C : 3 * C], axis=1, keepdims=True)
        + jnp.sum(query_gate[:, C:] * w_all[:, 3 * C :], axis=1, keepdims=True)
    )
    col_gain_grad = (
        jnp.sum(col_query_gate[:, :C] * w_column[:, :C], axis=1, keepdims=True)
        + jnp.sum(rest * w_column[:, C : C + 2 * DH], axis=1, keepdims=True)
        + jnp.sum(col_query_gate[:, C:] * w_column[:, C + 2 * DH :], axis=1, keepdims=True)
    )
    gains_out[0:1, :] = to_row(row_gain_grad)
    gains_out[1:2, :] = to_row(col_gain_grad)
    row_project_out[:, :C] = query_gate[:, :C] * gain_row
    row_project_out[:, C : 3 * C] = memory * gain_row
    row_project_out[:, 3 * C :] = query_gate[:, C:] * gain_row
    col_project_out[:, :C] = col_query_gate[:, :C] * gain_col
    col_project_out[:, C : C + 2 * DH] = rest * gain_col
    col_project_out[:, C + 2 * DH :] = col_query_gate[:, C:] * gain_col
    half = C // 2
    row_out_out[:half, :] = outs[:, :C]
    row_out_out[half:, :] = outs[:, C:]
    col_out_out[...] = col_rest[:, :C]


def call(body, outs, *operands, smem=0, unread=0, scratch=(), name):
    vmem = pl.BlockSpec(memory_space=pltpu.VMEM)
    scalar = pl.BlockSpec(memory_space=pltpu.SMEM)
    return pl.pallas_call(
        body,
        out_shape=[jax.ShapeDtypeStruct(shape, kind) for shape, kind in outs],
        in_specs=[scalar] * smem + [vmem] * (len(operands) - smem - unread)
        + [pl.BlockSpec(memory_space=pl.ANY)] * unread,
        out_specs=[vmem] * len(outs),
        scratch_shapes=list(scratch),
        compiler_params=pltpu.CompilerParams(vmem_limit_bytes=32 * 1024 * 1024),
        name=name,
    )(*operands)


def shift_residues(values, away, count):
    return lax.ppermute(values, "res", [((i + away) % count, i) for i in range(count)])


def cross(values, at, seq_count, res_count):
    pairs = []
    for r in range(res_count):
        bit = 1 << step_bits(seq_count, r % 2)[at]
        pairs += [(i * res_count + r, (i ^ bit) * res_count + r) for i in range(seq_count)]
    return lax.ppermute(values, ("seq", "res"), pairs)


def swap_blocks(values):
    return lax.all_to_all(values, "seq", 0, 0, tiled=True)


def local(
    alignment,
    cotangent,
    pair_bias,
    norm_gains,
    row_project,
    row_output,
    column_project,
    column_output,
    residue_mask,
    sequence_mask,
    seq_count,
    res_count,
):
    n_seq, n_rows, _ = alignment.shape
    n_keys = pair_bias.shape[2]
    block = n_rows // seq_count
    group = n_seq * block
    away_range = range(1, res_count)
    present_keys = jnp.broadcast_to(residue_mask.astype(F32)[None, :, None], (1, n_rows, C))
    sent = jnp.concatenate([alignment.astype(F32), present_keys], axis=0)
    payload, exponent, unit, own_unit, memory, query_gate, mixture, inverse = call(
        functools.partial(row_forward, res_count),
        [
            ((seq_count, n_seq + 1, block, 2 * C), F32),
            ((n_seq, n_keys, H * n_rows), F32),
            ((n_seq, n_keys, C), F32),
            ((n_seq, n_rows, C), F32),
            ((n_seq, n_keys, 2 * C), F32),
            ((n_seq, n_rows, 2 * C), F32),
            ((n_seq, n_rows, C), F32),
            ((n_seq, n_rows, C), F32),
        ],
        sequence_mask, sent, *[shift_residues(sent, away, res_count) for away in away_range],
        alignment, cotangent, pair_bias, norm_gains, row_project, row_output,
        smem=1,
        scratch=[
            pltpu.VMEM((res_count, n_seq + 1, n_rows, C), F32),
        ],
        name="row_forward",
    )
    arrived = swap_blocks(payload)
    (returned,) = call(
        functools.partial(column_step, n_seq=n_seq),
        [((seq_count, 3, block, 2 * C), F32)],
        arrived, norm_gains, column_project, column_output,
        scratch=[pltpu.VMEM((seq_count, group, 2 * C), F32), pltpu.VMEM((seq_count, group, C), F32)],
        name="column_step",
    )
    returned = swap_blocks(returned)
    part = -(-5 * C // (2 * ROWS * res_count)) * ROWS
    keys_each = n_keys // seq_count
    tiles = H * n_rows // LANES
    left = seq_count // 2 * tiles
    state, send, middle_grad, *sums = call(
        functools.partial(row_backward, res_count),
        [((left, keys_each, LANES), F32)] * 2
        + [((n_seq, n_rows, C), F32)]
        + [((part + ROWS + n_rows, LANES), F32)] * res_count,
        returned, exponent, unit, memory, query_gate, mixture, inverse, own_unit, row_project, row_output,
        scratch=[
            pltpu.VMEM((res_count, part + ROWS + n_rows, LANES), F32),
            pltpu.VMEM((n_keys, H * n_rows), F32),
        ],
        name="row_backward",
    )
    sums = sums[:1] + [shift_residues(sums[away], -away, res_count) for away in away_range]
    part_tiles = part // ROWS
    send, normed = call(
        add_shares,
        [((left + part_tiles + 1, ROWS, LANES), F32), ((n_rows, LANES), F32)],
        send, *sums,
        name="add_shares",
    )
    grad_alignment, done = call(
        finish_alignment,
        [(alignment.shape, alignment.dtype), ((ROWS, LANES), F32)],
        alignment, middle_grad, norm_gains, normed,
        name="finish_alignment",
    )
    steps = seq_count.bit_length() - 1
    for at in range(steps):
        arrived = cross(send, at, seq_count, res_count)
        if at < steps - 1:
            left //= 2
            state, send = call(
                functools.partial(step, part_tiles),
                [((left, ROWS, LANES), F32), ((left + part_tiles + (2 << at), ROWS, LANES), F32)],
                state, send, arrived,
                name="step",
            )
    shared, joined = call(
        last_step,
        [((part_tiles, ROWS, LANES), F32), ((seq_count, ROWS, LANES), F32)],
        send, arrived, done,
        unread=1,
        name="last_step",
    )
    (bias_grad,) = call(bias_last, [((H, keys_each, n_rows), F32)], state, arrived, name="bias_last")
    grads = call(
        functools.partial(unpack, res_count),
        [((2, C), F32), ((C, 4 * C), F32), ((C, C), F32), ((C, 2 * C + 2 * DH), F32), ((C, C), F32)],
        joined, shared, *[shift_residues(shared, away, res_count) for away in away_range],
        norm_gains, row_project, column_project,
        scratch=[
            pltpu.VMEM((res_count, part, LANES), F32),
            pltpu.VMEM((seq_count, 2, C // seq_count, LANES), F32),
        ],
        name="unpack",
    )
    return (grad_alignment, jnp.transpose(bias_grad, (0, 2, 1)), *grads)


def solution(mesh):
    placed = (
        P("seq", "res", None),
        P("seq", "res", None),
        P(None, "res", None),
        P(),
        P(),
        P(),
        P(),
        P(),
        P("res"),
        P("seq"),
    )
    return jax.shard_map(
        functools.partial(local, seq_count=mesh.shape["seq"], res_count=mesh.shape["res"]),
        mesh=mesh,
        in_specs=placed,
        out_specs=(P("seq", "res", None), P(None, "res", "seq"), P(), P(), P(), P(), P()),
        check_vma=False,
    )
```

```python
import functools

import jax
import jax.numpy as jnp
from jax import lax
from jax.experimental import pallas as pl
from jax.experimental.pallas import tpu as pltpu
from jax.sharding import PartitionSpec as P

C = 64
H = 8
DH = 8
LANES = 128
ROWS = 8

EXACT = lax.Precision.HIGHEST
THREE = lax.Precision.HIGH
EPSILON = 1e-05
MASKED = 1000000000.0
SCALE = DH ** (-0.5)
F32 = jnp.float32


def dot(a, b, over=((1,), (0,)), precision=THREE):
    return lax.dot_general(a, b, (over, ((), ())), precision=precision, preferred_element_type=F32)


def dot_rows(a, b):
    return dot(a, b, ((0,), (0,)))


def dot_t(a, b, precision=THREE):
    return dot(a, b, ((1,), (1,)), precision)


def to_column(row):
    eye = lax.broadcasted_iota(jnp.int32, (C, C), 0) == lax.broadcasted_iota(jnp.int32, (C, C), 1)
    return jnp.sum(jnp.where(eye, row, 0.0), axis=1, keepdims=True)


def to_row(column):
    eye = lax.broadcasted_iota(jnp.int32, (C, C), 0) == lax.broadcasted_iota(jnp.int32, (C, C), 1)
    return jnp.sum(jnp.where(eye, column, 0.0), axis=0, keepdims=True)


def normalise(values):
    centred = values - jnp.mean(values, axis=-1, keepdims=True)
    inverse = lax.rsqrt(jnp.mean(centred * centred, axis=-1, keepdims=True) + EPSILON)
    return centred * inverse, inverse


def normalise_back(grad_normed, gain, unit, inverse):
    grad_unit = grad_normed * gain
    along = jnp.mean(grad_unit * unit, axis=-1, keepdims=True)
    return inverse * (grad_unit - jnp.mean(grad_unit, axis=-1, keepdims=True) - unit * along)


def head_mask(rows):
    channel = lax.broadcasted_iota(jnp.int32, (C, H * rows), 0)
    lane = lax.broadcasted_iota(jnp.int32, (C, H * rows), 1)
    return (lane // rows == channel // DH).astype(F32)


def spread_heads(values, mask):
    rows = values.shape[0]
    turned = jnp.transpose(values)
    turned = jnp.concatenate([turned] * (LANES // rows), axis=1)
    return jnp.concatenate([turned] * (H * rows // LANES), axis=1) * mask


def join_heads(values, mask):
    masked = values * mask
    rows = mask.shape[1] // H
    total = masked[:, :LANES]
    for i in range(1, H * rows // LANES):
        total = total + masked[:, i * LANES : (i + 1) * LANES]
    joined = total[:, :rows]
    for i in range(1, LANES // rows):
        joined = joined + total[:, i * rows : (i + 1) * rows]
    return jnp.transpose(joined)


def own_half(seq_mask, own, bias, gains, w_row,
             own_unit_out, query_gate_out, query_heads_out, own_memory_out, bias_out, present_out):
    n_seq, n_rows, _ = own.shape
    n_keys = bias.shape[2]
    w_all = w_row[...]
    own_units, _ = normalise(own[...].reshape(n_seq * n_rows, C).astype(F32))
    projected = dot(own_units * gains[0:1, :], w_all, precision=EXACT)
    queries = projected[:, :C] * SCALE
    gates = jax.nn.sigmoid(projected[:, 3 * C :])
    own_unit_out[...] = own_units.reshape(n_seq, n_rows, C)
    query_gate_out[...] = jnp.concatenate([queries, gates], axis=1).reshape(n_seq, n_rows, 2 * C)
    own_memory_out[...] = projected[:, C : 3 * C].reshape(n_seq, n_rows, 2 * C)
    mask = head_mask(n_rows)
    for s in range(n_seq):
        query_heads_out[s] = spread_heads(queries[s * n_rows : (s + 1) * n_rows], mask)
    bias_out[...] = jnp.transpose(bias[...].reshape(H * n_rows, n_keys).astype(F32))
    lane = lax.broadcasted_iota(jnp.int32, present_out.shape, 1) // (2 * C // n_seq)
    present = jnp.zeros(present_out.shape, F32)
    for s in range(n_seq):
        present = jnp.where(lane == s, seq_mask[s].astype(F32), present)
    present_out[...] = present


def row_forward(n_res, *refs):
    sent = refs[:n_res]
    (own, cotangent, gains, w_row, w_out, own_unit, query_gate, query_heads, own_memory, bias_t, present) = refs[
        n_res : n_res + 11
    ]
    payload, exponent_out, unit_out, memory_out, mixture_out, inverse_out, residue = refs[n_res + 11 :]
    n_seq, n_rows, _ = own.shape
    n_keys = n_res * n_rows
    me = lax.axis_index("res")
    w_memory = w_row[:, C : 3 * C]
    for away in range(n_res):
        where = lax.rem(me + away, n_res)
        residue[where] = sent[away][n_seq]
        if away:
            units, _ = normalise(sent[away][:n_seq].reshape(n_seq * n_rows, C))
            memories = dot(units * gains[0:1, :], w_memory, precision=EXACT)
            units = units.reshape(n_seq, n_rows, C)
            memories = memories.reshape(n_seq, n_rows, 2 * C)
        else:
            units, memories = own_unit[...], own_memory[...]
        unit_out[where] = units
        memory_out[where] = memories
    n_blocks = payload.shape[0]
    block = n_rows // n_blocks
    key_bias = MASKED * (residue[...].reshape(n_keys, C)[:, 0:1] - 1.0)
    mask = head_mask(n_rows)
    wide_mask = jnp.concatenate([mask, mask], axis=0)
    initial = own[...].reshape(n_seq * n_rows, C).astype(F32)
    gates = query_gate[...].reshape(n_seq * n_rows, 2 * C)[:, C:]
    sums = []
    for s in range(n_seq):
        memory = memory_out[:, s].reshape(n_keys, 2 * C)
        scores = dot(memory[:, :C], query_heads[s], precision=EXACT) + bias_t[...] + key_bias
        exponent = jnp.exp(scores - jnp.max(scores, axis=0, keepdims=True))
        exponent_out[s] = exponent
        summed = dot_rows(jnp.concatenate([memory[:, C:], jnp.ones((n_keys, C), F32)], axis=1), exponent)
        sums.append(join_heads(summed, wide_mask))
    summed = jnp.concatenate(sums, axis=0)
    inverse = 1.0 / summed[:, C:]
    mixture = summed[:, :C] * inverse
    inverse_out[...] = inverse.reshape(n_seq, n_rows, C)
    mixture_out[...] = mixture.reshape(n_seq, n_rows, C)
    middle = initial + dot(gates * mixture, w_out[...])
    both = jnp.concatenate([middle, cotangent[...].reshape(n_seq * n_rows, C).astype(F32)], axis=1)
    for s in range(n_seq):
        for b in range(n_blocks):
            row = s * n_rows + b * block
            payload[b, s] = both[row : row + block, :]
    for b in range(n_blocks):
        payload[b, n_seq] = present[...]


def column_step(arrived, gains, w_col, w_out, returned, gathered, mask_rows, n_seq):
    n_src, _, block, _ = arrived.shape
    group = n_seq * block
    rows = n_src * group
    wide = 2 * C // n_seq
    share = C // n_src
    for src in range(n_src):
        for s in range(n_seq):
            gathered[src, s * block : (s + 1) * block, :] = arrived[src, s]
            mask_rows[src, s * block : (s + 1) * block, :] = jnp.broadcast_to(
                arrived[src, n_seq, :, s * wide : s * wide + 1], (block, C)
            )
    data = gathered[...].reshape(rows, 2 * C)
    present = mask_rows[...]
    middle = data[:, :C]
    cot = data[:, C:]
    gain = gains[1:2, :]

    def over_sequences(values, combine, reduce):
        total = reduce(values.reshape(n_src, group, C), axis=0)
        result = total
        for shift in range(1, n_seq):
            result = combine(result, pltpu.roll(total, shift * block, 0))
        return result

    def total_of(values):
        return over_sequences(values, jnp.add, jnp.sum)

    def spread(values):
        return jnp.broadcast_to(values[None], (n_src, group, C)).reshape(rows, C)

    lane = lax.broadcasted_iota(jnp.int32, (C, C), 1)
    row = lax.broadcasted_iota(jnp.int32, (C, C), 0)
    same_head = (row // DH == lane // DH).astype(F32)
    repeat = (lax.broadcasted_iota(jnp.int32, (DH, C), 0) == lax.broadcasted_iota(jnp.int32, (DH, C), 1) % DH).astype(F32)
    w_all = w_col[...]
    w_query = w_all[:, :C]
    w_key = dot(w_all[:, C : C + DH], repeat, precision=EXACT)
    w_value = dot(w_all[:, C + DH : C + 2 * DH], repeat)
    w_gate = w_all[:, C + 2 * DH :]
    w_rest = jnp.concatenate([w_key, w_value, w_gate], axis=1)

    unit, inverse = normalise(middle)
    normed = unit * gain
    present_rows = present.reshape(rows, C)
    counted = total_of(present_rows)
    mean_unit = total_of(present_rows * unit) / counted
    mean_normed = mean_unit * gain
    query = dot(mean_normed, w_query, precision=EXACT) * SCALE
    query_rows = spread(query)
    rest = dot(normed, w_rest, precision=EXACT)
    key, value = rest[:, :C], rest[:, C : 2 * C]
    gate = jax.nn.sigmoid(rest[:, 2 * C :])
    scores = dot(query_rows * key, same_head, precision=EXACT) + MASKED * (present_rows - 1.0)
    peak = over_sequences(scores, jnp.maximum, jnp.max)
    exponent = jnp.exp(scores - spread(peak))
    weights = exponent / spread(total_of(exponent))
    mixture = total_of(weights * value)
    mixture_rows = spread(mixture)

    grad_gated = dot_t(cot, w_out[...])
    out_grad = dot_rows(gate * mixture_rows, cot)
    grad_mixture = total_of(gate * grad_gated)
    grad_mixture_rows = spread(grad_mixture)
    grad_gate = grad_gated * mixture_rows * gate * (1.0 - gate)
    grad_weights = dot(grad_mixture_rows * value, same_head)
    inner = spread(dot(grad_mixture * mixture, same_head))
    grad_scores = weights * (grad_weights - inner)
    grad_rest = jnp.concatenate([grad_scores * query_rows, weights * grad_mixture_rows, grad_gate], axis=1)
    grad_query = total_of(grad_scores * key) * SCALE
    grad_mean = dot_t(grad_query, w_query)
    grad_normed = present_rows * spread(grad_mean / counted) + dot_t(grad_rest, w_rest)
    grad_query_weights = dot_rows(mean_unit, grad_query) * (1.0 / n_seq)
    grad_rest_weights = dot_rows(unit, grad_rest)
    fold_row = lax.broadcasted_iota(jnp.int32, (2 * C, 2 * DH), 0)
    fold_lane = lax.broadcasted_iota(jnp.int32, (2 * C, 2 * DH), 1)
    fold = ((fold_row // C == fold_lane // DH) & (fold_row % DH == fold_lane % DH)).astype(F32)
    grad_key_value = dot(grad_rest_weights[:, : 2 * C], fold)
    first = jnp.concatenate([grad_query_weights, grad_rest_weights[:, 2 * C :]], axis=1)
    second = jnp.concatenate([out_grad, grad_key_value, jnp.zeros((C, C - 2 * DH), F32)], axis=1)
    grad_middle = (cot + normalise_back(grad_normed, gain, unit, inverse)).reshape(n_src, group, C)
    for src in range(n_src):
        for s in range(n_seq):
            returned[src, 0, :, s * C : (s + 1) * C] = grad_middle[src, s * block : (s + 1) * block, :]
        returned[src, 1] = first[src * share : (src + 1) * share, :]
        returned[src, 2] = second[src * share : (src + 1) * share, :]


def row_backward(n_res, returned, exponent_in, unit_in, memory_in, query_gate_in, query_heads_in, mixture_in, inverse_in,
                 own_unit_in, w_row, w_out, bias_out, middle_grad, *refs):
    sums_out, shares = refs[:n_res], refs[n_res]
    me = lax.axis_index("res")
    n_seq, n_rows, _ = middle_grad.shape
    n_keys = n_res * n_rows
    n_blocks, _, block, _ = returned.shape
    w_all = w_row[...]
    w_memory = w_all[:, C : 3 * C]
    w_query_gate = jnp.concatenate([w_all[:, :C], w_all[:, 3 * C :]], axis=1)
    mask = head_mask(n_rows)
    for b in range(n_blocks):
        for s in range(n_seq):
            middle_grad[s, b * block : (b + 1) * block, :] = returned[b, 0, :, s * C : (s + 1) * C]
    grad_middle = middle_grad[...].reshape(n_seq * n_rows, C)
    queries_gates = query_gate_in[...].reshape(n_seq * n_rows, 2 * C)
    gates = queries_gates[:, C:]
    mixtures = mixture_in[...].reshape(n_seq * n_rows, C)
    grad_gated = dot_t(grad_middle, w_out[...])
    grad_out = dot_rows(gates * mixtures, grad_middle)
    grad_gates = grad_gated * mixtures * gates * (1.0 - gates)
    grad_mixtures = grad_gated * gates * inverse_in[...].reshape(n_seq * n_rows, C)
    inners = grad_mixtures * mixtures
    bias_grad = jnp.zeros((n_keys, H * n_rows), F32)
    grad_queries = []
    grad_memories = []
    for s in range(n_seq):
        rows = slice(s * n_rows, (s + 1) * n_rows)
        memory = memory_in[:, s].reshape(n_keys, 2 * C)
        exponent = exponent_in[s]
        grad_heads = spread_heads(grad_mixtures[rows], mask)
        right = jnp.concatenate([grad_heads, spread_heads(inners[rows], mask)], axis=0)
        left = jnp.concatenate([memory[:, C:], jnp.full((n_keys, C), -1.0, F32)], axis=1)
        grad_scores = exponent * dot(left, right)
        bias_grad = bias_grad + grad_scores
        grad_queries.append(join_heads(dot_rows(memory[:, :C], grad_scores), mask) * SCALE)
        grad_key = dot_t(grad_scores, query_heads_in[s])
        grad_value = dot_t(exponent, grad_heads)
        grad_memories.append(jnp.concatenate([grad_key, grad_value], axis=1))
    grad_query_gate = jnp.concatenate([jnp.concatenate(grad_queries, axis=0), grad_gates], axis=1)
    grad_memory = jnp.concatenate(grad_memories, axis=0)
    grad_query_gate_weights = dot_rows(own_unit_in[...].reshape(n_seq * n_rows, C), grad_query_gate)
    units = jnp.concatenate([unit_in[:, s].reshape(n_keys, C) for s in range(n_seq)], axis=0)
    grad_memory_weights = dot_rows(units, grad_memory)
    from_memory = dot_t(grad_memory, w_memory)
    from_own = dot_t(grad_query_gate, w_query_gate)
    from_memory = [from_memory[s * n_keys : (s + 1) * n_keys] for s in range(n_seq)]
    from_own = [from_own[s * n_rows : (s + 1) * n_rows] for s in range(n_seq)]
    bias_out[...] = bias_grad
    half = C // 2
    weight_grads = jnp.concatenate(
        [grad_query_gate_weights, grad_memory_weights, jnp.concatenate([grad_out[:half], grad_out[half:]], axis=1)],
        axis=0,
    )
    part = shares.shape[1] - ROWS - n_rows
    shares[...] = jnp.zeros(shares.shape, F32)
    share = C // n_blocks
    column = jnp.sum(returned[:, 1:, :, :], axis=0)
    normed = jnp.concatenate(from_memory, axis=1)
    for i in range(n_res):
        rows = min(part, max(0, weight_grads.shape[0] - i * part))
        if rows:
            shares[i, :rows, :] = weight_grads[i * part : i * part + rows, :]
        shares[i, part : part + share, :] = column[0]
        shares[i, part + share : part + 2 * share, :] = column[1]
        shares[i, part + ROWS :, :] = normed[i * n_rows : (i + 1) * n_rows, :]
    for away in range(n_res):
        sums_out[away][...] = shares[lax.rem(me + away, n_res)]
    sums_out[0][part + ROWS :, :] += jnp.concatenate(from_own, axis=1)


def step_bits(n_seq_devices, odd):
    bits = list(range(n_seq_devices.bit_length() - 1))
    if odd:
        for i in range(0, len(bits) - 1, 2):
            bits[i], bits[i + 1] = bits[i + 1], bits[i]
    return bits


def relative_block(mask_of_bits, n_blocks):
    odd = lax.rem(lax.axis_index("res"), 2)
    even_mask = mask_of_bits(step_bits(n_blocks, False))
    odd_mask = mask_of_bits(step_bits(n_blocks, True))
    return lax.axis_index("seq") ^ (even_mask + odd * (odd_mask - even_mask))


def split_blocks(bias_t, state, send):
    tiles = bias_t.shape[1] // LANES
    n_blocks = (state.shape[0] + send.shape[0]) // tiles
    keys_each = bias_t.shape[0] // n_blocks
    half = n_blocks // 2

    for slot in range(n_blocks):

        def mask_of_bits(bits):
            last = len(bits) - 1
            return sum(1 << bit for at, bit in enumerate(bits) if slot >> (last - at) & 1)

        block = relative_block(mask_of_bits, n_blocks)
        values = bias_t[pl.ds(pl.multiple_of(block * keys_each, keys_each), keys_each), :]
        for i in range(tiles):
            out, at = (state, slot) if slot < half else (send, slot - half)
            out[at * tiles + i] = values[:, i * LANES : (i + 1) * LANES]


def bias_last(state, arrived, bias_out):
    heads, _, n_rows = bias_out.shape
    each = LANES // n_rows
    for i in range(state.shape[0]):
        total = state[i] + arrived[i]
        for e in range(each):
            bias_out[i * each + e] = total[:, e * n_rows : (e + 1) * n_rows]


def add_shares(bias_send, *refs):
    sums, send, normed = refs[:-2], refs[-2], refs[-1]
    total = sums[0][...]
    for more in sums[1:]:
        total = total + more[...]
    left = bias_send.shape[0]
    rows = total.shape[0] - normed.shape[0]
    send[:left] = bias_send[...]
    send[left:] = total[:rows].reshape(rows // ROWS, ROWS, LANES)
    normed[...] = total[rows:]


def step(part, state, sent, arrived, state_out, send):
    left = state.shape[0]
    half = left // 2
    total = state[...] + arrived[:left]
    state_out[...] = total[:half]
    send[:half] = total[half:]
    send[half : half + part] = sent[left : left + part] + arrived[left : left + part]
    pieces = sent.shape[0] - left - part
    send[half + part : half + part + pieces] = sent[left + part :]
    send[half + part + pieces :] = arrived[left + part :]


def last_step(sent, arrived, _, shared, joined):
    part = shared.shape[0]
    pieces = joined.shape[0] // 2
    left = sent.shape[0] - part - pieces
    shared[...] = sent[left : left + part] + arrived[left : left + part]
    joined[:pieces] = sent[left + part :]
    joined[pieces:] = arrived[left + part :]


def finish_alignment(own, middle_grad, gains, normed, out, done):
    n_seq = own.shape[0]
    done[...] = jnp.zeros(done.shape, F32)
    for s in range(n_seq):
        unit, inverse = normalise(own[s].astype(F32))
        grad_normed = normed[:, s * C : (s + 1) * C]
        out[s] = (middle_grad[s] + normalise_back(grad_normed, gains[0:1, :], unit, inverse)).astype(out.dtype)


def unpack(n_res, joined, *refs):
    parts = refs[:n_res]
    gains, w_row, w_col, gains_out, row_project_out, row_out_out, col_project_out, col_out_out = refs[n_res : n_res + 8]
    shares, column = refs[n_res + 8 :]
    me = lax.axis_index("res")
    part = shares.shape[1]
    for away in range(n_res):
        shares[lax.rem(me + away, n_res)] = parts[away][...].reshape(part, LANES)
    n_blocks, _, share, _ = column.shape
    for slot in range(n_blocks):
        block = relative_block(
            lambda bits: sum(1 << bit for at, bit in enumerate(bits) if slot >> at & 1), n_blocks
        )
        piece = joined[slot]
        column[block, 0] = piece[:share]
        column[block, 1] = piece[share : 2 * share]
    flat = jnp.concatenate([shares[i] for i in range(n_res)], axis=0)
    query_gate, memory, outs = flat[:C], flat[C : 2 * C], flat[2 * C : 2 * C + C // 2]
    col_query_gate = jnp.concatenate([column[i, 0] for i in range(n_blocks)], axis=0)
    col_rest = jnp.concatenate([column[i, 1] for i in range(n_blocks)], axis=0)
    rest = col_rest[:, C : C + 2 * DH]
    gain_row = to_column(gains[0:1, :])
    gain_col = to_column(gains[1:2, :])
    w_all = w_row[...]
    w_column = w_col[...]
    row_gain_grad = (
        jnp.sum(query_gate[:, :C] * w_all[:, :C], axis=1, keepdims=True)
        + jnp.sum(memory * w_all[:, C : 3 * C], axis=1, keepdims=True)
        + jnp.sum(query_gate[:, C:] * w_all[:, 3 * C :], axis=1, keepdims=True)
    )
    col_gain_grad = (
        jnp.sum(col_query_gate[:, :C] * w_column[:, :C], axis=1, keepdims=True)
        + jnp.sum(rest * w_column[:, C : C + 2 * DH], axis=1, keepdims=True)
        + jnp.sum(col_query_gate[:, C:] * w_column[:, C + 2 * DH :], axis=1, keepdims=True)
    )
    gains_out[0:1, :] = to_row(row_gain_grad)
    gains_out[1:2, :] = to_row(col_gain_grad)
    row_project_out[:, :C] = query_gate[:, :C] * gain_row
    row_project_out[:, C : 3 * C] = memory * gain_row
    row_project_out[:, 3 * C :] = query_gate[:, C:] * gain_row
    col_project_out[:, :C] = col_query_gate[:, :C] * gain_col
    col_project_out[:, C : C + 2 * DH] = rest * gain_col
    col_project_out[:, C + 2 * DH :] = col_query_gate[:, C:] * gain_col
    half = C // 2
    row_out_out[:half, :] = outs[:, :C]
    row_out_out[half:, :] = outs[:, C:]
    col_out_out[...] = col_rest[:, :C]


def call(body, outs, *operands, smem=0, unread=0, scratch=(), name):
    vmem = pl.BlockSpec(memory_space=pltpu.VMEM)
    scalar = pl.BlockSpec(memory_space=pltpu.SMEM)
    return pl.pallas_call(
        body,
        out_shape=[jax.ShapeDtypeStruct(shape, kind) for shape, kind in outs],
        in_specs=[scalar] * smem + [vmem] * (len(operands) - smem - unread)
        + [pl.BlockSpec(memory_space=pl.ANY)] * unread,
        out_specs=[vmem] * len(outs),
        scratch_shapes=list(scratch),
        compiler_params=pltpu.CompilerParams(vmem_limit_bytes=32 * 1024 * 1024),
        name=name,
    )(*operands)


def shift_residues(values, away, count):
    return lax.ppermute(values, "res", [((i + away) % count, i) for i in range(count)])


def cross(values, at, seq_count, res_count):
    pairs = []
    for r in range(res_count):
        bit = 1 << step_bits(seq_count, r % 2)[at]
        pairs += [(i * res_count + r, (i ^ bit) * res_count + r) for i in range(seq_count)]
    return lax.ppermute(values, ("seq", "res"), pairs)


def swap_blocks(values):
    return lax.all_to_all(values, "seq", 0, 0, tiled=True)


def local(
    alignment,
    cotangent,
    pair_bias,
    norm_gains,
    row_project,
    row_output,
    column_project,
    column_output,
    residue_mask,
    sequence_mask,
    seq_count,
    res_count,
):
    n_seq, n_rows, _ = alignment.shape
    n_keys = pair_bias.shape[2]
    block = n_rows // seq_count
    group = n_seq * block
    away_range = range(1, res_count)
    present_keys = jnp.broadcast_to(residue_mask.astype(F32)[None, :, None], (1, n_rows, C))
    sent = jnp.concatenate([alignment.astype(F32), present_keys], axis=0)
    own_unit, query_gate, query_heads, own_memory, bias_t, present = call(
        own_half,
        [
            ((n_seq, n_rows, C), F32),
            ((n_seq, n_rows, 2 * C), F32),
            ((n_seq, C, H * n_rows), F32),
            ((n_seq, n_rows, 2 * C), F32),
            ((n_keys, H * n_rows), F32),
            ((block, 2 * C), F32),
        ],
        sequence_mask, alignment, pair_bias, norm_gains, row_project,
        smem=1,
        name="own_half",
    )
    payload, exponent, unit, memory, mixture, inverse = call(
        functools.partial(row_forward, res_count),
        [
            ((seq_count, n_seq + 1, block, 2 * C), F32),
            ((n_seq, n_keys, H * n_rows), F32),
            ((res_count, n_seq, n_rows, C), F32),
            ((res_count, n_seq, n_rows, 2 * C), F32),
            ((n_seq, n_rows, C), F32),
            ((n_seq, n_rows, C), F32),
        ],
        sent, *[shift_residues(sent, away, res_count) for away in away_range],
        alignment, cotangent, norm_gains, row_project, row_output, own_unit, query_gate, query_heads, own_memory, bias_t,
        present,
        scratch=[pltpu.VMEM((res_count, n_rows, C), F32)],
        name="row_forward",
    )
    arrived = swap_blocks(payload)
    (returned,) = call(
        functools.partial(column_step, n_seq=n_seq),
        [((seq_count, 3, block, 2 * C), F32)],
        arrived, norm_gains, column_project, column_output,
        scratch=[pltpu.VMEM((seq_count, group, 2 * C), F32), pltpu.VMEM((seq_count, group, C), F32)],
        name="column_step",
    )
    returned = swap_blocks(returned)
    part = -(-5 * C // (2 * ROWS * res_count)) * ROWS
    keys_each = n_keys // seq_count
    tiles = H * n_rows // LANES
    left = seq_count // 2 * tiles
    bias_grad, middle_grad, *sums = call(
        functools.partial(row_backward, res_count),
        [((n_keys, H * n_rows), F32), ((n_seq, n_rows, C), F32)]
        + [((part + ROWS + n_rows, LANES), F32)] * res_count,
        returned, exponent, unit, memory, query_gate, query_heads, mixture, inverse, own_unit, row_project, row_output,
        scratch=[pltpu.VMEM((res_count, part + ROWS + n_rows, LANES), F32)],
        name="row_backward",
    )
    sums = sums[:1] + [shift_residues(sums[away], -away, res_count) for away in away_range]
    state, send = call(
        split_blocks, [((left, keys_each, LANES), F32)] * 2, bias_grad, name="split_blocks"
    )
    part_tiles = part // ROWS
    send, normed = call(
        add_shares,
        [((left + part_tiles + 1, ROWS, LANES), F32), ((n_rows, LANES), F32)],
        send, *sums,
        name="add_shares",
    )
    grad_alignment, done = call(
        finish_alignment,
        [(alignment.shape, alignment.dtype), ((ROWS, LANES), F32)],
        alignment, middle_grad, norm_gains, normed,
        name="finish_alignment",
    )
    steps = seq_count.bit_length() - 1
    for at in range(steps):
        arrived = cross(send, at, seq_count, res_count)
        if at < steps - 1:
            left //= 2
            state, send = call(
                functools.partial(step, part_tiles),
                [((left, ROWS, LANES), F32), ((left + part_tiles + (2 << at), ROWS, LANES), F32)],
                state, send, arrived,
                name="step",
            )
    shared, joined = call(
        last_step,
        [((part_tiles, ROWS, LANES), F32), ((seq_count, ROWS, LANES), F32)],
        send, arrived, done,
        unread=1,
        name="last_step",
    )
    (bias_grad,) = call(bias_last, [((H, keys_each, n_rows), F32)], state, arrived, name="bias_last")
    grads = call(
        functools.partial(unpack, res_count),
        [((2, C), F32), ((C, 4 * C), F32), ((C, C), F32), ((C, 2 * C + 2 * DH), F32), ((C, C), F32)],
        joined, shared, *[shift_residues(shared, away, res_count) for away in away_range],
        norm_gains, row_project, column_project,
        scratch=[
            pltpu.VMEM((res_count, part, LANES), F32),
            pltpu.VMEM((seq_count, 2, C // seq_count, LANES), F32),
        ],
        name="unpack",
    )
    return (grad_alignment, jnp.transpose(bias_grad, (0, 2, 1)), *grads)


def solution(mesh):
    placed = (
        P("seq", "res", None),
        P("seq", "res", None),
        P(None, "res", None),
        P(),
        P(),
        P(),
        P(),
        P(),
        P("res"),
        P("seq"),
    )
    return jax.shard_map(
        functools.partial(local, seq_count=mesh.shape["seq"], res_count=mesh.shape["res"]),
        mesh=mesh,
        in_specs=placed,
        out_specs=(P("seq", "res", None), P(None, "res", "seq"), P(), P(), P(), P(), P()),
        check_vma=False,
    )
```

```python
import functools

import jax
import jax.numpy as jnp
from jax import lax
from jax.experimental import pallas as pl
from jax.experimental.pallas import tpu as pltpu
from jax.sharding import PartitionSpec as P

C = 64
H = 8
DH = 8
LANES = 128
ROWS = 8

EXACT = lax.Precision.HIGHEST
THREE = lax.Precision.HIGH
EPSILON = 1e-05
MASKED = 1000000000.0
SCALE = DH ** (-0.5)
F32 = jnp.float32


def dot(a, b, over=((1,), (0,)), precision=THREE):
    return lax.dot_general(a, b, (over, ((), ())), precision=precision, preferred_element_type=F32)


def dot_rows(a, b):
    return dot(a, b, ((0,), (0,)))


def dot_t(a, b, precision=THREE):
    return dot(a, b, ((1,), (1,)), precision)


def to_column(row):
    eye = lax.broadcasted_iota(jnp.int32, (C, C), 0) == lax.broadcasted_iota(jnp.int32, (C, C), 1)
    return jnp.sum(jnp.where(eye, row, 0.0), axis=1, keepdims=True)


def to_row(column):
    eye = lax.broadcasted_iota(jnp.int32, (C, C), 0) == lax.broadcasted_iota(jnp.int32, (C, C), 1)
    return jnp.sum(jnp.where(eye, column, 0.0), axis=0, keepdims=True)


def normalise(values):
    centred = values - jnp.mean(values, axis=-1, keepdims=True)
    inverse = lax.rsqrt(jnp.mean(centred * centred, axis=-1, keepdims=True) + EPSILON)
    return centred * inverse, inverse


def normalise_back(grad_normed, gain, unit, inverse):
    grad_unit = grad_normed * gain
    along = jnp.mean(grad_unit * unit, axis=-1, keepdims=True)
    return inverse * (grad_unit - jnp.mean(grad_unit, axis=-1, keepdims=True) - unit * along)


def head_mask(rows):
    channel = lax.broadcasted_iota(jnp.int32, (C, H * rows), 0)
    lane = lax.broadcasted_iota(jnp.int32, (C, H * rows), 1)
    return (lane // rows == channel // DH).astype(F32)


def spread_heads(values, mask):
    rows = values.shape[0]
    turned = jnp.transpose(values)
    turned = jnp.concatenate([turned] * (LANES // rows), axis=1)
    return jnp.concatenate([turned] * (H * rows // LANES), axis=1) * mask


def join_heads(values, mask):
    masked = values * mask
    rows = mask.shape[1] // H
    total = masked[:, :LANES]
    for i in range(1, H * rows // LANES):
        total = total + masked[:, i * LANES : (i + 1) * LANES]
    joined = total[:, :rows]
    for i in range(1, LANES // rows):
        joined = joined + total[:, i * rows : (i + 1) * rows]
    return jnp.transpose(joined)


def turn_bias(bias, bias_out):
    n_keys = bias.shape[2]
    bias_out[...] = jnp.transpose(bias[...].reshape(-1, n_keys).astype(F32))


def own_half(seq_mask, own, gains, w_row,
             own_unit_out, query_gate_out, query_heads_out, own_memory_out, present_out):
    n_seq, n_rows, _ = own.shape
    w_all = w_row[...]
    own_units, _ = normalise(own[...].reshape(n_seq * n_rows, C).astype(F32))
    projected = dot(own_units * gains[0:1, :], w_all, precision=EXACT)
    queries = projected[:, :C] * SCALE
    gates = jax.nn.sigmoid(projected[:, 3 * C :])
    own_unit_out[...] = own_units.reshape(n_seq, n_rows, C)
    query_gate_out[...] = jnp.concatenate([queries, gates], axis=1).reshape(n_seq, n_rows, 2 * C)
    own_memory_out[...] = projected[:, C : 3 * C].reshape(n_seq, n_rows, 2 * C)
    mask = head_mask(n_rows)
    for s in range(n_seq):
        query_heads_out[s] = spread_heads(queries[s * n_rows : (s + 1) * n_rows], mask)
    lane = lax.broadcasted_iota(jnp.int32, present_out.shape, 1) // (2 * C // n_seq)
    present = jnp.zeros(present_out.shape, F32)
    for s in range(n_seq):
        present = jnp.where(lane == s, seq_mask[s].astype(F32), present)
    present_out[...] = present


def row_forward(n_res, *refs):
    sent = refs[:n_res]
    (own, cotangent, gains, w_row, w_out, own_unit, query_gate, query_heads, own_memory, bias_t, present) = refs[
        n_res : n_res + 11
    ]
    residues = refs[n_res + 11 : 2 * n_res + 11]
    payload, exponent_out, unit_out, memory_out, mixture_out, inverse_out, residue = refs[2 * n_res + 11 :]
    n_seq, n_rows, _ = own.shape
    n_keys = n_res * n_rows
    me = lax.axis_index("res")
    w_memory = w_row[:, C : 3 * C]
    for away in range(n_res):
        where = lax.rem(me + away, n_res)
        residue[where] = jnp.broadcast_to(residues[away][...].astype(F32), (ROWS, n_rows))
        if away:
            units, _ = normalise(sent[away][...].reshape(n_seq * n_rows, C))
            memories = dot(units * gains[0:1, :], w_memory, precision=EXACT)
            units = units.reshape(n_seq, n_rows, C)
            memories = memories.reshape(n_seq, n_rows, 2 * C)
        else:
            units, memories = own_unit[...], own_memory[...]
        unit_out[where] = units
        memory_out[where] = memories
    n_blocks = payload.shape[0]
    block = n_rows // n_blocks
    present_keys = jnp.transpose(jnp.concatenate([residue[i] for i in range(n_res)], axis=1))[:, 0:1]
    key_bias = MASKED * (present_keys - 1.0)
    mask = head_mask(n_rows)
    wide_mask = jnp.concatenate([mask, mask], axis=0)
    initial = own[...].reshape(n_seq * n_rows, C).astype(F32)
    gates = query_gate[...].reshape(n_seq * n_rows, 2 * C)[:, C:]
    sums = []
    for s in range(n_seq):
        memory = memory_out[:, s].reshape(n_keys, 2 * C)
        scores = dot(memory[:, :C], query_heads[s], precision=EXACT) + bias_t[...] + key_bias
        exponent = jnp.exp(scores - jnp.max(scores, axis=0, keepdims=True))
        exponent_out[s] = exponent
        summed = dot_rows(jnp.concatenate([memory[:, C:], jnp.ones((n_keys, C), F32)], axis=1), exponent)
        sums.append(join_heads(summed, wide_mask))
    summed = jnp.concatenate(sums, axis=0)
    inverse = 1.0 / summed[:, C:]
    mixture = summed[:, :C] * inverse
    inverse_out[...] = inverse.reshape(n_seq, n_rows, C)
    mixture_out[...] = mixture.reshape(n_seq, n_rows, C)
    middle = initial + dot(gates * mixture, w_out[...])
    both = jnp.concatenate([middle, cotangent[...].reshape(n_seq * n_rows, C).astype(F32)], axis=1)
    for s in range(n_seq):
        for b in range(n_blocks):
            row = s * n_rows + b * block
            payload[b, s] = both[row : row + block, :]
    for b in range(n_blocks):
        payload[b, n_seq] = present[...]


def column_step(arrived, gains, w_col, w_out, returned, gathered, mask_rows, n_seq):
    n_src, _, block, _ = arrived.shape
    group = n_seq * block
    rows = n_src * group
    wide = 2 * C // n_seq
    share = C // n_src
    for src in range(n_src):
        for s in range(n_seq):
            gathered[src, s * block : (s + 1) * block, :] = arrived[src, s]
            mask_rows[src, s * block : (s + 1) * block, :] = jnp.broadcast_to(
                arrived[src, n_seq, :, s * wide : s * wide + 1], (block, C)
            )
    data = gathered[...].reshape(rows, 2 * C)
    present = mask_rows[...]
    middle = data[:, :C]
    cot = data[:, C:]
    gain = gains[1:2, :]

    def over_sequences(values, combine, reduce):
        total = reduce(values.reshape(n_src, group, C), axis=0)
        result = total
        for shift in range(1, n_seq):
            result = combine(result, pltpu.roll(total, shift * block, 0))
        return result

    def total_of(values):
        return over_sequences(values, jnp.add, jnp.sum)

    def spread(values):
        return jnp.broadcast_to(values[None], (n_src, group, C)).reshape(rows, C)

    lane = lax.broadcasted_iota(jnp.int32, (C, C), 1)
    row = lax.broadcasted_iota(jnp.int32, (C, C), 0)
    same_head = (row // DH == lane // DH).astype(F32)
    repeat = (lax.broadcasted_iota(jnp.int32, (DH, C), 0) == lax.broadcasted_iota(jnp.int32, (DH, C), 1) % DH).astype(F32)
    w_all = w_col[...]
    w_query = w_all[:, :C]
    w_key = dot(w_all[:, C : C + DH], repeat, precision=EXACT)
    w_value = dot(w_all[:, C + DH : C + 2 * DH], repeat)
    w_gate = w_all[:, C + 2 * DH :]
    w_rest = jnp.concatenate([w_key, w_value, w_gate], axis=1)

    unit, inverse = normalise(middle)
    normed = unit * gain
    present_rows = present.reshape(rows, C)
    counted = total_of(present_rows)
    mean_unit = total_of(present_rows * unit) / counted
    mean_normed = mean_unit * gain
    query = dot(mean_normed, w_query, precision=EXACT) * SCALE
    query_rows = spread(query)
    rest = dot(normed, w_rest, precision=EXACT)
    key, value = rest[:, :C], rest[:, C : 2 * C]
    gate = jax.nn.sigmoid(rest[:, 2 * C :])
    scores = dot(query_rows * key, same_head, precision=EXACT) + MASKED * (present_rows - 1.0)
    peak = over_sequences(scores, jnp.maximum, jnp.max)
    exponent = jnp.exp(scores - spread(peak))
    weights = exponent / spread(total_of(exponent))
    mixture = total_of(weights * value)
    mixture_rows = spread(mixture)

    grad_gated = dot_t(cot, w_out[...])
    out_grad = dot_rows(gate * mixture_rows, cot)
    grad_mixture = total_of(gate * grad_gated)
    grad_mixture_rows = spread(grad_mixture)
    grad_gate = grad_gated * mixture_rows * gate * (1.0 - gate)
    grad_weights = dot(grad_mixture_rows * value, same_head)
    inner = spread(dot(grad_mixture * mixture, same_head))
    grad_scores = weights * (grad_weights - inner)
    grad_rest = jnp.concatenate([grad_scores * query_rows, weights * grad_mixture_rows, grad_gate], axis=1)
    grad_query = total_of(grad_scores * key) * SCALE
    grad_mean = dot_t(grad_query, w_query)
    grad_normed = present_rows * spread(grad_mean / counted) + dot_t(grad_rest, w_rest)
    grad_query_weights = dot_rows(mean_unit, grad_query) * (1.0 / n_seq)
    grad_rest_weights = dot_rows(unit, grad_rest)
    fold_row = lax.broadcasted_iota(jnp.int32, (2 * C, 2 * DH), 0)
    fold_lane = lax.broadcasted_iota(jnp.int32, (2 * C, 2 * DH), 1)
    fold = ((fold_row // C == fold_lane // DH) & (fold_row % DH == fold_lane % DH)).astype(F32)
    grad_key_value = dot(grad_rest_weights[:, : 2 * C], fold)
    first = jnp.concatenate([grad_query_weights, grad_rest_weights[:, 2 * C :]], axis=1)
    second = jnp.concatenate([out_grad, grad_key_value, jnp.zeros((C, C - 2 * DH), F32)], axis=1)
    grad_middle = (cot + normalise_back(grad_normed, gain, unit, inverse)).reshape(n_src, group, C)
    for src in range(n_src):
        for s in range(n_seq):
            returned[src, 0, :, s * C : (s + 1) * C] = grad_middle[src, s * block : (s + 1) * block, :]
        returned[src, 1] = first[src * share : (src + 1) * share, :]
        returned[src, 2] = second[src * share : (src + 1) * share, :]


def row_backward(n_res, returned, exponent_in, unit_in, memory_in, query_gate_in, query_heads_in, mixture_in, inverse_in,
                 own_unit_in, w_row, w_out, bias_out, middle_grad, *refs):
    sums_out, shares = refs[:n_res], refs[n_res]
    me = lax.axis_index("res")
    n_seq, n_rows, _ = middle_grad.shape
    n_keys = n_res * n_rows
    n_blocks, _, block, _ = returned.shape
    w_all = w_row[...]
    w_memory = w_all[:, C : 3 * C]
    w_query_gate = jnp.concatenate([w_all[:, :C], w_all[:, 3 * C :]], axis=1)
    mask = head_mask(n_rows)
    for b in range(n_blocks):
        for s in range(n_seq):
            middle_grad[s, b * block : (b + 1) * block, :] = returned[b, 0, :, s * C : (s + 1) * C]
    grad_middle = middle_grad[...].reshape(n_seq * n_rows, C)
    queries_gates = query_gate_in[...].reshape(n_seq * n_rows, 2 * C)
    gates = queries_gates[:, C:]
    mixtures = mixture_in[...].reshape(n_seq * n_rows, C)
    grad_gated = dot_t(grad_middle, w_out[...])
    grad_out = dot_rows(gates * mixtures, grad_middle)
    grad_gates = grad_gated * mixtures * gates * (1.0 - gates)
    grad_mixtures = grad_gated * gates * inverse_in[...].reshape(n_seq * n_rows, C)
    inners = grad_mixtures * mixtures
    bias_grad = jnp.zeros((n_keys, H * n_rows), F32)
    grad_queries = []
    grad_memories = []
    for s in range(n_seq):
        rows = slice(s * n_rows, (s + 1) * n_rows)
        memory = memory_in[:, s].reshape(n_keys, 2 * C)
        exponent = exponent_in[s]
        grad_heads = spread_heads(grad_mixtures[rows], mask)
        right = jnp.concatenate([grad_heads, spread_heads(inners[rows], mask)], axis=0)
        left = jnp.concatenate([memory[:, C:], jnp.full((n_keys, C), -1.0, F32)], axis=1)
        grad_scores = exponent * dot(left, right)
        bias_grad = bias_grad + grad_scores
        grad_queries.append(join_heads(dot_rows(memory[:, :C], grad_scores), mask) * SCALE)
        grad_key = dot_t(grad_scores, query_heads_in[s])
        grad_value = dot_t(exponent, grad_heads)
        grad_memories.append(jnp.concatenate([grad_key, grad_value], axis=1))
    grad_query_gate = jnp.concatenate([jnp.concatenate(grad_queries, axis=0), grad_gates], axis=1)
    grad_memory = jnp.concatenate(grad_memories, axis=0)
    grad_query_gate_weights = dot_rows(own_unit_in[...].reshape(n_seq * n_rows, C), grad_query_gate)
    units = jnp.concatenate([unit_in[:, s].reshape(n_keys, C) for s in range(n_seq)], axis=0)
    grad_memory_weights = dot_rows(units, grad_memory)
    from_memory = dot_t(grad_memory, w_memory)
    from_own = dot_t(grad_query_gate, w_query_gate)
    from_memory = [from_memory[s * n_keys : (s + 1) * n_keys] for s in range(n_seq)]
    from_own = [from_own[s * n_rows : (s + 1) * n_rows] for s in range(n_seq)]
    bias_out[...] = bias_grad
    half = C // 2
    weight_grads = jnp.concatenate(
        [grad_query_gate_weights, grad_memory_weights, jnp.concatenate([grad_out[:half], grad_out[half:]], axis=1)],
        axis=0,
    )
    part = shares.shape[1] - ROWS - n_rows
    shares[...] = jnp.zeros(shares.shape, F32)
    share = C // n_blocks
    column = jnp.sum(returned[:, 1:, :, :], axis=0)
    normed = jnp.concatenate(from_memory, axis=1)
    for i in range(n_res):
        rows = min(part, max(0, weight_grads.shape[0] - i * part))
        if rows:
            shares[i, :rows, :] = weight_grads[i * part : i * part + rows, :]
        shares[i, part : part + share, :] = column[0]
        shares[i, part + share : part + 2 * share, :] = column[1]
        shares[i, part + ROWS :, :] = normed[i * n_rows : (i + 1) * n_rows, :]
    for away in range(n_res):
        sums_out[away][...] = shares[lax.rem(me + away, n_res)]
    sums_out[0][part + ROWS :, :] += jnp.concatenate(from_own, axis=1)


def step_bits(n_seq_devices, odd):
    bits = list(range(n_seq_devices.bit_length() - 1))
    if odd:
        for i in range(0, len(bits) - 1, 2):
            bits[i], bits[i + 1] = bits[i + 1], bits[i]
    return bits


def relative_block(mask_of_bits, n_blocks):
    odd = lax.rem(lax.axis_index("res"), 2)
    even_mask = mask_of_bits(step_bits(n_blocks, False))
    odd_mask = mask_of_bits(step_bits(n_blocks, True))
    return lax.axis_index("seq") ^ (even_mask + odd * (odd_mask - even_mask))


def split_blocks(bias_t, state, send):
    tiles = bias_t.shape[1] // LANES
    n_blocks = (state.shape[0] + send.shape[0]) // tiles
    keys_each = bias_t.shape[0] // n_blocks
    half = n_blocks // 2

    for slot in range(n_blocks):

        def mask_of_bits(bits):
            last = len(bits) - 1
            return sum(1 << bit for at, bit in enumerate(bits) if slot >> (last - at) & 1)

        block = relative_block(mask_of_bits, n_blocks)
        values = bias_t[pl.ds(pl.multiple_of(block * keys_each, keys_each), keys_each), :]
        for i in range(tiles):
            out, at = (state, slot) if slot < half else (send, slot - half)
            out[at * tiles + i] = values[:, i * LANES : (i + 1) * LANES]


def bias_last(state, arrived, bias_out):
    heads, _, n_rows = bias_out.shape
    each = LANES // n_rows
    for i in range(state.shape[0]):
        total = state[i] + arrived[i]
        for e in range(each):
            bias_out[i * each + e] = total[:, e * n_rows : (e + 1) * n_rows]


def add_shares(bias_send, *refs):
    sums, send, normed = refs[:-2], refs[-2], refs[-1]
    total = sums[0][...]
    for more in sums[1:]:
        total = total + more[...]
    left = bias_send.shape[0]
    rows = total.shape[0] - normed.shape[0]
    send[:left] = bias_send[...]
    send[left:] = total[:rows].reshape(rows // ROWS, ROWS, LANES)
    normed[...] = total[rows:]


def step(part, state, sent, arrived, state_out, send):
    left = state.shape[0]
    half = left // 2
    total = state[...] + arrived[:left]
    state_out[...] = total[:half]
    send[:half] = total[half:]
    send[half : half + part] = sent[left : left + part] + arrived[left : left + part]
    pieces = sent.shape[0] - left - part
    send[half + part : half + part + pieces] = sent[left + part :]
    send[half + part + pieces :] = arrived[left + part :]


def last_step(sent, arrived, _, shared, joined):
    part = shared.shape[0]
    pieces = joined.shape[0] // 2
    left = sent.shape[0] - part - pieces
    shared[...] = sent[left : left + part] + arrived[left : left + part]
    joined[:pieces] = sent[left + part :]
    joined[pieces:] = arrived[left + part :]


def finish_alignment(own, middle_grad, gains, normed, out, done):
    n_seq = own.shape[0]
    done[...] = jnp.zeros(done.shape, F32)
    for s in range(n_seq):
        unit, inverse = normalise(own[s].astype(F32))
        grad_normed = normed[:, s * C : (s + 1) * C]
        out[s] = (middle_grad[s] + normalise_back(grad_normed, gains[0:1, :], unit, inverse)).astype(out.dtype)


def unpack(n_res, joined, *refs):
    parts = refs[:n_res]
    gains, w_row, w_col, gains_out, row_project_out, row_out_out, col_project_out, col_out_out = refs[n_res : n_res + 8]
    shares, column = refs[n_res + 8 :]
    me = lax.axis_index("res")
    part = shares.shape[1]
    for away in range(n_res):
        shares[lax.rem(me + away, n_res)] = parts[away][...].reshape(part, LANES)
    n_blocks, _, share, _ = column.shape
    for slot in range(n_blocks):
        block = relative_block(
            lambda bits: sum(1 << bit for at, bit in enumerate(bits) if slot >> at & 1), n_blocks
        )
        piece = joined[slot]
        column[block, 0] = piece[:share]
        column[block, 1] = piece[share : 2 * share]
    flat = jnp.concatenate([shares[i] for i in range(n_res)], axis=0)
    query_gate, memory, outs = flat[:C], flat[C : 2 * C], flat[2 * C : 2 * C + C // 2]
    col_query_gate = jnp.concatenate([column[i, 0] for i in range(n_blocks)], axis=0)
    col_rest = jnp.concatenate([column[i, 1] for i in range(n_blocks)], axis=0)
    rest = col_rest[:, C : C + 2 * DH]
    gain_row = to_column(gains[0:1, :])
    gain_col = to_column(gains[1:2, :])
    w_all = w_row[...]
    w_column = w_col[...]
    row_gain_grad = (
        jnp.sum(query_gate[:, :C] * w_all[:, :C], axis=1, keepdims=True)
        + jnp.sum(memory * w_all[:, C : 3 * C], axis=1, keepdims=True)
        + jnp.sum(query_gate[:, C:] * w_all[:, 3 * C :], axis=1, keepdims=True)
    )
    col_gain_grad = (
        jnp.sum(col_query_gate[:, :C] * w_column[:, :C], axis=1, keepdims=True)
        + jnp.sum(rest * w_column[:, C : C + 2 * DH], axis=1, keepdims=True)
        + jnp.sum(col_query_gate[:, C:] * w_column[:, C + 2 * DH :], axis=1, keepdims=True)
    )
    gains_out[0:1, :] = to_row(row_gain_grad)
    gains_out[1:2, :] = to_row(col_gain_grad)
    row_project_out[:, :C] = query_gate[:, :C] * gain_row
    row_project_out[:, C : 3 * C] = memory * gain_row
    row_project_out[:, 3 * C :] = query_gate[:, C:] * gain_row
    col_project_out[:, :C] = col_query_gate[:, :C] * gain_col
    col_project_out[:, C : C + 2 * DH] = rest * gain_col
    col_project_out[:, C + 2 * DH :] = col_query_gate[:, C:] * gain_col
    half = C // 2
    row_out_out[:half, :] = outs[:, :C]
    row_out_out[half:, :] = outs[:, C:]
    col_out_out[...] = col_rest[:, :C]


def call(body, outs, *operands, smem=0, unread=0, scratch=(), name):
    vmem = pl.BlockSpec(memory_space=pltpu.VMEM)
    scalar = pl.BlockSpec(memory_space=pltpu.SMEM)
    return pl.pallas_call(
        body,
        out_shape=[jax.ShapeDtypeStruct(shape, kind) for shape, kind in outs],
        in_specs=[scalar] * smem + [vmem] * (len(operands) - smem - unread)
        + [pl.BlockSpec(memory_space=pl.ANY)] * unread,
        out_specs=[vmem] * len(outs),
        scratch_shapes=list(scratch),
        compiler_params=pltpu.CompilerParams(vmem_limit_bytes=32 * 1024 * 1024),
        name=name,
    )(*operands)


def shift_residues(values, away, count):
    return lax.ppermute(values, "res", [((i + away) % count, i) for i in range(count)])


def cross(values, at, seq_count, res_count):
    pairs = []
    for r in range(res_count):
        bit = 1 << step_bits(seq_count, r % 2)[at]
        pairs += [(i * res_count + r, (i ^ bit) * res_count + r) for i in range(seq_count)]
    return lax.ppermute(values, ("seq", "res"), pairs)


def swap_blocks(values):
    return lax.all_to_all(values, "seq", 0, 0, tiled=True)


def local(
    alignment,
    cotangent,
    pair_bias,
    norm_gains,
    row_project,
    row_output,
    column_project,
    column_output,
    residue_mask,
    sequence_mask,
    seq_count,
    res_count,
):
    n_seq, n_rows, _ = alignment.shape
    n_keys = pair_bias.shape[2]
    block = n_rows // seq_count
    group = n_seq * block
    away_range = range(1, res_count)
    residues = [residue_mask] + [shift_residues(residue_mask, away, res_count) for away in away_range]
    residues = [value.reshape(1, n_rows) for value in residues]
    sent = lax.optimization_barrier(alignment.astype(F32))
    own_unit, query_gate, query_heads, own_memory, present = call(
        own_half,
        [
            ((n_seq, n_rows, C), F32),
            ((n_seq, n_rows, 2 * C), F32),
            ((n_seq, C, H * n_rows), F32),
            ((n_seq, n_rows, 2 * C), F32),
            ((block, 2 * C), F32),
        ],
        sequence_mask, alignment, norm_gains, row_project,
        smem=1,
        name="own_half",
    )
    (bias_t,) = call(turn_bias, [((n_keys, H * n_rows), F32)], pair_bias, name="turn_bias")
    payload, exponent, unit, memory, mixture, inverse = call(
        functools.partial(row_forward, res_count),
        [
            ((seq_count, n_seq + 1, block, 2 * C), F32),
            ((n_seq, n_keys, H * n_rows), F32),
            ((res_count, n_seq, n_rows, C), F32),
            ((res_count, n_seq, n_rows, 2 * C), F32),
            ((n_seq, n_rows, C), F32),
            ((n_seq, n_rows, C), F32),
        ],
        sent, *[shift_residues(sent, away, res_count) for away in away_range],
        alignment, cotangent, norm_gains, row_project, row_output, own_unit, query_gate, query_heads, own_memory, bias_t,
        present, *residues,
        scratch=[pltpu.VMEM((res_count, ROWS, n_rows), F32)],
        name="row_forward",
    )
    arrived = swap_blocks(payload)
    (returned,) = call(
        functools.partial(column_step, n_seq=n_seq),
        [((seq_count, 3, block, 2 * C), F32)],
        arrived, norm_gains, column_project, column_output,
        scratch=[pltpu.VMEM((seq_count, group, 2 * C), F32), pltpu.VMEM((seq_count, group, C), F32)],
        name="column_step",
    )
    returned = swap_blocks(returned)
    part = -(-5 * C // (2 * ROWS * res_count)) * ROWS
    keys_each = n_keys // seq_count
    tiles = H * n_rows // LANES
    left = seq_count // 2 * tiles
    bias_grad, middle_grad, *sums = call(
        functools.partial(row_backward, res_count),
        [((n_keys, H * n_rows), F32), ((n_seq, n_rows, C), F32)]
        + [((part + ROWS + n_rows, LANES), F32)] * res_count,
        returned, exponent, unit, memory, query_gate, query_heads, mixture, inverse, own_unit, row_project, row_output,
        scratch=[pltpu.VMEM((res_count, part + ROWS + n_rows, LANES), F32)],
        name="row_backward",
    )
    sums = sums[:1] + [shift_residues(sums[away], -away, res_count) for away in away_range]
    state, send = call(
        split_blocks, [((left, keys_each, LANES), F32)] * 2, bias_grad, name="split_blocks"
    )
    part_tiles = part // ROWS
    send, normed = call(
        add_shares,
        [((left + part_tiles + 1, ROWS, LANES), F32), ((n_rows, LANES), F32)],
        send, *sums,
        name="add_shares",
    )
    grad_alignment, done = call(
        finish_alignment,
        [(alignment.shape, alignment.dtype), ((ROWS, LANES), F32)],
        alignment, middle_grad, norm_gains, normed,
        name="finish_alignment",
    )
    steps = seq_count.bit_length() - 1
    for at in range(steps):
        arrived = cross(send, at, seq_count, res_count)
        if at < steps - 1:
            left //= 2
            state, send = call(
                functools.partial(step, part_tiles),
                [((left, ROWS, LANES), F32), ((left + part_tiles + (2 << at), ROWS, LANES), F32)],
                state, send, arrived,
                name="step",
            )
    shared, joined = call(
        last_step,
        [((part_tiles, ROWS, LANES), F32), ((seq_count, ROWS, LANES), F32)],
        send, arrived, done,
        unread=1,
        name="last_step",
    )
    (bias_grad,) = call(bias_last, [((H, keys_each, n_rows), F32)], state, arrived, name="bias_last")
    grads = call(
        functools.partial(unpack, res_count),
        [((2, C), F32), ((C, 4 * C), F32), ((C, C), F32), ((C, 2 * C + 2 * DH), F32), ((C, C), F32)],
        joined, shared, *[shift_residues(shared, away, res_count) for away in away_range],
        norm_gains, row_project, column_project,
        scratch=[
            pltpu.VMEM((res_count, part, LANES), F32),
            pltpu.VMEM((seq_count, 2, C // seq_count, LANES), F32),
        ],
        name="unpack",
    )
    return (grad_alignment, jnp.transpose(bias_grad, (0, 2, 1)), *grads)


def solution(mesh):
    placed = (
        P("seq", "res", None),
        P("seq", "res", None),
        P(None, "res", None),
        P(),
        P(),
        P(),
        P(),
        P(),
        P("res"),
        P("seq"),
    )
    return jax.shard_map(
        functools.partial(local, seq_count=mesh.shape["seq"], res_count=mesh.shape["res"]),
        mesh=mesh,
        in_specs=placed,
        out_specs=(P("seq", "res", None), P(None, "res", "seq"), P(), P(), P(), P(), P()),
        check_vma=False,
    )
```

```python
import functools

import jax
import jax.numpy as jnp
from jax import lax
from jax.experimental import pallas as pl
from jax.experimental.pallas import tpu as pltpu
from jax.sharding import PartitionSpec as P

C = 64
H = 8
DH = 8
LANES = 128
ROWS = 8

EXACT = lax.Precision.HIGHEST
THREE = lax.Precision.HIGH
EPSILON = 1e-05
MASKED = 1000000000.0
SCALE = DH ** (-0.5)
F32 = jnp.float32


def dot(a, b, over=((1,), (0,)), precision=THREE):
    return lax.dot_general(a, b, (over, ((), ())), precision=precision, preferred_element_type=F32)


def dot_rows(a, b):
    return dot(a, b, ((0,), (0,)))


def dot_t(a, b, precision=THREE):
    return dot(a, b, ((1,), (1,)), precision)


def to_column(row):
    eye = lax.broadcasted_iota(jnp.int32, (C, C), 0) == lax.broadcasted_iota(jnp.int32, (C, C), 1)
    return jnp.sum(jnp.where(eye, row, 0.0), axis=1, keepdims=True)


def to_row(column):
    eye = lax.broadcasted_iota(jnp.int32, (C, C), 0) == lax.broadcasted_iota(jnp.int32, (C, C), 1)
    return jnp.sum(jnp.where(eye, column, 0.0), axis=0, keepdims=True)


def normalise(values):
    centred = values - jnp.mean(values, axis=-1, keepdims=True)
    inverse = lax.rsqrt(jnp.mean(centred * centred, axis=-1, keepdims=True) + EPSILON)
    return centred * inverse, inverse


def normalise_back(grad_normed, gain, unit, inverse):
    grad_unit = grad_normed * gain
    along = jnp.mean(grad_unit * unit, axis=-1, keepdims=True)
    return inverse * (grad_unit - jnp.mean(grad_unit, axis=-1, keepdims=True) - unit * along)


def head_mask(rows):
    channel = lax.broadcasted_iota(jnp.int32, (C, H * rows), 0)
    lane = lax.broadcasted_iota(jnp.int32, (C, H * rows), 1)
    return (lane // rows == channel // DH).astype(F32)


def spread_heads(values, mask):
    rows = values.shape[0]
    turned = jnp.transpose(values)
    turned = jnp.concatenate([turned] * (LANES // rows), axis=1)
    return jnp.concatenate([turned] * (H * rows // LANES), axis=1) * mask


def join_heads(values, mask):
    masked = values * mask
    rows = mask.shape[1] // H
    total = masked[:, :LANES]
    for i in range(1, H * rows // LANES):
        total = total + masked[:, i * LANES : (i + 1) * LANES]
    joined = total[:, :rows]
    for i in range(1, LANES // rows):
        joined = joined + total[:, i * rows : (i + 1) * rows]
    return jnp.transpose(joined)


def own_half(seq_mask, own, gains, w_row,
             own_unit_out, query_gate_out, query_heads_out, own_memory_out, present_out):
    n_seq, n_rows, _ = own.shape
    w_all = w_row[...]
    own_units, _ = normalise(own[...].reshape(n_seq * n_rows, C).astype(F32))
    projected = dot(own_units * gains[0:1, :], w_all, precision=EXACT)
    queries = projected[:, :C] * SCALE
    gates = jax.nn.sigmoid(projected[:, 3 * C :])
    own_unit_out[...] = own_units.reshape(n_seq, n_rows, C)
    query_gate_out[...] = jnp.concatenate([queries, gates], axis=1).reshape(n_seq, n_rows, 2 * C)
    own_memory_out[...] = projected[:, C : 3 * C].reshape(n_seq, n_rows, 2 * C)
    mask = head_mask(n_rows)
    for s in range(n_seq):
        query_heads_out[s] = spread_heads(queries[s * n_rows : (s + 1) * n_rows], mask)
    lane = lax.broadcasted_iota(jnp.int32, present_out.shape, 1) // (2 * C // n_seq)
    present = jnp.zeros(present_out.shape, F32)
    for s in range(n_seq):
        present = jnp.where(lane == s, seq_mask[s].astype(F32), present)
    present_out[...] = present


def row_forward(n_res, *refs):
    sent = refs[:n_res]
    (own, cotangent, gains, w_row, w_out, own_unit, query_gate, query_heads, own_memory, bias, present) = refs[
        n_res : n_res + 11
    ]
    payload, exponent_out, unit_out, memory_out, mixture_out, inverse_out, residue = refs[n_res + 11 :]
    n_seq, n_rows, _ = own.shape
    n_keys = n_res * n_rows
    me = lax.axis_index("res")
    w_memory = w_row[:, C : 3 * C]
    for away in range(n_res):
        where = lax.rem(me + away, n_res)
        residue[where] = sent[away][n_seq]
        if away:
            units, _ = normalise(sent[away][:n_seq].reshape(n_seq * n_rows, C))
            memories = dot(units * gains[0:1, :], w_memory, precision=EXACT)
            units = units.reshape(n_seq, n_rows, C)
            memories = memories.reshape(n_seq, n_rows, 2 * C)
        else:
            units, memories = own_unit[...], own_memory[...]
        unit_out[where] = units
        memory_out[where] = memories
    n_blocks = payload.shape[0]
    block = n_rows // n_blocks
    bias_t = jnp.transpose(bias[...].reshape(H * n_rows, n_keys).astype(F32))
    key_bias = MASKED * (residue[...].reshape(n_keys, C)[:, 0:1] - 1.0)
    mask = head_mask(n_rows)
    wide_mask = jnp.concatenate([mask, mask], axis=0)
    initial = own[...].reshape(n_seq * n_rows, C).astype(F32)
    gates = query_gate[...].reshape(n_seq * n_rows, 2 * C)[:, C:]
    sums = []
    for s in range(n_seq):
        memory = memory_out[:, s].reshape(n_keys, 2 * C)
        scores = dot(memory[:, :C], query_heads[s], precision=EXACT) + bias_t + key_bias
        exponent = jnp.exp(scores - jnp.max(scores, axis=0, keepdims=True))
        exponent_out[s] = exponent
        summed = dot_rows(jnp.concatenate([memory[:, C:], jnp.ones((n_keys, C), F32)], axis=1), exponent)
        sums.append(join_heads(summed, wide_mask))
    summed = jnp.concatenate(sums, axis=0)
    inverse = 1.0 / summed[:, C:]
    mixture = summed[:, :C] * inverse
    inverse_out[...] = inverse.reshape(n_seq, n_rows, C)
    mixture_out[...] = mixture.reshape(n_seq, n_rows, C)
    middle = initial + dot(gates * mixture, w_out[...])
    both = jnp.concatenate([middle, cotangent[...].reshape(n_seq * n_rows, C).astype(F32)], axis=1)
    for s in range(n_seq):
        for b in range(n_blocks):
            row = s * n_rows + b * block
            payload[b, s] = both[row : row + block, :]
    for b in range(n_blocks):
        payload[b, n_seq] = present[...]


def column_step(arrived, gains, w_col, w_out, returned, gathered, mask_rows, n_seq):
    n_src, _, block, _ = arrived.shape
    group = n_seq * block
    rows = n_src * group
    wide = 2 * C // n_seq
    share = C // n_src
    for src in range(n_src):
        for s in range(n_seq):
            gathered[src, s * block : (s + 1) * block, :] = arrived[src, s]
            mask_rows[src, s * block : (s + 1) * block, :] = jnp.broadcast_to(
                arrived[src, n_seq, :, s * wide : s * wide + 1], (block, C)
            )
    data = gathered[...].reshape(rows, 2 * C)
    present = mask_rows[...]
    middle = data[:, :C]
    cot = data[:, C:]
    gain = gains[1:2, :]

    def over_sequences(values, combine, reduce):
        total = reduce(values.reshape(n_src, group, C), axis=0)
        result = total
        for shift in range(1, n_seq):
            result = combine(result, pltpu.roll(total, shift * block, 0))
        return result

    def total_of(values):
        return over_sequences(values, jnp.add, jnp.sum)

    def spread(values):
        return jnp.broadcast_to(values[None], (n_src, group, C)).reshape(rows, C)

    lane = lax.broadcasted_iota(jnp.int32, (C, C), 1)
    row = lax.broadcasted_iota(jnp.int32, (C, C), 0)
    same_head = (row // DH == lane // DH).astype(F32)
    repeat = (lax.broadcasted_iota(jnp.int32, (DH, C), 0) == lax.broadcasted_iota(jnp.int32, (DH, C), 1) % DH).astype(F32)
    w_all = w_col[...]
    w_query = w_all[:, :C]
    w_key = dot(w_all[:, C : C + DH], repeat, precision=EXACT)
    w_value = dot(w_all[:, C + DH : C + 2 * DH], repeat)
    w_gate = w_all[:, C + 2 * DH :]
    w_rest = jnp.concatenate([w_key, w_value, w_gate], axis=1)

    unit, inverse = normalise(middle)
    normed = unit * gain
    present_rows = present.reshape(rows, C)
    counted = total_of(present_rows)
    mean_unit = total_of(present_rows * unit) / counted
    mean_normed = mean_unit * gain
    query = dot(mean_normed, w_query, precision=EXACT) * SCALE
    query_rows = spread(query)
    rest = dot(normed, w_rest, precision=EXACT)
    key, value = rest[:, :C], rest[:, C : 2 * C]
    gate = jax.nn.sigmoid(rest[:, 2 * C :])
    scores = dot(query_rows * key, same_head, precision=EXACT) + MASKED * (present_rows - 1.0)
    peak = over_sequences(scores, jnp.maximum, jnp.max)
    exponent = jnp.exp(scores - spread(peak))
    weights = exponent / spread(total_of(exponent))
    mixture = total_of(weights * value)
    mixture_rows = spread(mixture)

    grad_gated = dot_t(cot, w_out[...])
    out_grad = dot_rows(gate * mixture_rows, cot)
    grad_mixture = total_of(gate * grad_gated)
    grad_mixture_rows = spread(grad_mixture)
    grad_gate = grad_gated * mixture_rows * gate * (1.0 - gate)
    grad_weights = dot(grad_mixture_rows * value, same_head)
    inner = spread(dot(grad_mixture * mixture, same_head))
    grad_scores = weights * (grad_weights - inner)
    grad_rest = jnp.concatenate([grad_scores * query_rows, weights * grad_mixture_rows, grad_gate], axis=1)
    grad_query = total_of(grad_scores * key) * SCALE
    grad_mean = dot_t(grad_query, w_query)
    grad_normed = present_rows * spread(grad_mean / counted) + dot_t(grad_rest, w_rest)
    grad_query_weights = dot_rows(mean_unit, grad_query) * (1.0 / n_seq)
    grad_rest_weights = dot_rows(unit, grad_rest)
    fold_row = lax.broadcasted_iota(jnp.int32, (2 * C, 2 * DH), 0)
    fold_lane = lax.broadcasted_iota(jnp.int32, (2 * C, 2 * DH), 1)
    fold = ((fold_row // C == fold_lane // DH) & (fold_row % DH == fold_lane % DH)).astype(F32)
    grad_key_value = dot(grad_rest_weights[:, : 2 * C], fold)
    first = jnp.concatenate([grad_query_weights, grad_rest_weights[:, 2 * C :]], axis=1)
    second = jnp.concatenate([out_grad, grad_key_value, jnp.zeros((C, C - 2 * DH), F32)], axis=1)
    grad_middle = (cot + normalise_back(grad_normed, gain, unit, inverse)).reshape(n_src, group, C)
    for src in range(n_src):
        for s in range(n_seq):
            returned[src, 0, :, s * C : (s + 1) * C] = grad_middle[src, s * block : (s + 1) * block, :]
        returned[src, 1] = first[src * share : (src + 1) * share, :]
        returned[src, 2] = second[src * share : (src + 1) * share, :]


def row_backward(n_res, returned, exponent_in, unit_in, memory_in, query_gate_in, query_heads_in, mixture_in, inverse_in,
                 own_unit_in, w_row, w_out, bias_out, middle_grad, *refs):
    sums_out, shares = refs[:n_res], refs[n_res]
    me = lax.axis_index("res")
    n_seq, n_rows, _ = middle_grad.shape
    n_keys = n_res * n_rows
    n_blocks, _, block, _ = returned.shape
    w_all = w_row[...]
    w_memory = w_all[:, C : 3 * C]
    w_query_gate = jnp.concatenate([w_all[:, :C], w_all[:, 3 * C :]], axis=1)
    mask = head_mask(n_rows)
    for b in range(n_blocks):
        for s in range(n_seq):
            middle_grad[s, b * block : (b + 1) * block, :] = returned[b, 0, :, s * C : (s + 1) * C]
    grad_middle = middle_grad[...].reshape(n_seq * n_rows, C)
    queries_gates = query_gate_in[...].reshape(n_seq * n_rows, 2 * C)
    gates = queries_gates[:, C:]
    mixtures = mixture_in[...].reshape(n_seq * n_rows, C)
    grad_gated = dot_t(grad_middle, w_out[...])
    grad_out = dot_rows(gates * mixtures, grad_middle)
    grad_gates = grad_gated * mixtures * gates * (1.0 - gates)
    grad_mixtures = grad_gated * gates * inverse_in[...].reshape(n_seq * n_rows, C)
    inners = grad_mixtures * mixtures
    bias_grad = jnp.zeros((n_keys, H * n_rows), F32)
    grad_queries = []
    grad_memories = []
    for s in range(n_seq):
        rows = slice(s * n_rows, (s + 1) * n_rows)
        memory = memory_in[:, s].reshape(n_keys, 2 * C)
        exponent = exponent_in[s]
        grad_heads = spread_heads(grad_mixtures[rows], mask)
        right = jnp.concatenate([grad_heads, spread_heads(inners[rows], mask)], axis=0)
        left = jnp.concatenate([memory[:, C:], jnp.full((n_keys, C), -1.0, F32)], axis=1)
        grad_scores = exponent * dot(left, right)
        bias_grad = bias_grad + grad_scores
        grad_queries.append(join_heads(dot_rows(memory[:, :C], grad_scores), mask) * SCALE)
        grad_key = dot_t(grad_scores, query_heads_in[s])
        grad_value = dot_t(exponent, grad_heads)
        grad_memories.append(jnp.concatenate([grad_key, grad_value], axis=1))
    grad_query_gate = jnp.concatenate([jnp.concatenate(grad_queries, axis=0), grad_gates], axis=1)
    grad_memory = jnp.concatenate(grad_memories, axis=0)
    grad_query_gate_weights = dot_rows(own_unit_in[...].reshape(n_seq * n_rows, C), grad_query_gate)
    units = jnp.concatenate([unit_in[:, s].reshape(n_keys, C) for s in range(n_seq)], axis=0)
    grad_memory_weights = dot_rows(units, grad_memory)
    from_memory = dot_t(grad_memory, w_memory)
    from_own = dot_t(grad_query_gate, w_query_gate)
    from_memory = [from_memory[s * n_keys : (s + 1) * n_keys] for s in range(n_seq)]
    from_own = [from_own[s * n_rows : (s + 1) * n_rows] for s in range(n_seq)]
    bias_out[...] = bias_grad
    half = C // 2
    weight_grads = jnp.concatenate(
        [grad_query_gate_weights, grad_memory_weights, jnp.concatenate([grad_out[:half], grad_out[half:]], axis=1)],
        axis=0,
    )
    part = shares.shape[1] - ROWS - n_rows
    shares[...] = jnp.zeros(shares.shape, F32)
    share = C // n_blocks
    column = jnp.sum(returned[:, 1:, :, :], axis=0)
    normed = jnp.concatenate(from_memory, axis=1)
    for i in range(n_res):
        rows = min(part, max(0, weight_grads.shape[0] - i * part))
        if rows:
            shares[i, :rows, :] = weight_grads[i * part : i * part + rows, :]
        shares[i, part : part + share, :] = column[0]
        shares[i, part + share : part + 2 * share, :] = column[1]
        shares[i, part + ROWS :, :] = normed[i * n_rows : (i + 1) * n_rows, :]
    for away in range(n_res):
        sums_out[away][...] = shares[lax.rem(me + away, n_res)]
    sums_out[0][part + ROWS :, :] += jnp.concatenate(from_own, axis=1)


def step_bits(n_seq_devices, odd):
    bits = list(range(n_seq_devices.bit_length() - 1))
    if odd:
        for i in range(0, len(bits) - 1, 2):
            bits[i], bits[i + 1] = bits[i + 1], bits[i]
    return bits


def relative_block(mask_of_bits, n_blocks):
    odd = lax.rem(lax.axis_index("res"), 2)
    even_mask = mask_of_bits(step_bits(n_blocks, False))
    odd_mask = mask_of_bits(step_bits(n_blocks, True))
    return lax.axis_index("seq") ^ (even_mask + odd * (odd_mask - even_mask))


def split_blocks(bias_t, state, send):
    tiles = bias_t.shape[1] // LANES
    n_blocks = (state.shape[0] + send.shape[0]) // tiles
    keys_each = bias_t.shape[0] // n_blocks
    half = n_blocks // 2

    for slot in range(n_blocks):

        def mask_of_bits(bits):
            last = len(bits) - 1
            return sum(1 << bit for at, bit in enumerate(bits) if slot >> (last - at) & 1)

        block = relative_block(mask_of_bits, n_blocks)
        values = bias_t[pl.ds(pl.multiple_of(block * keys_each, keys_each), keys_each), :]
        for i in range(tiles):
            out, at = (state, slot) if slot < half else (send, slot - half)
            out[at * tiles + i] = values[:, i * LANES : (i + 1) * LANES]


def bias_last(state, arrived, bias_out):
    heads, _, n_rows = bias_out.shape
    each = LANES // n_rows
    for i in range(state.shape[0]):
        total = state[i] + arrived[i]
        for e in range(each):
            bias_out[i * each + e] = total[:, e * n_rows : (e + 1) * n_rows]


def add_shares(bias_send, *refs):
    sums, send, normed = refs[:-2], refs[-2], refs[-1]
    total = sums[0][...]
    for more in sums[1:]:
        total = total + more[...]
    left = bias_send.shape[0]
    rows = total.shape[0] - normed.shape[0]
    send[:left] = bias_send[...]
    send[left:] = total[:rows].reshape(rows // ROWS, ROWS, LANES)
    normed[...] = total[rows:]


def step(part, state, sent, arrived, state_out, send):
    left = state.shape[0]
    half = left // 2
    total = state[...] + arrived[:left]
    state_out[...] = total[:half]
    send[:half] = total[half:]
    send[half : half + part] = sent[left : left + part] + arrived[left : left + part]
    pieces = sent.shape[0] - left - part
    send[half + part : half + part + pieces] = sent[left + part :]
    send[half + part + pieces :] = arrived[left + part :]


def last_step(sent, arrived, _, shared, joined):
    part = shared.shape[0]
    pieces = joined.shape[0] // 2
    left = sent.shape[0] - part - pieces
    shared[...] = sent[left : left + part] + arrived[left : left + part]
    joined[:pieces] = sent[left + part :]
    joined[pieces:] = arrived[left + part :]


def finish_alignment(own, middle_grad, gains, normed, out, done):
    n_seq = own.shape[0]
    done[...] = jnp.zeros(done.shape, F32)
    for s in range(n_seq):
        unit, inverse = normalise(own[s].astype(F32))
        grad_normed = normed[:, s * C : (s + 1) * C]
        out[s] = (middle_grad[s] + normalise_back(grad_normed, gains[0:1, :], unit, inverse)).astype(out.dtype)


def unpack(n_res, joined, *refs):
    parts = refs[:n_res]
    gains, w_row, w_col, gains_out, row_project_out, row_out_out, col_project_out, col_out_out = refs[n_res : n_res + 8]
    shares, column = refs[n_res + 8 :]
    me = lax.axis_index("res")
    part = shares.shape[1]
    for away in range(n_res):
        shares[lax.rem(me + away, n_res)] = parts[away][...].reshape(part, LANES)
    n_blocks, _, share, _ = column.shape
    for slot in range(n_blocks):
        block = relative_block(
            lambda bits: sum(1 << bit for at, bit in enumerate(bits) if slot >> at & 1), n_blocks
        )
        piece = joined[slot]
        column[block, 0] = piece[:share]
        column[block, 1] = piece[share : 2 * share]
    flat = jnp.concatenate([shares[i] for i in range(n_res)], axis=0)
    query_gate, memory, outs = flat[:C], flat[C : 2 * C], flat[2 * C : 2 * C + C // 2]
    col_query_gate = jnp.concatenate([column[i, 0] for i in range(n_blocks)], axis=0)
    col_rest = jnp.concatenate([column[i, 1] for i in range(n_blocks)], axis=0)
    rest = col_rest[:, C : C + 2 * DH]
    gain_row = to_column(gains[0:1, :])
    gain_col = to_column(gains[1:2, :])
    w_all = w_row[...]
    w_column = w_col[...]
    row_gain_grad = (
        jnp.sum(query_gate[:, :C] * w_all[:, :C], axis=1, keepdims=True)
        + jnp.sum(memory * w_all[:, C : 3 * C], axis=1, keepdims=True)
        + jnp.sum(query_gate[:, C:] * w_all[:, 3 * C :], axis=1, keepdims=True)
    )
    col_gain_grad = (
        jnp.sum(col_query_gate[:, :C] * w_column[:, :C], axis=1, keepdims=True)
        + jnp.sum(rest * w_column[:, C : C + 2 * DH], axis=1, keepdims=True)
        + jnp.sum(col_query_gate[:, C:] * w_column[:, C + 2 * DH :], axis=1, keepdims=True)
    )
    gains_out[0:1, :] = to_row(row_gain_grad)
    gains_out[1:2, :] = to_row(col_gain_grad)
    row_project_out[:, :C] = query_gate[:, :C] * gain_row
    row_project_out[:, C : 3 * C] = memory * gain_row
    row_project_out[:, 3 * C :] = query_gate[:, C:] * gain_row
    col_project_out[:, :C] = col_query_gate[:, :C] * gain_col
    col_project_out[:, C : C + 2 * DH] = rest * gain_col
    col_project_out[:, C + 2 * DH :] = col_query_gate[:, C:] * gain_col
    half = C // 2
    row_out_out[:half, :] = outs[:, :C]
    row_out_out[half:, :] = outs[:, C:]
    col_out_out[...] = col_rest[:, :C]


def call(body, outs, *operands, smem=0, unread=0, scratch=(), name):
    vmem = pl.BlockSpec(memory_space=pltpu.VMEM)
    scalar = pl.BlockSpec(memory_space=pltpu.SMEM)
    return pl.pallas_call(
        body,
        out_shape=[jax.ShapeDtypeStruct(shape, kind) for shape, kind in outs],
        in_specs=[scalar] * smem + [vmem] * (len(operands) - smem - unread)
        + [pl.BlockSpec(memory_space=pl.ANY)] * unread,
        out_specs=[vmem] * len(outs),
        scratch_shapes=list(scratch),
        compiler_params=pltpu.CompilerParams(vmem_limit_bytes=32 * 1024 * 1024),
        name=name,
    )(*operands)


def shift_residues(values, away, count):
    return lax.ppermute(values, "res", [((i + away) % count, i) for i in range(count)])


def cross(values, at, seq_count, res_count):
    pairs = []
    for r in range(res_count):
        bit = 1 << step_bits(seq_count, r % 2)[at]
        pairs += [(i * res_count + r, (i ^ bit) * res_count + r) for i in range(seq_count)]
    return lax.ppermute(values, ("seq", "res"), pairs)


def swap_blocks(values):
    return lax.all_to_all(values, "seq", 0, 0, tiled=True)


def local(
    alignment,
    cotangent,
    pair_bias,
    norm_gains,
    row_project,
    row_output,
    column_project,
    column_output,
    residue_mask,
    sequence_mask,
    seq_count,
    res_count,
):
    n_seq, n_rows, _ = alignment.shape
    n_keys = pair_bias.shape[2]
    block = n_rows // seq_count
    group = n_seq * block
    away_range = range(1, res_count)
    present_keys = jnp.broadcast_to(residue_mask.astype(F32)[None, :, None], (1, n_rows, C))
    sent = jnp.concatenate([alignment.astype(F32), present_keys], axis=0)
    own_unit, query_gate, query_heads, own_memory, present = call(
        own_half,
        [
            ((n_seq, n_rows, C), F32),
            ((n_seq, n_rows, 2 * C), F32),
            ((n_seq, C, H * n_rows), F32),
            ((n_seq, n_rows, 2 * C), F32),
            ((block, 2 * C), F32),
        ],
        sequence_mask, alignment, norm_gains, row_project,
        smem=1,
        name="own_half",
    )
    payload, exponent, unit, memory, mixture, inverse = call(
        functools.partial(row_forward, res_count),
        [
            ((seq_count, n_seq + 1, block, 2 * C), F32),
            ((n_seq, n_keys, H * n_rows), F32),
            ((res_count, n_seq, n_rows, C), F32),
            ((res_count, n_seq, n_rows, 2 * C), F32),
            ((n_seq, n_rows, C), F32),
            ((n_seq, n_rows, C), F32),
        ],
        sent, *[shift_residues(sent, away, res_count) for away in away_range],
        alignment, cotangent, norm_gains, row_project, row_output, own_unit, query_gate, query_heads, own_memory, pair_bias,
        present,
        scratch=[pltpu.VMEM((res_count, n_rows, C), F32)],
        name="row_forward",
    )
    arrived = swap_blocks(payload)
    (returned,) = call(
        functools.partial(column_step, n_seq=n_seq),
        [((seq_count, 3, block, 2 * C), F32)],
        arrived, norm_gains, column_project, column_output,
        scratch=[pltpu.VMEM((seq_count, group, 2 * C), F32), pltpu.VMEM((seq_count, group, C), F32)],
        name="column_step",
    )
    returned = swap_blocks(returned)
    part = -(-5 * C // (2 * ROWS * res_count)) * ROWS
    keys_each = n_keys // seq_count
    tiles = H * n_rows // LANES
    left = seq_count // 2 * tiles
    bias_grad, middle_grad, *sums = call(
        functools.partial(row_backward, res_count),
        [((n_keys, H * n_rows), F32), ((n_seq, n_rows, C), F32)]
        + [((part + ROWS + n_rows, LANES), F32)] * res_count,
        returned, exponent, unit, memory, query_gate, query_heads, mixture, inverse, own_unit, row_project, row_output,
        scratch=[pltpu.VMEM((res_count, part + ROWS + n_rows, LANES), F32)],
        name="row_backward",
    )
    sums = sums[:1] + [shift_residues(sums[away], -away, res_count) for away in away_range]
    state, send = call(
        split_blocks, [((left, keys_each, LANES), F32)] * 2, bias_grad, name="split_blocks"
    )
    part_tiles = part // ROWS
    send, normed = call(
        add_shares,
        [((left + part_tiles + 1, ROWS, LANES), F32), ((n_rows, LANES), F32)],
        send, *sums,
        name="add_shares",
    )
    grad_alignment, done = call(
        finish_alignment,
        [(alignment.shape, alignment.dtype), ((ROWS, LANES), F32)],
        alignment, middle_grad, norm_gains, normed,
        name="finish_alignment",
    )
    steps = seq_count.bit_length() - 1
    for at in range(steps):
        arrived = cross(send, at, seq_count, res_count)
        if at < steps - 1:
            left //= 2
            state, send = call(
                functools.partial(step, part_tiles),
                [((left, ROWS, LANES), F32), ((left + part_tiles + (2 << at), ROWS, LANES), F32)],
                state, send, arrived,
                name="step",
            )
    shared, joined = call(
        last_step,
        [((part_tiles, ROWS, LANES), F32), ((seq_count, ROWS, LANES), F32)],
        send, arrived, done,
        unread=1,
        name="last_step",
    )
    (bias_grad,) = call(bias_last, [((H, keys_each, n_rows), F32)], state, arrived, name="bias_last")
    grads = call(
        functools.partial(unpack, res_count),
        [((2, C), F32), ((C, 4 * C), F32), ((C, C), F32), ((C, 2 * C + 2 * DH), F32), ((C, C), F32)],
        joined, shared, *[shift_residues(shared, away, res_count) for away in away_range],
        norm_gains, row_project, column_project,
        scratch=[
            pltpu.VMEM((res_count, part, LANES), F32),
            pltpu.VMEM((seq_count, 2, C // seq_count, LANES), F32),
        ],
        name="unpack",
    )
    return (grad_alignment, jnp.transpose(bias_grad, (0, 2, 1)), *grads)


def solution(mesh):
    placed = (
        P("seq", "res", None),
        P("seq", "res", None),
        P(None, "res", None),
        P(),
        P(),
        P(),
        P(),
        P(),
        P("res"),
        P("seq"),
    )
    return jax.shard_map(
        functools.partial(local, seq_count=mesh.shape["seq"], res_count=mesh.shape["res"]),
        mesh=mesh,
        in_specs=placed,
        out_specs=(P("seq", "res", None), P(None, "res", "seq"), P(), P(), P(), P(), P()),
        check_vma=False,
    )
```

```python
import functools

import jax
import jax.numpy as jnp
from jax import lax
from jax.experimental import pallas as pl
from jax.experimental.pallas import tpu as pltpu
from jax.sharding import PartitionSpec as P

C = 64
H = 8
DH = 8
LANES = 128
ROWS = 8

EXACT = lax.Precision.HIGHEST
THREE = lax.Precision.HIGH
EPSILON = 1e-05
MASKED = 1000000000.0
SCALE = DH ** (-0.5)
F32 = jnp.float32


def dot(a, b, over=((1,), (0,)), precision=THREE):
    return lax.dot_general(a, b, (over, ((), ())), precision=precision, preferred_element_type=F32)


def dot_rows(a, b):
    return dot(a, b, ((0,), (0,)))


def dot_t(a, b, precision=THREE):
    return dot(a, b, ((1,), (1,)), precision)


def to_column(row):
    eye = lax.broadcasted_iota(jnp.int32, (C, C), 0) == lax.broadcasted_iota(jnp.int32, (C, C), 1)
    return jnp.sum(jnp.where(eye, row, 0.0), axis=1, keepdims=True)


def to_row(column):
    eye = lax.broadcasted_iota(jnp.int32, (C, C), 0) == lax.broadcasted_iota(jnp.int32, (C, C), 1)
    return jnp.sum(jnp.where(eye, column, 0.0), axis=0, keepdims=True)


def normalise(values):
    centred = values - jnp.mean(values, axis=-1, keepdims=True)
    inverse = lax.rsqrt(jnp.mean(centred * centred, axis=-1, keepdims=True) + EPSILON)
    return centred * inverse, inverse


def normalise_back(grad_normed, gain, unit, inverse):
    grad_unit = grad_normed * gain
    along = jnp.mean(grad_unit * unit, axis=-1, keepdims=True)
    return inverse * (grad_unit - jnp.mean(grad_unit, axis=-1, keepdims=True) - unit * along)


def head_mask(rows):
    channel = lax.broadcasted_iota(jnp.int32, (C, H * rows), 0)
    lane = lax.broadcasted_iota(jnp.int32, (C, H * rows), 1)
    return (lane // rows == channel // DH).astype(F32)


def spread_heads(values, mask):
    rows = values.shape[0]
    turned = jnp.transpose(values)
    turned = jnp.concatenate([turned] * (LANES // rows), axis=1)
    return jnp.concatenate([turned] * (H * rows // LANES), axis=1) * mask


def join_heads(values, mask):
    masked = values * mask
    rows = mask.shape[1] // H
    total = masked[:, :LANES]
    for i in range(1, H * rows // LANES):
        total = total + masked[:, i * LANES : (i + 1) * LANES]
    joined = total[:, :rows]
    for i in range(1, LANES // rows):
        joined = joined + total[:, i * rows : (i + 1) * rows]
    return jnp.transpose(joined)


def own_half(seq_mask, own, gains, w_row,
             own_unit_out, query_gate_out, query_heads_out, own_memory_out, present_out):
    n_seq, n_rows, _ = own.shape
    w_all = w_row[...]
    own_units, _ = normalise(own[...].reshape(n_seq * n_rows, C).astype(F32))
    projected = dot(own_units * gains[0:1, :], w_all, precision=EXACT)
    queries = projected[:, :C] * SCALE
    gates = jax.nn.sigmoid(projected[:, 3 * C :])
    own_unit_out[...] = own_units.reshape(n_seq, n_rows, C)
    query_gate_out[...] = jnp.concatenate([queries, gates], axis=1).reshape(n_seq, n_rows, 2 * C)
    own_memory_out[...] = projected[:, C : 3 * C].reshape(n_seq, n_rows, 2 * C)
    mask = head_mask(n_rows)
    for s in range(n_seq):
        query_heads_out[s] = spread_heads(queries[s * n_rows : (s + 1) * n_rows], mask)
    lane = lax.broadcasted_iota(jnp.int32, present_out.shape, 1) // (2 * C // n_seq)
    present = jnp.zeros(present_out.shape, F32)
    for s in range(n_seq):
        present = jnp.where(lane == s, seq_mask[s].astype(F32), present)
    present_out[...] = present


def row_forward(n_res, *refs):
    sent = refs[:n_res]
    (own, cotangent, gains, w_row, w_out, own_unit, query_gate, query_heads, own_memory, bias, present) = refs[
        n_res : n_res + 11
    ]
    payload, exponent_out, unit_out, memory_out, mixture_out, inverse_out, residue = refs[n_res + 11 :]
    n_seq, n_rows, _ = own.shape
    n_keys = n_res * n_rows
    me = lax.axis_index("res")
    w_memory = w_row[:, C : 3 * C]
    for away in range(n_res):
        where = lax.rem(me + away, n_res)
        residue[where] = sent[away][n_seq]
        if away:
            units, _ = normalise(sent[away][:n_seq].reshape(n_seq * n_rows, C))
            memories = dot(units * gains[0:1, :], w_memory, precision=EXACT)
            units = units.reshape(n_seq, n_rows, C)
            memories = memories.reshape(n_seq, n_rows, 2 * C)
        else:
            units, memories = own_unit[...], own_memory[...]
        unit_out[where] = units
        memory_out[where] = memories
    n_blocks = payload.shape[0]
    block = n_rows // n_blocks
    bias_t = jnp.transpose(bias[...].reshape(H * n_rows, n_keys).astype(F32))
    key_bias = MASKED * (residue[...].reshape(n_keys, C)[:, 0:1] - 1.0)
    mask = head_mask(n_rows)
    wide_mask = jnp.concatenate([mask, mask], axis=0)
    initial = own[...].reshape(n_seq * n_rows, C).astype(F32)
    gates = query_gate[...].reshape(n_seq * n_rows, 2 * C)[:, C:]
    sums = []
    for s in range(n_seq):
        memory = memory_out[:, s].reshape(n_keys, 2 * C)
        scores = dot(memory[:, :C], query_heads[s], precision=EXACT) + bias_t + key_bias
        exponent = jnp.exp(scores - jnp.max(scores, axis=0, keepdims=True))
        exponent_out[s] = exponent
        summed = dot_rows(jnp.concatenate([memory[:, C:], jnp.ones((n_keys, C), F32)], axis=1), exponent)
        sums.append(join_heads(summed, wide_mask))
    summed = jnp.concatenate(sums, axis=0)
    inverse = 1.0 / summed[:, C:]
    mixture = summed[:, :C] * inverse
    inverse_out[...] = inverse.reshape(n_seq, n_rows, C)
    mixture_out[...] = mixture.reshape(n_seq, n_rows, C)
    middle = initial + dot(gates * mixture, w_out[...])
    both = jnp.concatenate([middle, cotangent[...].reshape(n_seq * n_rows, C).astype(F32)], axis=1)
    for s in range(n_seq):
        for b in range(n_blocks):
            row = s * n_rows + b * block
            payload[b, s] = both[row : row + block, :]
    for b in range(n_blocks):
        payload[b, n_seq] = present[...]


def column_step(arrived, gains, w_col, w_out, returned, gathered, mask_rows, n_seq):
    n_src, _, block, _ = arrived.shape
    group = n_seq * block
    rows = n_src * group
    wide = 2 * C // n_seq
    share = C // n_src
    for src in range(n_src):
        for s in range(n_seq):
            gathered[src, s * block : (s + 1) * block, :] = arrived[src, s]
            mask_rows[src, s * block : (s + 1) * block, :] = jnp.broadcast_to(
                arrived[src, n_seq, :, s * wide : s * wide + 1], (block, C)
            )
    data = gathered[...].reshape(rows, 2 * C)
    present = mask_rows[...]
    middle = data[:, :C]
    cot = data[:, C:]
    gain = gains[1:2, :]

    def over_sequences(values, combine, reduce):
        total = reduce(values.reshape(n_src, group, C), axis=0)
        result = total
        for shift in range(1, n_seq):
            result = combine(result, pltpu.roll(total, shift * block, 0))
        return result

    def total_of(values):
        return over_sequences(values, jnp.add, jnp.sum)

    def spread(values):
        return jnp.broadcast_to(values[None], (n_src, group, C)).reshape(rows, C)

    lane = lax.broadcasted_iota(jnp.int32, (C, C), 1)
    row = lax.broadcasted_iota(jnp.int32, (C, C), 0)
    same_head = (row // DH == lane // DH).astype(F32)
    repeat = (lax.broadcasted_iota(jnp.int32, (DH, C), 0) == lax.broadcasted_iota(jnp.int32, (DH, C), 1) % DH).astype(F32)
    w_all = w_col[...]
    w_query = w_all[:, :C]
    w_key = dot(w_all[:, C : C + DH], repeat, precision=EXACT)
    w_value = dot(w_all[:, C + DH : C + 2 * DH], repeat)
    w_gate = w_all[:, C + 2 * DH :]
    w_rest = jnp.concatenate([w_key, w_value, w_gate], axis=1)

    unit, inverse = normalise(middle)
    normed = unit * gain
    present_rows = present.reshape(rows, C)
    counted = total_of(present_rows)
    mean_unit = total_of(present_rows * unit) / counted
    mean_normed = mean_unit * gain
    query = dot(mean_normed, w_query, precision=EXACT) * SCALE
    query_rows = spread(query)
    rest = dot(normed, w_rest, precision=EXACT)
    key, value = rest[:, :C], rest[:, C : 2 * C]
    gate = jax.nn.sigmoid(rest[:, 2 * C :])
    scores = dot(query_rows * key, same_head, precision=EXACT) + MASKED * (present_rows - 1.0)
    peak = over_sequences(scores, jnp.maximum, jnp.max)
    exponent = jnp.exp(scores - spread(peak))
    weights = exponent / spread(total_of(exponent))
    mixture = total_of(weights * value)
    mixture_rows = spread(mixture)

    grad_gated = dot_t(cot, w_out[...])
    out_grad = dot_rows(gate * mixture_rows, cot)
    grad_mixture = total_of(gate * grad_gated)
    grad_mixture_rows = spread(grad_mixture)
    grad_gate = grad_gated * mixture_rows * gate * (1.0 - gate)
    grad_weights = dot(grad_mixture_rows * value, same_head)
    inner = spread(dot(grad_mixture * mixture, same_head))
    grad_scores = weights * (grad_weights - inner)
    grad_rest = jnp.concatenate([grad_scores * query_rows, weights * grad_mixture_rows, grad_gate], axis=1)
    grad_query = total_of(grad_scores * key) * SCALE
    grad_mean = dot_t(grad_query, w_query)
    grad_normed = present_rows * spread(grad_mean / counted) + dot_t(grad_rest, w_rest)
    grad_query_weights = dot_rows(mean_unit, grad_query) * (1.0 / n_seq)
    grad_rest_weights = dot_rows(unit, grad_rest)
    fold_row = lax.broadcasted_iota(jnp.int32, (2 * C, 2 * DH), 0)
    fold_lane = lax.broadcasted_iota(jnp.int32, (2 * C, 2 * DH), 1)
    fold = ((fold_row // C == fold_lane // DH) & (fold_row % DH == fold_lane % DH)).astype(F32)
    grad_key_value = dot(grad_rest_weights[:, : 2 * C], fold)
    first = jnp.concatenate([grad_query_weights, grad_rest_weights[:, 2 * C :]], axis=1)
    second = jnp.concatenate([out_grad, grad_key_value, jnp.zeros((C, C - 2 * DH), F32)], axis=1)
    grad_middle = (cot + normalise_back(grad_normed, gain, unit, inverse)).reshape(n_src, group, C)
    for src in range(n_src):
        for s in range(n_seq):
            returned[src, 0, :, s * C : (s + 1) * C] = grad_middle[src, s * block : (s + 1) * block, :]
        returned[src, 1] = first[src * share : (src + 1) * share, :]
        returned[src, 2] = second[src * share : (src + 1) * share, :]


def row_backward(n_res, returned, exponent_in, unit_in, memory_in, query_gate_in, query_heads_in, mixture_in, inverse_in,
                 own_unit_in, w_row, w_out, bias_out, middle_grad, *refs):
    sums_out, shares = refs[:n_res], refs[n_res]
    me = lax.axis_index("res")
    n_seq, n_rows, _ = middle_grad.shape
    n_keys = n_res * n_rows
    n_blocks, _, block, _ = returned.shape
    w_all = w_row[...]
    w_memory = w_all[:, C : 3 * C]
    w_query_gate = jnp.concatenate([w_all[:, :C], w_all[:, 3 * C :]], axis=1)
    mask = head_mask(n_rows)
    for b in range(n_blocks):
        for s in range(n_seq):
            middle_grad[s, b * block : (b + 1) * block, :] = returned[b, 0, :, s * C : (s + 1) * C]
    grad_middle = middle_grad[...].reshape(n_seq * n_rows, C)
    queries_gates = query_gate_in[...].reshape(n_seq * n_rows, 2 * C)
    gates = queries_gates[:, C:]
    mixtures = mixture_in[...].reshape(n_seq * n_rows, C)
    grad_gated = dot_t(grad_middle, w_out[...])
    grad_out = dot_rows(gates * mixtures, grad_middle)
    grad_gates = grad_gated * mixtures * gates * (1.0 - gates)
    grad_mixtures = grad_gated * gates * inverse_in[...].reshape(n_seq * n_rows, C)
    inners = grad_mixtures * mixtures
    bias_grad = jnp.zeros((n_keys, H * n_rows), F32)
    grad_queries = []
    grad_memories = []
    for s in range(n_seq):
        rows = slice(s * n_rows, (s + 1) * n_rows)
        memory = memory_in[:, s].reshape(n_keys, 2 * C)
        exponent = exponent_in[s]
        grad_heads = spread_heads(grad_mixtures[rows], mask)
        right = jnp.concatenate([grad_heads, spread_heads(inners[rows], mask)], axis=0)
        left = jnp.concatenate([memory[:, C:], jnp.full((n_keys, C), -1.0, F32)], axis=1)
        grad_scores = exponent * dot(left, right)
        bias_grad = bias_grad + grad_scores
        grad_queries.append(join_heads(dot_rows(memory[:, :C], grad_scores), mask) * SCALE)
        grad_key = dot_t(grad_scores, query_heads_in[s])
        grad_value = dot_t(exponent, grad_heads)
        grad_memories.append(jnp.concatenate([grad_key, grad_value], axis=1))
    grad_query_gate = jnp.concatenate([jnp.concatenate(grad_queries, axis=0), grad_gates], axis=1)
    grad_memory = jnp.concatenate(grad_memories, axis=0)
    grad_query_gate_weights = dot_rows(own_unit_in[...].reshape(n_seq * n_rows, C), grad_query_gate)
    units = jnp.concatenate([unit_in[:, s].reshape(n_keys, C) for s in range(n_seq)], axis=0)
    grad_memory_weights = dot_rows(units, grad_memory)
    from_memory = dot_t(grad_memory, w_memory)
    from_own = dot_t(grad_query_gate, w_query_gate)
    from_memory = [from_memory[s * n_keys : (s + 1) * n_keys] for s in range(n_seq)]
    from_own = [from_own[s * n_rows : (s + 1) * n_rows] for s in range(n_seq)]
    bias_out[...] = bias_grad
    half = C // 2
    weight_grads = jnp.concatenate(
        [grad_query_gate_weights, grad_memory_weights, jnp.concatenate([grad_out[:half], grad_out[half:]], axis=1)],
        axis=0,
    )
    part = shares.shape[1] - ROWS - n_rows
    shares[...] = jnp.zeros(shares.shape, F32)
    share = C // n_blocks
    column = jnp.sum(returned[:, 1:, :, :], axis=0)
    normed = jnp.concatenate(from_memory, axis=1)
    for i in range(n_res):
        rows = min(part, max(0, weight_grads.shape[0] - i * part))
        if rows:
            shares[i, :rows, :] = weight_grads[i * part : i * part + rows, :]
        shares[i, part : part + share, :] = column[0]
        shares[i, part + ROWS // 2 : part + ROWS // 2 + share, :] = column[1]
        shares[i, part + ROWS :, :] = normed[i * n_rows : (i + 1) * n_rows, :]
    for away in range(n_res):
        sums_out[away][...] = shares[lax.rem(me + away, n_res)]
    sums_out[0][part + ROWS :, :] += jnp.concatenate(from_own, axis=1)


def step_bits(n_seq_devices, odd):
    bits = list(range(n_seq_devices.bit_length() - 1))
    if odd:
        for i in range(0, len(bits) - 1, 2):
            bits[i], bits[i + 1] = bits[i + 1], bits[i]
    return bits


def relative_block(mask_of_bits, n_blocks):
    odd = lax.rem(lax.axis_index("res"), 2)
    even_mask = mask_of_bits(step_bits(n_blocks, False))
    odd_mask = mask_of_bits(step_bits(n_blocks, True))
    return lax.axis_index("seq") ^ (even_mask + odd * (odd_mask - even_mask))


def split_blocks(bias_t, state, send):
    tiles = bias_t.shape[1] // LANES
    n_blocks = (state.shape[0] + send.shape[0]) // tiles
    keys_each = bias_t.shape[0] // n_blocks
    half = n_blocks // 2

    for slot in range(n_blocks):

        def mask_of_bits(bits):
            last = len(bits) - 1
            return sum(1 << bit for at, bit in enumerate(bits) if slot >> (last - at) & 1)

        block = relative_block(mask_of_bits, n_blocks)
        values = bias_t[pl.ds(pl.multiple_of(block * keys_each, keys_each), keys_each), :]
        for i in range(tiles):
            out, at = (state, slot) if slot < half else (send, slot - half)
            out[at * tiles + i] = values[:, i * LANES : (i + 1) * LANES]


def bias_last(state, arrived, bias_out):
    heads, _, n_rows = bias_out.shape
    each = LANES // n_rows
    for i in range(state.shape[0]):
        total = state[i] + arrived[i]
        for e in range(each):
            bias_out[i * each + e] = total[:, e * n_rows : (e + 1) * n_rows]


def add_shares(bias_send, *refs):
    sums, send, normed = refs[:-2], refs[-2], refs[-1]
    total = sums[0][...]
    for more in sums[1:]:
        total = total + more[...]
    left = bias_send.shape[0]
    rows = total.shape[0] - normed.shape[0]
    send[:left] = bias_send[...]
    send[left : send.shape[0] - 1] = total[: rows - ROWS].reshape(rows // ROWS - 1, ROWS, LANES)
    piece = total[rows - ROWS : rows]
    odd = lax.rem(lax.axis_index("res"), 2)
    send[send.shape[0] - 1] = jnp.where(odd == 1, pltpu.roll(piece, ROWS // 2, 0), piece)
    normed[...] = total[rows:]


def step(part, first, state, sent, arrived, state_out, send):
    left = state.shape[0]
    half = left // 2
    total = state[...] + arrived[:left]
    state_out[...] = total[:half]
    send[:half] = total[half:]
    send[half : half + part] = sent[left : left + part] + arrived[left : left + part]
    at = half + part
    if first:
        half_rows = ROWS // 2
        send[at] = jnp.concatenate([sent[left + part][:half_rows], arrived[left + part][:half_rows]], axis=0)
    else:
        pieces = sent.shape[0] - left - part
        send[at : at + pieces] = sent[left + part :]
        send[at + pieces :] = arrived[left + part :]


def last_step(part, sent, arrived, _, shared):
    pieces = (shared.shape[0] - part) // 2
    left = sent.shape[0] - part - pieces
    shared[:part] = sent[left : left + part] + arrived[left : left + part]
    shared[part : part + pieces] = sent[left + part :]
    shared[part + pieces :] = arrived[left + part :]


def finish_alignment(own, middle_grad, gains, normed, out, done):
    n_seq = own.shape[0]
    done[...] = jnp.zeros(done.shape, F32)
    for s in range(n_seq):
        unit, inverse = normalise(own[s].astype(F32))
        grad_normed = normed[:, s * C : (s + 1) * C]
        out[s] = (middle_grad[s] + normalise_back(grad_normed, gains[0:1, :], unit, inverse)).astype(out.dtype)


def unpack(n_res, *refs):
    parts = refs[:n_res]
    gains, w_row, w_col, gains_out, row_project_out, row_out_out, col_project_out, col_out_out = refs[n_res : n_res + 8]
    shares, column = refs[n_res + 8 :]
    me = lax.axis_index("res")
    for away in range(n_res):
        shares[lax.rem(me + away, n_res)] = parts[away][...]
    n_blocks, _, share, _ = column.shape
    part = shares.shape[1] - n_blocks // 2
    place = lax.axis_index("seq")
    for half in range(2):
        bits = step_bits(n_blocks, half == 1)
        for slot in range(n_blocks):
            block = place ^ sum(1 << bit for at, bit in enumerate(bits) if slot >> at & 1)
            row = slot % 2 * (ROWS // 2)
            column[block, half] = shares[half, part + slot // 2, row : row + share, :]
    flat = jnp.concatenate([shares[i, :part].reshape(part * ROWS, LANES) for i in range(n_res)], axis=0)
    query_gate, memory, outs = flat[:C], flat[C : 2 * C], flat[2 * C : 2 * C + C // 2]
    col_query_gate = jnp.concatenate([column[i, 0] for i in range(n_blocks)], axis=0)
    col_rest = jnp.concatenate([column[i, 1] for i in range(n_blocks)], axis=0)
    rest = col_rest[:, C : C + 2 * DH]
    gain_row = to_column(gains[0:1, :])
    gain_col = to_column(gains[1:2, :])
    w_all = w_row[...]
    w_column = w_col[...]
    row_gain_grad = (
        jnp.sum(query_gate[:, :C] * w_all[:, :C], axis=1, keepdims=True)
        + jnp.sum(memory * w_all[:, C : 3 * C], axis=1, keepdims=True)
        + jnp.sum(query_gate[:, C:] * w_all[:, 3 * C :], axis=1, keepdims=True)
    )
    col_gain_grad = (
        jnp.sum(col_query_gate[:, :C] * w_column[:, :C], axis=1, keepdims=True)
        + jnp.sum(rest * w_column[:, C : C + 2 * DH], axis=1, keepdims=True)
        + jnp.sum(col_query_gate[:, C:] * w_column[:, C + 2 * DH :], axis=1, keepdims=True)
    )
    gains_out[0:1, :] = to_row(row_gain_grad)
    gains_out[1:2, :] = to_row(col_gain_grad)
    row_project_out[:, :C] = query_gate[:, :C] * gain_row
    row_project_out[:, C : 3 * C] = memory * gain_row
    row_project_out[:, 3 * C :] = query_gate[:, C:] * gain_row
    col_project_out[:, :C] = col_query_gate[:, :C] * gain_col
    col_project_out[:, C : C + 2 * DH] = rest * gain_col
    col_project_out[:, C + 2 * DH :] = col_query_gate[:, C:] * gain_col
    half = C // 2
    row_out_out[:half, :] = outs[:, :C]
    row_out_out[half:, :] = outs[:, C:]
    col_out_out[...] = col_rest[:, :C]


def call(body, outs, *operands, smem=0, unread=0, scratch=(), name):
    vmem = pl.BlockSpec(memory_space=pltpu.VMEM)
    scalar = pl.BlockSpec(memory_space=pltpu.SMEM)
    return pl.pallas_call(
        body,
        out_shape=[jax.ShapeDtypeStruct(shape, kind) for shape, kind in outs],
        in_specs=[scalar] * smem + [vmem] * (len(operands) - smem - unread)
        + [pl.BlockSpec(memory_space=pl.ANY)] * unread,
        out_specs=[vmem] * len(outs),
        scratch_shapes=list(scratch),
        compiler_params=pltpu.CompilerParams(vmem_limit_bytes=32 * 1024 * 1024),
        name=name,
    )(*operands)


def shift_residues(values, away, count):
    return lax.ppermute(values, "res", [((i + away) % count, i) for i in range(count)])


def cross(values, at, seq_count, res_count):
    pairs = []
    for r in range(res_count):
        bit = 1 << step_bits(seq_count, r % 2)[at]
        pairs += [(i * res_count + r, (i ^ bit) * res_count + r) for i in range(seq_count)]
    return lax.ppermute(values, ("seq", "res"), pairs)


def swap_blocks(values):
    return lax.all_to_all(values, "seq", 0, 0, tiled=True)


def local(
    alignment,
    cotangent,
    pair_bias,
    norm_gains,
    row_project,
    row_output,
    column_project,
    column_output,
    residue_mask,
    sequence_mask,
    seq_count,
    res_count,
):
    n_seq, n_rows, _ = alignment.shape
    n_keys = pair_bias.shape[2]
    block = n_rows // seq_count
    group = n_seq * block
    away_range = range(1, res_count)
    present_keys = jnp.broadcast_to(residue_mask.astype(F32)[None, :, None], (1, n_rows, C))
    sent = jnp.concatenate([alignment.astype(F32), present_keys], axis=0)
    own_unit, query_gate, query_heads, own_memory, present = call(
        own_half,
        [
            ((n_seq, n_rows, C), F32),
            ((n_seq, n_rows, 2 * C), F32),
            ((n_seq, C, H * n_rows), F32),
            ((n_seq, n_rows, 2 * C), F32),
            ((block, 2 * C), F32),
        ],
        sequence_mask, alignment, norm_gains, row_project,
        smem=1,
        name="own_half",
    )
    payload, exponent, unit, memory, mixture, inverse = call(
        functools.partial(row_forward, res_count),
        [
            ((seq_count, n_seq + 1, block, 2 * C), F32),
            ((n_seq, n_keys, H * n_rows), F32),
            ((res_count, n_seq, n_rows, C), F32),
            ((res_count, n_seq, n_rows, 2 * C), F32),
            ((n_seq, n_rows, C), F32),
            ((n_seq, n_rows, C), F32),
        ],
        sent, *[shift_residues(sent, away, res_count) for away in away_range],
        alignment, cotangent, norm_gains, row_project, row_output, own_unit, query_gate, query_heads, own_memory, pair_bias,
        present,
        scratch=[pltpu.VMEM((res_count, n_rows, C), F32)],
        name="row_forward",
    )
    arrived = swap_blocks(payload)
    (returned,) = call(
        functools.partial(column_step, n_seq=n_seq),
        [((seq_count, 3, block, 2 * C), F32)],
        arrived, norm_gains, column_project, column_output,
        scratch=[pltpu.VMEM((seq_count, group, 2 * C), F32), pltpu.VMEM((seq_count, group, C), F32)],
        name="column_step",
    )
    returned = swap_blocks(returned)
    part = -(-5 * C // (2 * ROWS * res_count)) * ROWS
    keys_each = n_keys // seq_count
    tiles = H * n_rows // LANES
    left = seq_count // 2 * tiles
    bias_grad, middle_grad, *sums = call(
        functools.partial(row_backward, res_count),
        [((n_keys, H * n_rows), F32), ((n_seq, n_rows, C), F32)]
        + [((part + ROWS + n_rows, LANES), F32)] * res_count,
        returned, exponent, unit, memory, query_gate, query_heads, mixture, inverse, own_unit, row_project, row_output,
        scratch=[pltpu.VMEM((res_count, part + ROWS + n_rows, LANES), F32)],
        name="row_backward",
    )
    sums = sums[:1] + [shift_residues(sums[away], -away, res_count) for away in away_range]
    state, send = call(
        split_blocks, [((left, keys_each, LANES), F32)] * 2, bias_grad, name="split_blocks"
    )
    part_tiles = part // ROWS
    send, normed = call(
        add_shares,
        [((left + part_tiles + 1, ROWS, LANES), F32), ((n_rows, LANES), F32)],
        send, *sums,
        name="add_shares",
    )
    grad_alignment, done = call(
        finish_alignment,
        [(alignment.shape, alignment.dtype), ((ROWS, LANES), F32)],
        alignment, middle_grad, norm_gains, normed,
        name="finish_alignment",
    )
    steps = seq_count.bit_length() - 1
    for at in range(steps):
        arrived = cross(send, at, seq_count, res_count)
        if at < steps - 1:
            left //= 2
            state, send = call(
                functools.partial(step, part_tiles, at == 0),
                [((left, ROWS, LANES), F32), ((left + part_tiles + (1 << at), ROWS, LANES), F32)],
                state, send, arrived,
                name="step",
            )
    (shared,) = call(
        functools.partial(last_step, part_tiles),
        [((part_tiles + seq_count // 2, ROWS, LANES), F32)],
        send, arrived, done,
        unread=1,
        name="last_step",
    )
    (bias_grad,) = call(bias_last, [((H, keys_each, n_rows), F32)], state, arrived, name="bias_last")
    grads = call(
        functools.partial(unpack, res_count),
        [((2, C), F32), ((C, 4 * C), F32), ((C, C), F32), ((C, 2 * C + 2 * DH), F32), ((C, C), F32)],
        shared, *[shift_residues(shared, away, res_count) for away in away_range],
        norm_gains, row_project, column_project,
        scratch=[
            pltpu.VMEM((res_count, part_tiles + seq_count // 2, ROWS, LANES), F32),
            pltpu.VMEM((seq_count, 2, C // seq_count, LANES), F32),
        ],
        name="unpack",
    )
    return (grad_alignment, jnp.transpose(bias_grad, (0, 2, 1)), *grads)


def solution(mesh):
    placed = (
        P("seq", "res", None),
        P("seq", "res", None),
        P(None, "res", None),
        P(),
        P(),
        P(),
        P(),
        P(),
        P("res"),
        P("seq"),
    )
    return jax.shard_map(
        functools.partial(local, seq_count=mesh.shape["seq"], res_count=mesh.shape["res"]),
        mesh=mesh,
        in_specs=placed,
        out_specs=(P("seq", "res", None), P(None, "res", "seq"), P(), P(), P(), P(), P()),
        check_vma=False,
    )
```

```python
import functools

import jax
import jax.numpy as jnp
from jax import lax
from jax.experimental import pallas as pl
from jax.experimental.pallas import tpu as pltpu
from jax.sharding import PartitionSpec as P

C = 64
H = 8
DH = 8
LANES = 128
ROWS = 8

EXACT = lax.Precision.HIGHEST
THREE = lax.Precision.HIGH
EPSILON = 1e-05
MASKED = 1000000000.0
SCALE = DH ** (-0.5)
F32 = jnp.float32


def dot(a, b, over=((1,), (0,)), precision=THREE):
    return lax.dot_general(a, b, (over, ((), ())), precision=precision, preferred_element_type=F32)


def dot_rows(a, b):
    return dot(a, b, ((0,), (0,)))


def dot_t(a, b, precision=THREE):
    return dot(a, b, ((1,), (1,)), precision)


def to_column(row):
    eye = lax.broadcasted_iota(jnp.int32, (C, C), 0) == lax.broadcasted_iota(jnp.int32, (C, C), 1)
    return jnp.sum(jnp.where(eye, row, 0.0), axis=1, keepdims=True)


def to_row(column):
    eye = lax.broadcasted_iota(jnp.int32, (C, C), 0) == lax.broadcasted_iota(jnp.int32, (C, C), 1)
    return jnp.sum(jnp.where(eye, column, 0.0), axis=0, keepdims=True)


def normalise(values):
    centred = values - jnp.mean(values, axis=-1, keepdims=True)
    inverse = lax.rsqrt(jnp.mean(centred * centred, axis=-1, keepdims=True) + EPSILON)
    return centred * inverse, inverse


def normalise_back(grad_normed, gain, unit, inverse):
    grad_unit = grad_normed * gain
    along = jnp.mean(grad_unit * unit, axis=-1, keepdims=True)
    return inverse * (grad_unit - jnp.mean(grad_unit, axis=-1, keepdims=True) - unit * along)


def head_mask(rows):
    channel = lax.broadcasted_iota(jnp.int32, (C, H * rows), 0)
    lane = lax.broadcasted_iota(jnp.int32, (C, H * rows), 1)
    return (lane // rows == channel // DH).astype(F32)


def spread_heads(values, mask):
    rows = values.shape[0]
    turned = jnp.transpose(values)
    turned = jnp.concatenate([turned] * (LANES // rows), axis=1)
    return jnp.concatenate([turned] * (H * rows // LANES), axis=1) * mask


def join_heads(values, mask):
    masked = values * mask
    rows = mask.shape[1] // H
    total = masked[:, :LANES]
    for i in range(1, H * rows // LANES):
        total = total + masked[:, i * LANES : (i + 1) * LANES]
    joined = total[:, :rows]
    for i in range(1, LANES // rows):
        joined = joined + total[:, i * rows : (i + 1) * rows]
    return jnp.transpose(joined)


def own_norm(sent, own_unit_out):
    n_seq, n_rows, _ = own_unit_out.shape
    units, _ = normalise(sent[:n_seq].reshape(n_seq * n_rows, C))
    own_unit_out[...] = units.reshape(n_seq, n_rows, C)


def own_half(seq_mask, own_unit, gains, w_row,
             query_gate_out, query_heads_out, own_memory_out, present_out):
    n_seq, n_rows, _ = own_unit.shape
    w_all = w_row[...]
    own_units = own_unit[...].reshape(n_seq * n_rows, C)
    projected = dot(own_units * gains[0:1, :], w_all, precision=EXACT)
    queries = projected[:, :C] * SCALE
    gates = jax.nn.sigmoid(projected[:, 3 * C :])
    query_gate_out[...] = jnp.concatenate([queries, gates], axis=1).reshape(n_seq, n_rows, 2 * C)
    own_memory_out[...] = projected[:, C : 3 * C].reshape(n_seq, n_rows, 2 * C)
    mask = head_mask(n_rows)
    for s in range(n_seq):
        query_heads_out[s] = spread_heads(queries[s * n_rows : (s + 1) * n_rows], mask)
    lane = lax.broadcasted_iota(jnp.int32, present_out.shape, 1) // (2 * C // n_seq)
    present = jnp.zeros(present_out.shape, F32)
    for s in range(n_seq):
        present = jnp.where(lane == s, seq_mask[s].astype(F32), present)
    present_out[...] = present


def row_forward(n_res, *refs):
    sent = refs[:n_res]
    (own, cotangent, gains, w_row, w_out, own_unit, query_gate, query_heads, own_memory, bias, present) = refs[
        n_res : n_res + 11
    ]
    payload, exponent_out, unit_out, memory_out, mixture_out, inverse_out, residue = refs[n_res + 11 :]
    n_seq, n_rows, _ = own.shape
    n_keys = n_res * n_rows
    me = lax.axis_index("res")
    w_memory = w_row[:, C : 3 * C]
    for away in range(n_res):
        where = lax.rem(me + away, n_res)
        residue[where] = sent[away][n_seq]
        if away:
            units, _ = normalise(sent[away][:n_seq].reshape(n_seq * n_rows, C))
            memories = dot(units * gains[0:1, :], w_memory, precision=EXACT)
            units = units.reshape(n_seq, n_rows, C)
            memories = memories.reshape(n_seq, n_rows, 2 * C)
        else:
            units, memories = own_unit[...], own_memory[...]
        unit_out[where] = units
        memory_out[where] = memories
    n_blocks = payload.shape[0]
    block = n_rows // n_blocks
    bias_t = jnp.transpose(bias[...].reshape(H * n_rows, n_keys).astype(F32))
    key_bias = MASKED * (residue[...].reshape(n_keys, C)[:, 0:1] - 1.0)
    mask = head_mask(n_rows)
    wide_mask = jnp.concatenate([mask, mask], axis=0)
    initial = own[...].reshape(n_seq * n_rows, C).astype(F32)
    gates = query_gate[...].reshape(n_seq * n_rows, 2 * C)[:, C:]
    sums = []
    for s in range(n_seq):
        memory = memory_out[:, s].reshape(n_keys, 2 * C)
        scores = dot(memory[:, :C], query_heads[s], precision=EXACT) + bias_t + key_bias
        exponent = jnp.exp(scores - jnp.max(scores, axis=0, keepdims=True))
        exponent_out[s] = exponent
        summed = dot_rows(jnp.concatenate([memory[:, C:], jnp.ones((n_keys, C), F32)], axis=1), exponent)
        sums.append(join_heads(summed, wide_mask))
    summed = jnp.concatenate(sums, axis=0)
    inverse = 1.0 / summed[:, C:]
    mixture = summed[:, :C] * inverse
    inverse_out[...] = inverse.reshape(n_seq, n_rows, C)
    mixture_out[...] = mixture.reshape(n_seq, n_rows, C)
    middle = initial + dot(gates * mixture, w_out[...])
    both = jnp.concatenate([middle, cotangent[...].reshape(n_seq * n_rows, C).astype(F32)], axis=1)
    for s in range(n_seq):
        for b in range(n_blocks):
            row = s * n_rows + b * block
            payload[b, s] = both[row : row + block, :]
    for b in range(n_blocks):
        payload[b, n_seq] = present[...]


def column_step(arrived, gains, w_col, w_out, returned, gathered, mask_rows, n_seq):
    n_src, _, block, _ = arrived.shape
    group = n_seq * block
    rows = n_src * group
    wide = 2 * C // n_seq
    share = C // n_src
    for src in range(n_src):
        for s in range(n_seq):
            gathered[src, s * block : (s + 1) * block, :] = arrived[src, s]
            mask_rows[src, s * block : (s + 1) * block, :] = jnp.broadcast_to(
                arrived[src, n_seq, :, s * wide : s * wide + 1], (block, C)
            )
    data = gathered[...].reshape(rows, 2 * C)
    present = mask_rows[...]
    middle = data[:, :C]
    cot = data[:, C:]
    gain = gains[1:2, :]

    def over_sequences(values, combine, reduce):
        total = reduce(values.reshape(n_src, group, C), axis=0)
        result = total
        for shift in range(1, n_seq):
            result = combine(result, pltpu.roll(total, shift * block, 0))
        return result

    def total_of(values):
        return over_sequences(values, jnp.add, jnp.sum)

    def spread(values):
        return jnp.broadcast_to(values[None], (n_src, group, C)).reshape(rows, C)

    lane = lax.broadcasted_iota(jnp.int32, (C, C), 1)
    row = lax.broadcasted_iota(jnp.int32, (C, C), 0)
    same_head = (row // DH == lane // DH).astype(F32)
    repeat = (lax.broadcasted_iota(jnp.int32, (DH, C), 0) == lax.broadcasted_iota(jnp.int32, (DH, C), 1) % DH).astype(F32)
    w_all = w_col[...]
    w_query = w_all[:, :C]
    w_key = dot(w_all[:, C : C + DH], repeat, precision=EXACT)
    w_value = dot(w_all[:, C + DH : C + 2 * DH], repeat)
    w_gate = w_all[:, C + 2 * DH :]
    w_rest = jnp.concatenate([w_key, w_value, w_gate], axis=1)

    unit, inverse = normalise(middle)
    normed = unit * gain
    present_rows = present.reshape(rows, C)
    counted = total_of(present_rows)
    mean_unit = total_of(present_rows * unit) / counted
    mean_normed = mean_unit * gain
    query = dot(mean_normed, w_query, precision=EXACT) * SCALE
    query_rows = spread(query)
    rest = dot(normed, w_rest, precision=EXACT)
    key, value = rest[:, :C], rest[:, C : 2 * C]
    gate = jax.nn.sigmoid(rest[:, 2 * C :])
    scores = dot(query_rows * key, same_head, precision=EXACT) + MASKED * (present_rows - 1.0)
    peak = over_sequences(scores, jnp.maximum, jnp.max)
    exponent = jnp.exp(scores - spread(peak))
    weights = exponent / spread(total_of(exponent))
    mixture = total_of(weights * value)
    mixture_rows = spread(mixture)

    grad_gated = dot_t(cot, w_out[...])
    out_grad = dot_rows(gate * mixture_rows, cot)
    grad_mixture = total_of(gate * grad_gated)
    grad_mixture_rows = spread(grad_mixture)
    grad_gate = grad_gated * mixture_rows * gate * (1.0 - gate)
    grad_weights = dot(grad_mixture_rows * value, same_head)
    inner = spread(dot(grad_mixture * mixture, same_head))
    grad_scores = weights * (grad_weights - inner)
    grad_rest = jnp.concatenate([grad_scores * query_rows, weights * grad_mixture_rows, grad_gate], axis=1)
    grad_query = total_of(grad_scores * key) * SCALE
    grad_mean = dot_t(grad_query, w_query)
    grad_normed = present_rows * spread(grad_mean / counted) + dot_t(grad_rest, w_rest)
    grad_query_weights = dot_rows(mean_unit, grad_query) * (1.0 / n_seq)
    grad_rest_weights = dot_rows(unit, grad_rest)
    fold_row = lax.broadcasted_iota(jnp.int32, (2 * C, 2 * DH), 0)
    fold_lane = lax.broadcasted_iota(jnp.int32, (2 * C, 2 * DH), 1)
    fold = ((fold_row // C == fold_lane // DH) & (fold_row % DH == fold_lane % DH)).astype(F32)
    grad_key_value = dot(grad_rest_weights[:, : 2 * C], fold)
    first = jnp.concatenate([grad_query_weights, grad_rest_weights[:, 2 * C :]], axis=1)
    second = jnp.concatenate([out_grad, grad_key_value, jnp.zeros((C, C - 2 * DH), F32)], axis=1)
    grad_middle = (cot + normalise_back(grad_normed, gain, unit, inverse)).reshape(n_src, group, C)
    for src in range(n_src):
        for s in range(n_seq):
            returned[src, 0, :, s * C : (s + 1) * C] = grad_middle[src, s * block : (s + 1) * block, :]
        returned[src, 1] = first[src * share : (src + 1) * share, :]
        returned[src, 2] = second[src * share : (src + 1) * share, :]


def row_backward(n_res, returned, exponent_in, unit_in, memory_in, query_gate_in, query_heads_in, mixture_in, inverse_in,
                 own_unit_in, w_row, w_out, bias_out, middle_grad, *refs):
    sums_out, shares = refs[:n_res], refs[n_res]
    me = lax.axis_index("res")
    n_seq, n_rows, _ = middle_grad.shape
    n_keys = n_res * n_rows
    n_blocks, _, block, _ = returned.shape
    w_all = w_row[...]
    w_memory = w_all[:, C : 3 * C]
    w_query_gate = jnp.concatenate([w_all[:, :C], w_all[:, 3 * C :]], axis=1)
    mask = head_mask(n_rows)
    for b in range(n_blocks):
        for s in range(n_seq):
            middle_grad[s, b * block : (b + 1) * block, :] = returned[b, 0, :, s * C : (s + 1) * C]
    grad_middle = middle_grad[...].reshape(n_seq * n_rows, C)
    queries_gates = query_gate_in[...].reshape(n_seq * n_rows, 2 * C)
    gates = queries_gates[:, C:]
    mixtures = mixture_in[...].reshape(n_seq * n_rows, C)
    grad_gated = dot_t(grad_middle, w_out[...])
    grad_out = dot_rows(gates * mixtures, grad_middle)
    grad_gates = grad_gated * mixtures * gates * (1.0 - gates)
    grad_mixtures = grad_gated * gates * inverse_in[...].reshape(n_seq * n_rows, C)
    inners = grad_mixtures * mixtures
    bias_grad = jnp.zeros((n_keys, H * n_rows), F32)
    grad_queries = []
    grad_memories = []
    for s in range(n_seq):
        rows = slice(s * n_rows, (s + 1) * n_rows)
        memory = memory_in[:, s].reshape(n_keys, 2 * C)
        exponent = exponent_in[s]
        grad_heads = spread_heads(grad_mixtures[rows], mask)
        right = jnp.concatenate([grad_heads, spread_heads(inners[rows], mask)], axis=0)
        left = jnp.concatenate([memory[:, C:], jnp.full((n_keys, C), -1.0, F32)], axis=1)
        grad_scores = exponent * dot(left, right)
        bias_grad = bias_grad + grad_scores
        grad_queries.append(join_heads(dot_rows(memory[:, :C], grad_scores), mask) * SCALE)
        grad_key = dot_t(grad_scores, query_heads_in[s])
        grad_value = dot_t(exponent, grad_heads)
        grad_memories.append(jnp.concatenate([grad_key, grad_value], axis=1))
    grad_query_gate = jnp.concatenate([jnp.concatenate(grad_queries, axis=0), grad_gates], axis=1)
    grad_memory = jnp.concatenate(grad_memories, axis=0)
    grad_query_gate_weights = dot_rows(own_unit_in[...].reshape(n_seq * n_rows, C), grad_query_gate)
    units = jnp.concatenate([unit_in[:, s].reshape(n_keys, C) for s in range(n_seq)], axis=0)
    grad_memory_weights = dot_rows(units, grad_memory)
    from_memory = dot_t(grad_memory, w_memory)
    from_own = dot_t(grad_query_gate, w_query_gate)
    from_memory = [from_memory[s * n_keys : (s + 1) * n_keys] for s in range(n_seq)]
    from_own = [from_own[s * n_rows : (s + 1) * n_rows] for s in range(n_seq)]
    bias_out[...] = bias_grad
    half = C // 2
    weight_grads = jnp.concatenate(
        [grad_query_gate_weights, grad_memory_weights, jnp.concatenate([grad_out[:half], grad_out[half:]], axis=1)],
        axis=0,
    )
    part = shares.shape[1] - ROWS - n_rows
    shares[...] = jnp.zeros(shares.shape, F32)
    share = C // n_blocks
    column = jnp.sum(returned[:, 1:, :, :], axis=0)
    normed = jnp.concatenate(from_memory, axis=1)
    for i in range(n_res):
        rows = min(part, max(0, weight_grads.shape[0] - i * part))
        if rows:
            shares[i, :rows, :] = weight_grads[i * part : i * part + rows, :]
        shares[i, part : part + share, :] = column[0]
        shares[i, part + ROWS // 2 : part + ROWS // 2 + share, :] = column[1]
        shares[i, part + ROWS :, :] = normed[i * n_rows : (i + 1) * n_rows, :]
    for away in range(n_res):
        sums_out[away][...] = shares[lax.rem(me + away, n_res)]
    sums_out[0][part + ROWS :, :] += jnp.concatenate(from_own, axis=1)


def step_bits(n_seq_devices, odd):
    bits = list(range(n_seq_devices.bit_length() - 1))
    if odd:
        for i in range(0, len(bits) - 1, 2):
            bits[i], bits[i + 1] = bits[i + 1], bits[i]
    return bits


def relative_block(mask_of_bits, n_blocks):
    odd = lax.rem(lax.axis_index("res"), 2)
    even_mask = mask_of_bits(step_bits(n_blocks, False))
    odd_mask = mask_of_bits(step_bits(n_blocks, True))
    return lax.axis_index("seq") ^ (even_mask + odd * (odd_mask - even_mask))


def split_blocks(bias_t, state, send):
    tiles = bias_t.shape[1] // LANES
    n_blocks = (state.shape[0] + send.shape[0]) // tiles
    keys_each = bias_t.shape[0] // n_blocks
    half = n_blocks // 2

    for slot in range(n_blocks):

        def mask_of_bits(bits):
            last = len(bits) - 1
            return sum(1 << bit for at, bit in enumerate(bits) if slot >> (last - at) & 1)

        block = relative_block(mask_of_bits, n_blocks)
        values = bias_t[pl.ds(pl.multiple_of(block * keys_each, keys_each), keys_each), :]
        for i in range(tiles):
            out, at = (state, slot) if slot < half else (send, slot - half)
            out[at * tiles + i] = values[:, i * LANES : (i + 1) * LANES]


def bias_last(state, arrived, bias_out):
    heads, _, n_rows = bias_out.shape
    each = LANES // n_rows
    for i in range(state.shape[0]):
        total = state[i] + arrived[i]
        for e in range(each):
            bias_out[i * each + e] = total[:, e * n_rows : (e + 1) * n_rows]


def add_shares(bias_send, *refs):
    sums, send, normed = refs[:-2], refs[-2], refs[-1]
    total = sums[0][...]
    for more in sums[1:]:
        total = total + more[...]
    left = bias_send.shape[0]
    rows = total.shape[0] - normed.shape[0]
    send[:left] = bias_send[...]
    send[left : send.shape[0] - 1] = total[: rows - ROWS].reshape(rows // ROWS - 1, ROWS, LANES)
    piece = total[rows - ROWS : rows]
    odd = lax.rem(lax.axis_index("res"), 2)
    send[send.shape[0] - 1] = jnp.where(odd == 1, pltpu.roll(piece, ROWS // 2, 0), piece)
    normed[...] = total[rows:]


def step(part, first, state, sent, arrived, state_out, send):
    left = state.shape[0]
    half = left // 2
    total = state[...] + arrived[:left]
    state_out[...] = total[:half]
    send[:half] = total[half:]
    send[half : half + part] = sent[left : left + part] + arrived[left : left + part]
    at = half + part
    if first:
        half_rows = ROWS // 2
        send[at] = jnp.concatenate([sent[left + part][:half_rows], arrived[left + part][:half_rows]], axis=0)
    else:
        pieces = sent.shape[0] - left - part
        send[at : at + pieces] = sent[left + part :]
        send[at + pieces :] = arrived[left + part :]


def last_step(part, sent, arrived, _, shared):
    pieces = (shared.shape[0] - part) // 2
    left = sent.shape[0] - part - pieces
    shared[:part] = sent[left : left + part] + arrived[left : left + part]
    shared[part : part + pieces] = sent[left + part :]
    shared[part + pieces :] = arrived[left + part :]


def finish_alignment(own, middle_grad, gains, normed, out, done):
    n_seq = own.shape[0]
    done[...] = jnp.zeros(done.shape, F32)
    for s in range(n_seq):
        unit, inverse = normalise(own[s].astype(F32))
        grad_normed = normed[:, s * C : (s + 1) * C]
        out[s] = (middle_grad[s] + normalise_back(grad_normed, gains[0:1, :], unit, inverse)).astype(out.dtype)


def unpack(n_res, *refs):
    parts = refs[:n_res]
    gains, w_row, w_col, gains_out, row_project_out, row_out_out, col_project_out, col_out_out = refs[n_res : n_res + 8]
    shares, column = refs[n_res + 8 :]
    me = lax.axis_index("res")
    for away in range(n_res):
        shares[lax.rem(me + away, n_res)] = parts[away][...]
    n_blocks, _, share, _ = column.shape
    part = shares.shape[1] - n_blocks // 2
    place = lax.axis_index("seq")
    for half in range(2):
        bits = step_bits(n_blocks, half == 1)
        for slot in range(n_blocks):
            block = place ^ sum(1 << bit for at, bit in enumerate(bits) if slot >> at & 1)
            row = slot % 2 * (ROWS // 2)
            column[block, half] = shares[half, part + slot // 2, row : row + share, :]
    flat = jnp.concatenate([shares[i, :part].reshape(part * ROWS, LANES) for i in range(n_res)], axis=0)
    query_gate, memory, outs = flat[:C], flat[C : 2 * C], flat[2 * C : 2 * C + C // 2]
    col_query_gate = jnp.concatenate([column[i, 0] for i in range(n_blocks)], axis=0)
    col_rest = jnp.concatenate([column[i, 1] for i in range(n_blocks)], axis=0)
    rest = col_rest[:, C : C + 2 * DH]
    gain_row = to_column(gains[0:1, :])
    gain_col = to_column(gains[1:2, :])
    w_all = w_row[...]
    w_column = w_col[...]
    row_gain_grad = (
        jnp.sum(query_gate[:, :C] * w_all[:, :C], axis=1, keepdims=True)
        + jnp.sum(memory * w_all[:, C : 3 * C], axis=1, keepdims=True)
        + jnp.sum(query_gate[:, C:] * w_all[:, 3 * C :], axis=1, keepdims=True)
    )
    col_gain_grad = (
        jnp.sum(col_query_gate[:, :C] * w_column[:, :C], axis=1, keepdims=True)
        + jnp.sum(rest * w_column[:, C : C + 2 * DH], axis=1, keepdims=True)
        + jnp.sum(col_query_gate[:, C:] * w_column[:, C + 2 * DH :], axis=1, keepdims=True)
    )
    gains_out[0:1, :] = to_row(row_gain_grad)
    gains_out[1:2, :] = to_row(col_gain_grad)
    row_project_out[:, :C] = query_gate[:, :C] * gain_row
    row_project_out[:, C : 3 * C] = memory * gain_row
    row_project_out[:, 3 * C :] = query_gate[:, C:] * gain_row
    col_project_out[:, :C] = col_query_gate[:, :C] * gain_col
    col_project_out[:, C : C + 2 * DH] = rest * gain_col
    col_project_out[:, C + 2 * DH :] = col_query_gate[:, C:] * gain_col
    half = C // 2
    row_out_out[:half, :] = outs[:, :C]
    row_out_out[half:, :] = outs[:, C:]
    col_out_out[...] = col_rest[:, :C]


def call(body, outs, *operands, smem=0, unread=0, scratch=(), name):
    vmem = pl.BlockSpec(memory_space=pltpu.VMEM)
    scalar = pl.BlockSpec(memory_space=pltpu.SMEM)
    return pl.pallas_call(
        body,
        out_shape=[jax.ShapeDtypeStruct(shape, kind) for shape, kind in outs],
        in_specs=[scalar] * smem + [vmem] * (len(operands) - smem - unread)
        + [pl.BlockSpec(memory_space=pl.ANY)] * unread,
        out_specs=[vmem] * len(outs),
        scratch_shapes=list(scratch),
        compiler_params=pltpu.CompilerParams(vmem_limit_bytes=32 * 1024 * 1024),
        name=name,
    )(*operands)


def shift_residues(values, away, count):
    return lax.ppermute(values, "res", [((i + away) % count, i) for i in range(count)])


def cross(values, at, seq_count, res_count):
    pairs = []
    for r in range(res_count):
        bit = 1 << step_bits(seq_count, r % 2)[at]
        pairs += [(i * res_count + r, (i ^ bit) * res_count + r) for i in range(seq_count)]
    return lax.ppermute(values, ("seq", "res"), pairs)


def swap_blocks(values):
    return lax.all_to_all(values, "seq", 0, 0, tiled=True)


def local(
    alignment,
    cotangent,
    pair_bias,
    norm_gains,
    row_project,
    row_output,
    column_project,
    column_output,
    residue_mask,
    sequence_mask,
    seq_count,
    res_count,
):
    n_seq, n_rows, _ = alignment.shape
    n_keys = pair_bias.shape[2]
    block = n_rows // seq_count
    group = n_seq * block
    away_range = range(1, res_count)
    present_keys = jnp.broadcast_to(residue_mask.astype(F32)[None, :, None], (1, n_rows, C))
    sent = jnp.concatenate([alignment.astype(F32), present_keys], axis=0)
    (own_unit,) = call(own_norm, [((n_seq, n_rows, C), F32)], sent, name="own_norm")
    query_gate, query_heads, own_memory, present = call(
        own_half,
        [
            ((n_seq, n_rows, 2 * C), F32),
            ((n_seq, C, H * n_rows), F32),
            ((n_seq, n_rows, 2 * C), F32),
            ((block, 2 * C), F32),
        ],
        sequence_mask, own_unit, norm_gains, row_project,
        smem=1,
        name="own_half",
    )
    payload, exponent, unit, memory, mixture, inverse = call(
        functools.partial(row_forward, res_count),
        [
            ((seq_count, n_seq + 1, block, 2 * C), F32),
            ((n_seq, n_keys, H * n_rows), F32),
            ((res_count, n_seq, n_rows, C), F32),
            ((res_count, n_seq, n_rows, 2 * C), F32),
            ((n_seq, n_rows, C), F32),
            ((n_seq, n_rows, C), F32),
        ],
        sent, *[shift_residues(sent, away, res_count) for away in away_range],
        alignment, cotangent, norm_gains, row_project, row_output, own_unit, query_gate, query_heads, own_memory, pair_bias,
        present,
        scratch=[pltpu.VMEM((res_count, n_rows, C), F32)],
        name="row_forward",
    )
    arrived = swap_blocks(payload)
    (returned,) = call(
        functools.partial(column_step, n_seq=n_seq),
        [((seq_count, 3, block, 2 * C), F32)],
        arrived, norm_gains, column_project, column_output,
        scratch=[pltpu.VMEM((seq_count, group, 2 * C), F32), pltpu.VMEM((seq_count, group, C), F32)],
        name="column_step",
    )
    returned = swap_blocks(returned)
    part = -(-5 * C // (2 * ROWS * res_count)) * ROWS
    keys_each = n_keys // seq_count
    tiles = H * n_rows // LANES
    left = seq_count // 2 * tiles
    bias_grad, middle_grad, *sums = call(
        functools.partial(row_backward, res_count),
        [((n_keys, H * n_rows), F32), ((n_seq, n_rows, C), F32)]
        + [((part + ROWS + n_rows, LANES), F32)] * res_count,
        returned, exponent, unit, memory, query_gate, query_heads, mixture, inverse, own_unit, row_project, row_output,
        scratch=[pltpu.VMEM((res_count, part + ROWS + n_rows, LANES), F32)],
        name="row_backward",
    )
    sums = sums[:1] + [shift_residues(sums[away], -away, res_count) for away in away_range]
    state, send = call(
        split_blocks, [((left, keys_each, LANES), F32)] * 2, bias_grad, name="split_blocks"
    )
    part_tiles = part // ROWS
    send, normed = call(
        add_shares,
        [((left + part_tiles + 1, ROWS, LANES), F32), ((n_rows, LANES), F32)],
        send, *sums,
        name="add_shares",
    )
    grad_alignment, done = call(
        finish_alignment,
        [(alignment.shape, alignment.dtype), ((ROWS, LANES), F32)],
        alignment, middle_grad, norm_gains, normed,
        name="finish_alignment",
    )
    steps = seq_count.bit_length() - 1
    for at in range(steps):
        arrived = cross(send, at, seq_count, res_count)
        if at < steps - 1:
            left //= 2
            state, send = call(
                functools.partial(step, part_tiles, at == 0),
                [((left, ROWS, LANES), F32), ((left + part_tiles + (1 << at), ROWS, LANES), F32)],
                state, send, arrived,
                name="step",
            )
    (shared,) = call(
        functools.partial(last_step, part_tiles),
        [((part_tiles + seq_count // 2, ROWS, LANES), F32)],
        send, arrived, done,
        unread=1,
        name="last_step",
    )
    (bias_grad,) = call(bias_last, [((H, keys_each, n_rows), F32)], state, arrived, name="bias_last")
    grads = call(
        functools.partial(unpack, res_count),
        [((2, C), F32), ((C, 4 * C), F32), ((C, C), F32), ((C, 2 * C + 2 * DH), F32), ((C, C), F32)],
        shared, *[shift_residues(shared, away, res_count) for away in away_range],
        norm_gains, row_project, column_project,
        scratch=[
            pltpu.VMEM((res_count, part_tiles + seq_count // 2, ROWS, LANES), F32),
            pltpu.VMEM((seq_count, 2, C // seq_count, LANES), F32),
        ],
        name="unpack",
    )
    return (grad_alignment, jnp.transpose(bias_grad, (0, 2, 1)), *grads)


def solution(mesh):
    placed = (
        P("seq", "res", None),
        P("seq", "res", None),
        P(None, "res", None),
        P(),
        P(),
        P(),
        P(),
        P(),
        P("res"),
        P("seq"),
    )
    return jax.shard_map(
        functools.partial(local, seq_count=mesh.shape["seq"], res_count=mesh.shape["res"]),
        mesh=mesh,
        in_specs=placed,
        out_specs=(P("seq", "res", None), P(None, "res", "seq"), P(), P(), P(), P(), P()),
        check_vma=False,
    )
```

```python
import functools

import jax
import jax.numpy as jnp
from jax import lax
from jax.experimental import pallas as pl
from jax.experimental.pallas import tpu as pltpu
from jax.sharding import PartitionSpec as P

C = 64
H = 8
DH = 8
LANES = 128
ROWS = 8

EXACT = lax.Precision.HIGHEST
THREE = lax.Precision.HIGH
EPSILON = 1e-05
MASKED = 1000000000.0
SCALE = DH ** (-0.5)
F32 = jnp.float32


def dot(a, b, over=((1,), (0,)), precision=THREE):
    return lax.dot_general(a, b, (over, ((), ())), precision=precision, preferred_element_type=F32)


def dot_rows(a, b):
    return dot(a, b, ((0,), (0,)))


def dot_t(a, b, precision=THREE):
    return dot(a, b, ((1,), (1,)), precision)


def to_column(row):
    eye = lax.broadcasted_iota(jnp.int32, (C, C), 0) == lax.broadcasted_iota(jnp.int32, (C, C), 1)
    return jnp.sum(jnp.where(eye, row, 0.0), axis=1, keepdims=True)


def to_row(column):
    eye = lax.broadcasted_iota(jnp.int32, (C, C), 0) == lax.broadcasted_iota(jnp.int32, (C, C), 1)
    return jnp.sum(jnp.where(eye, column, 0.0), axis=0, keepdims=True)


def normalise(values):
    centred = values - jnp.mean(values, axis=-1, keepdims=True)
    inverse = lax.rsqrt(jnp.mean(centred * centred, axis=-1, keepdims=True) + EPSILON)
    return centred * inverse, inverse


def normalise_back(grad_normed, gain, unit, inverse):
    grad_unit = grad_normed * gain
    along = jnp.mean(grad_unit * unit, axis=-1, keepdims=True)
    return inverse * (grad_unit - jnp.mean(grad_unit, axis=-1, keepdims=True) - unit * along)


def head_mask(rows):
    channel = lax.broadcasted_iota(jnp.int32, (C, H * rows), 0)
    lane = lax.broadcasted_iota(jnp.int32, (C, H * rows), 1)
    return (lane // rows == channel // DH).astype(F32)


def spread_heads(values, mask):
    rows = values.shape[0]
    turned = jnp.transpose(values)
    turned = jnp.concatenate([turned] * (LANES // rows), axis=1)
    return jnp.concatenate([turned] * (H * rows // LANES), axis=1) * mask


def join_heads(values, mask):
    masked = values * mask
    rows = mask.shape[1] // H
    total = masked[:, :LANES]
    for i in range(1, H * rows // LANES):
        total = total + masked[:, i * LANES : (i + 1) * LANES]
    joined = total[:, :rows]
    for i in range(1, LANES // rows):
        joined = joined + total[:, i * rows : (i + 1) * rows]
    return jnp.transpose(joined)


def own_norm(sent, own_unit_out):
    n_seq, n_rows, _ = own_unit_out.shape
    units, _ = normalise(sent[:n_seq].reshape(n_seq * n_rows, C))
    own_unit_out[...] = units.reshape(n_seq, n_rows, C)


def own_half(seq_mask, own_unit, gains, w_row,
             query_gate_out, query_heads_out, own_memory_out, present_out):
    n_seq, n_rows, _ = own_unit.shape
    w_all = w_row[...]
    own_units = own_unit[...].reshape(n_seq * n_rows, C)
    projected = dot(own_units * gains[0:1, :], w_all, precision=EXACT)
    queries = projected[:, :C] * SCALE
    gates = jax.nn.sigmoid(projected[:, 3 * C :])
    query_gate_out[...] = jnp.concatenate([queries, gates], axis=1).reshape(n_seq, n_rows, 2 * C)
    own_memory_out[...] = projected[:, C : 3 * C].reshape(n_seq, n_rows, 2 * C)
    mask = head_mask(n_rows)
    for s in range(n_seq):
        query_heads_out[s] = spread_heads(queries[s * n_rows : (s + 1) * n_rows], mask)
    lane = lax.broadcasted_iota(jnp.int32, present_out.shape, 1) // (2 * C // n_seq)
    present = jnp.zeros(present_out.shape, F32)
    for s in range(n_seq):
        present = jnp.where(lane == s, seq_mask[s].astype(F32), present)
    present_out[...] = present


def row_forward(n_res, *refs):
    sent = refs[:n_res]
    (own, cotangent, gains, w_row, w_out, own_unit, query_gate, query_heads, own_memory, bias, present) = refs[
        n_res : n_res + 11
    ]
    payload, exponent_out, unit_out, memory_out, mixture_out, inverse_out, residue = refs[n_res + 11 :]
    n_seq, n_rows, _ = own.shape
    n_keys = n_res * n_rows
    me = lax.axis_index("res")
    w_memory = w_row[:, C : 3 * C]
    for away in range(n_res):
        where = lax.rem(me + away, n_res)
        residue[where] = sent[away][n_seq]
        if away:
            units, _ = normalise(sent[away][:n_seq].reshape(n_seq * n_rows, C))
            memories = dot(units * gains[0:1, :], w_memory, precision=EXACT)
            units = units.reshape(n_seq, n_rows, C)
            memories = memories.reshape(n_seq, n_rows, 2 * C)
        else:
            units, memories = own_unit[...], own_memory[...]
        unit_out[where] = units
        memory_out[where] = memories
    n_blocks = payload.shape[0]
    block = n_rows // n_blocks
    bias_t = jnp.transpose(bias[...].reshape(H * n_rows, n_keys).astype(F32))
    key_bias = MASKED * (residue[...].reshape(n_keys, C)[:, 0:1] - 1.0)
    mask = head_mask(n_rows)
    wide_mask = jnp.concatenate([mask, mask], axis=0)
    initial = own[...].reshape(n_seq * n_rows, C).astype(F32)
    gates = query_gate[...].reshape(n_seq * n_rows, 2 * C)[:, C:]
    sums = []
    for s in range(n_seq):
        memory = memory_out[:, s].reshape(n_keys, 2 * C)
        scores = dot(memory[:, :C], query_heads[s], precision=EXACT) + bias_t + key_bias
        exponent = jnp.exp(scores - jnp.max(scores, axis=0, keepdims=True))
        exponent_out[s] = exponent
        summed = dot_rows(jnp.concatenate([memory[:, C:], jnp.ones((n_keys, C), F32)], axis=1), exponent)
        sums.append(join_heads(summed, wide_mask))
    summed = jnp.concatenate(sums, axis=0)
    inverse = 1.0 / summed[:, C:]
    mixture = summed[:, :C] * inverse
    inverse_out[...] = inverse.reshape(n_seq, n_rows, C)
    mixture_out[...] = mixture.reshape(n_seq, n_rows, C)
    middle = initial + dot(gates * mixture, w_out[...])
    both = jnp.concatenate([middle, cotangent[...].reshape(n_seq * n_rows, C).astype(F32)], axis=1)
    for s in range(n_seq):
        for b in range(n_blocks):
            row = s * n_rows + b * block
            payload[b, s] = both[row : row + block, :]
    for b in range(n_blocks):
        payload[b, n_seq] = present[...]


def column_step(arrived, gains, w_col, w_out, returned, gathered, mask_rows, n_seq):
    n_src, _, block, _ = arrived.shape
    group = n_seq * block
    rows = n_src * group
    wide = 2 * C // n_seq
    share = C // n_src
    for src in range(n_src):
        for s in range(n_seq):
            gathered[src, s * block : (s + 1) * block, :] = arrived[src, s]
            mask_rows[src, s * block : (s + 1) * block, :] = jnp.broadcast_to(
                arrived[src, n_seq, :, s * wide : s * wide + 1], (block, C)
            )
    data = gathered[...].reshape(rows, 2 * C)
    present = mask_rows[...]
    middle = data[:, :C]
    cot = data[:, C:]
    gain = gains[1:2, :]

    def over_sequences(values, combine, reduce):
        total = reduce(values.reshape(n_src, group, C), axis=0)
        result = total
        for shift in range(1, n_seq):
            result = combine(result, pltpu.roll(total, shift * block, 0))
        return result

    def total_of(values):
        return over_sequences(values, jnp.add, jnp.sum)

    def spread(values):
        return jnp.broadcast_to(values[None], (n_src, group, C)).reshape(rows, C)

    lane = lax.broadcasted_iota(jnp.int32, (C, C), 1)
    row = lax.broadcasted_iota(jnp.int32, (C, C), 0)
    same_head = (row // DH == lane // DH).astype(F32)
    repeat = (lax.broadcasted_iota(jnp.int32, (DH, C), 0) == lax.broadcasted_iota(jnp.int32, (DH, C), 1) % DH).astype(F32)
    w_all = w_col[...]
    w_query = w_all[:, :C]
    w_key = dot(w_all[:, C : C + DH], repeat, precision=EXACT)
    w_value = dot(w_all[:, C + DH : C + 2 * DH], repeat)
    w_gate = w_all[:, C + 2 * DH :]
    w_rest = jnp.concatenate([w_key, w_value, w_gate], axis=1)

    unit, inverse = normalise(middle)
    normed = unit * gain
    present_rows = present.reshape(rows, C)
    counted = total_of(present_rows)
    mean_unit = total_of(present_rows * unit) / counted
    mean_normed = mean_unit * gain
    query = dot(mean_normed, w_query, precision=EXACT) * SCALE
    query_rows = spread(query)
    rest = dot(normed, w_rest, precision=EXACT)
    key, value = rest[:, :C], rest[:, C : 2 * C]
    gate = jax.nn.sigmoid(rest[:, 2 * C :])
    scores = dot(query_rows * key, same_head, precision=EXACT) + MASKED * (present_rows - 1.0)
    peak = over_sequences(scores, jnp.maximum, jnp.max)
    exponent = jnp.exp(scores - spread(peak))
    weights = exponent / spread(total_of(exponent))
    mixture = total_of(weights * value)
    mixture_rows = spread(mixture)

    grad_gated = dot_t(cot, w_out[...])
    out_grad = dot_rows(gate * mixture_rows, cot)
    grad_mixture = total_of(gate * grad_gated)
    grad_mixture_rows = spread(grad_mixture)
    grad_gate = grad_gated * mixture_rows * gate * (1.0 - gate)
    grad_weights = dot(grad_mixture_rows * value, same_head)
    inner = spread(dot(grad_mixture * mixture, same_head))
    grad_scores = weights * (grad_weights - inner)
    grad_rest = jnp.concatenate([grad_scores * query_rows, weights * grad_mixture_rows, grad_gate], axis=1)
    grad_query = total_of(grad_scores * key) * SCALE
    grad_mean = dot_t(grad_query, w_query)
    grad_normed = present_rows * spread(grad_mean / counted) + dot_t(grad_rest, w_rest)
    grad_query_weights = dot_rows(mean_unit, grad_query) * (1.0 / n_seq)
    grad_rest_weights = dot_rows(unit, grad_rest)
    fold_row = lax.broadcasted_iota(jnp.int32, (2 * C, 2 * DH), 0)
    fold_lane = lax.broadcasted_iota(jnp.int32, (2 * C, 2 * DH), 1)
    fold = ((fold_row // C == fold_lane // DH) & (fold_row % DH == fold_lane % DH)).astype(F32)
    grad_key_value = dot(grad_rest_weights[:, : 2 * C], fold)
    first = jnp.concatenate([grad_query_weights, grad_rest_weights[:, 2 * C :]], axis=1)
    second = jnp.concatenate([out_grad, grad_key_value, jnp.zeros((C, C - 2 * DH), F32)], axis=1)
    grad_middle = (cot + normalise_back(grad_normed, gain, unit, inverse)).reshape(n_src, group, C)
    for src in range(n_src):
        for s in range(n_seq):
            returned[src, 0, :, s * C : (s + 1) * C] = grad_middle[src, s * block : (s + 1) * block, :]
        returned[src, 1] = first[src * share : (src + 1) * share, :]
        returned[src, 2] = second[src * share : (src + 1) * share, :]


def row_backward(n_res, returned, exponent_in, unit_in, memory_in, query_gate_in, query_heads_in, mixture_in, inverse_in,
                 own_unit_in, w_row, w_out, bias_out, middle_grad, *refs):
    sums_out, shares = refs[:n_res], refs[n_res]
    me = lax.axis_index("res")
    n_seq, n_rows, _ = middle_grad.shape
    n_keys = n_res * n_rows
    n_blocks, _, block, _ = returned.shape
    w_all = w_row[...]
    w_memory = w_all[:, C : 3 * C]
    w_query_gate = jnp.concatenate([w_all[:, :C], w_all[:, 3 * C :]], axis=1)
    mask = head_mask(n_rows)
    for b in range(n_blocks):
        for s in range(n_seq):
            middle_grad[s, b * block : (b + 1) * block, :] = returned[b, 0, :, s * C : (s + 1) * C]
    grad_middle = middle_grad[...].reshape(n_seq * n_rows, C)
    queries_gates = query_gate_in[...].reshape(n_seq * n_rows, 2 * C)
    gates = queries_gates[:, C:]
    mixtures = mixture_in[...].reshape(n_seq * n_rows, C)
    grad_gated = dot_t(grad_middle, w_out[...])
    grad_out = dot_rows(gates * mixtures, grad_middle)
    grad_gates = grad_gated * mixtures * gates * (1.0 - gates)
    grad_mixtures = grad_gated * gates * inverse_in[...].reshape(n_seq * n_rows, C)
    inners = grad_mixtures * mixtures
    bias_grad = jnp.zeros((n_keys, H * n_rows), F32)
    grad_queries = []
    grad_memories = []
    for s in range(n_seq):
        rows = slice(s * n_rows, (s + 1) * n_rows)
        memory = memory_in[:, s].reshape(n_keys, 2 * C)
        exponent = exponent_in[s]
        grad_heads = spread_heads(grad_mixtures[rows], mask)
        right = jnp.concatenate([grad_heads, spread_heads(inners[rows], mask)], axis=0)
        left = jnp.concatenate([memory[:, C:], jnp.full((n_keys, C), -1.0, F32)], axis=1)
        grad_scores = exponent * dot(left, right)
        bias_grad = bias_grad + grad_scores
        grad_queries.append(join_heads(dot_rows(memory[:, :C], grad_scores), mask) * SCALE)
        grad_key = dot_t(grad_scores, query_heads_in[s])
        grad_value = dot_t(exponent, grad_heads)
        grad_memories.append(jnp.concatenate([grad_key, grad_value], axis=1))
    grad_query_gate = jnp.concatenate([jnp.concatenate(grad_queries, axis=0), grad_gates], axis=1)
    grad_memory = jnp.concatenate(grad_memories, axis=0)
    grad_query_gate_weights = dot_rows(own_unit_in[...].reshape(n_seq * n_rows, C), grad_query_gate)
    units = jnp.concatenate([unit_in[:, s].reshape(n_keys, C) for s in range(n_seq)], axis=0)
    grad_memory_weights = dot_rows(units, grad_memory)
    from_memory = dot_t(grad_memory, w_memory)
    from_own = dot_t(grad_query_gate, w_query_gate)
    from_memory = [from_memory[s * n_keys : (s + 1) * n_keys] for s in range(n_seq)]
    from_own = [from_own[s * n_rows : (s + 1) * n_rows] for s in range(n_seq)]
    bias_out[...] = bias_grad
    half = C // 2
    weight_grads = jnp.concatenate(
        [grad_query_gate_weights, grad_memory_weights, jnp.concatenate([grad_out[:half], grad_out[half:]], axis=1)],
        axis=0,
    )
    part = shares.shape[1] - ROWS - n_rows
    shares[...] = jnp.zeros(shares.shape, F32)
    share = C // n_blocks
    column = jnp.sum(returned[:, 1:, :, :], axis=0)
    normed = jnp.concatenate(from_memory, axis=1)
    for i in range(n_res):
        rows = min(part, max(0, weight_grads.shape[0] - i * part))
        if rows:
            shares[i, :rows, :] = weight_grads[i * part : i * part + rows, :]
        shares[i, part : part + share, :] = column[0]
        shares[i, part + ROWS // 2 : part + ROWS // 2 + share, :] = column[1]
        shares[i, part + ROWS :, :] = normed[i * n_rows : (i + 1) * n_rows, :]
    for away in range(n_res):
        sums_out[away][...] = shares[lax.rem(me + away, n_res)]
    sums_out[0][part + ROWS :, :] += jnp.concatenate(from_own, axis=1)


def step_bits(n_seq_devices, odd):
    bits = list(range(n_seq_devices.bit_length() - 1))
    if odd:
        for i in range(0, len(bits) - 1, 2):
            bits[i], bits[i + 1] = bits[i + 1], bits[i]
    return bits


def relative_block(mask_of_bits, n_blocks):
    odd = lax.rem(lax.axis_index("res"), 2)
    even_mask = mask_of_bits(step_bits(n_blocks, False))
    odd_mask = mask_of_bits(step_bits(n_blocks, True))
    return lax.axis_index("seq") ^ (even_mask + odd * (odd_mask - even_mask))


def split_blocks(bias_t, state, send):
    tiles = bias_t.shape[1] // LANES
    n_blocks = (state.shape[0] + send.shape[0]) // tiles
    keys_each = bias_t.shape[0] // n_blocks
    half = n_blocks // 2

    for slot in range(n_blocks):

        def mask_of_bits(bits):
            last = len(bits) - 1
            return sum(1 << bit for at, bit in enumerate(bits) if slot >> (last - at) & 1)

        block = relative_block(mask_of_bits, n_blocks)
        values = bias_t[pl.ds(pl.multiple_of(block * keys_each, keys_each), keys_each), :]
        for i in range(tiles):
            out, at = (state, slot) if slot < half else (send, slot - half)
            out[at * tiles + i] = values[:, i * LANES : (i + 1) * LANES]


def bias_last(state, arrived, bias_out):
    heads, _, n_rows = bias_out.shape
    each = LANES // n_rows
    for i in range(state.shape[0]):
        total = state[i] + arrived[i]
        for e in range(each):
            bias_out[i * each + e] = total[:, e * n_rows : (e + 1) * n_rows]


def add_shares(bias_send, *refs):
    sums, send, normed = refs[:-2], refs[-2], refs[-1]
    total = sums[0][...]
    for more in sums[1:]:
        total = total + more[...]
    left = bias_send.shape[0]
    rows = total.shape[0] - normed.shape[0]
    send[:left] = bias_send[...]
    send[left : send.shape[0] - 1] = total[: rows - ROWS].reshape(rows // ROWS - 1, ROWS, LANES)
    piece = total[rows - ROWS : rows]
    odd = lax.rem(lax.axis_index("res"), 2)
    send[send.shape[0] - 1] = jnp.where(odd == 1, pltpu.roll(piece, ROWS // 2, 0), piece)
    normed[...] = total[rows:]


def step(part, first, state, sent, arrived, state_out, send):
    left = state.shape[0]
    half = left // 2
    total = state[...] + arrived[:left]
    state_out[...] = total[:half]
    send[:half] = total[half:]
    send[half : half + part] = sent[left : left + part] + arrived[left : left + part]
    at = half + part
    if first:
        half_rows = ROWS // 2
        send[at] = jnp.concatenate([sent[left + part][:half_rows], arrived[left + part][:half_rows]], axis=0)
    else:
        pieces = sent.shape[0] - left - part
        send[at : at + pieces] = sent[left + part :]
        send[at + pieces :] = arrived[left + part :]


def last_step(part, sent, arrived, _, shared):
    pieces = (shared.shape[0] - part) // 2
    left = sent.shape[0] - part - pieces
    shared[:part] = sent[left : left + part] + arrived[left : left + part]
    shared[part : part + pieces] = sent[left + part :]
    shared[part + pieces :] = arrived[left + part :]


def finish_alignment(own, middle_grad, gains, normed, out, done):
    n_seq = own.shape[0]
    done[...] = jnp.zeros(done.shape, F32)
    for s in range(n_seq):
        unit, inverse = normalise(own[s].astype(F32))
        grad_normed = normed[:, s * C : (s + 1) * C]
        out[s] = (middle_grad[s] + normalise_back(grad_normed, gains[0:1, :], unit, inverse)).astype(out.dtype)


def unpack(n_res, part_tiles, *refs):
    parts = refs[:n_res]
    gains, w_row, w_col, gains_out, row_project_out, row_out_out, col_project_out, col_out_out = refs[n_res : n_res + 8]
    shares, column = refs[n_res + 8 :]
    me = lax.axis_index("res")
    for away in range(n_res):
        shares[lax.rem(me + away, n_res)] = parts[away][...]
    n_blocks = 2 * parts[0].shape[0] - 2 * part_tiles
    share = C // n_blocks
    part = shares.shape[1] - n_blocks // 2
    place = lax.axis_index("seq")
    for half in range(2):
        bits = step_bits(n_blocks, half == 1)
        for slot in range(n_blocks):
            block = place ^ sum(1 << bit for at, bit in enumerate(bits) if slot >> at & 1)
            row = slot % 2 * (ROWS // 2)
            column[half, pl.ds(block * share, share), :] = shares[half, part + slot // 2, row : row + share, :]
    flat = jnp.concatenate([shares[i, :part].reshape(part * ROWS, LANES) for i in range(n_res)], axis=0)
    query_gate, memory, outs = flat[:C], flat[C : 2 * C], flat[2 * C : 2 * C + C // 2]
    col_query_gate = column[0]
    col_rest = column[1]
    rest = col_rest[:, C : C + 2 * DH]
    gain_row = to_column(gains[0:1, :])
    gain_col = to_column(gains[1:2, :])
    w_all = w_row[...]
    w_column = w_col[...]
    row_gain_grad = (
        jnp.sum(query_gate[:, :C] * w_all[:, :C], axis=1, keepdims=True)
        + jnp.sum(memory * w_all[:, C : 3 * C], axis=1, keepdims=True)
        + jnp.sum(query_gate[:, C:] * w_all[:, 3 * C :], axis=1, keepdims=True)
    )
    col_gain_grad = (
        jnp.sum(col_query_gate[:, :C] * w_column[:, :C], axis=1, keepdims=True)
        + jnp.sum(rest * w_column[:, C : C + 2 * DH], axis=1, keepdims=True)
        + jnp.sum(col_query_gate[:, C:] * w_column[:, C + 2 * DH :], axis=1, keepdims=True)
    )
    gains_out[0:1, :] = to_row(row_gain_grad)
    gains_out[1:2, :] = to_row(col_gain_grad)
    row_project_out[:, :C] = query_gate[:, :C] * gain_row
    row_project_out[:, C : 3 * C] = memory * gain_row
    row_project_out[:, 3 * C :] = query_gate[:, C:] * gain_row
    col_project_out[:, :C] = col_query_gate[:, :C] * gain_col
    col_project_out[:, C : C + 2 * DH] = rest * gain_col
    col_project_out[:, C + 2 * DH :] = col_query_gate[:, C:] * gain_col
    half = C // 2
    row_out_out[:half, :] = outs[:, :C]
    row_out_out[half:, :] = outs[:, C:]
    col_out_out[...] = col_rest[:, :C]


def call(body, outs, *operands, smem=0, unread=0, scratch=(), name):
    vmem = pl.BlockSpec(memory_space=pltpu.VMEM)
    scalar = pl.BlockSpec(memory_space=pltpu.SMEM)
    return pl.pallas_call(
        body,
        out_shape=[jax.ShapeDtypeStruct(shape, kind) for shape, kind in outs],
        in_specs=[scalar] * smem + [vmem] * (len(operands) - smem - unread)
        + [pl.BlockSpec(memory_space=pl.ANY)] * unread,
        out_specs=[vmem] * len(outs),
        scratch_shapes=list(scratch),
        compiler_params=pltpu.CompilerParams(vmem_limit_bytes=32 * 1024 * 1024),
        name=name,
    )(*operands)


def shift_residues(values, away, count):
    return lax.ppermute(values, "res", [((i + away) % count, i) for i in range(count)])


def cross(values, at, seq_count, res_count):
    pairs = []
    for r in range(res_count):
        bit = 1 << step_bits(seq_count, r % 2)[at]
        pairs += [(i * res_count + r, (i ^ bit) * res_count + r) for i in range(seq_count)]
    return lax.ppermute(values, ("seq", "res"), pairs)


def swap_blocks(values):
    return lax.all_to_all(values, "seq", 0, 0, tiled=True)


def local(
    alignment,
    cotangent,
    pair_bias,
    norm_gains,
    row_project,
    row_output,
    column_project,
    column_output,
    residue_mask,
    sequence_mask,
    seq_count,
    res_count,
):
    n_seq, n_rows, _ = alignment.shape
    n_keys = pair_bias.shape[2]
    block = n_rows // seq_count
    group = n_seq * block
    away_range = range(1, res_count)
    present_keys = jnp.broadcast_to(residue_mask.astype(F32)[None, :, None], (1, n_rows, C))
    sent = jnp.concatenate([alignment.astype(F32), present_keys], axis=0)
    (own_unit,) = call(own_norm, [((n_seq, n_rows, C), F32)], sent, name="own_norm")
    query_gate, query_heads, own_memory, present = call(
        own_half,
        [
            ((n_seq, n_rows, 2 * C), F32),
            ((n_seq, C, H * n_rows), F32),
            ((n_seq, n_rows, 2 * C), F32),
            ((block, 2 * C), F32),
        ],
        sequence_mask, own_unit, norm_gains, row_project,
        smem=1,
        name="own_half",
    )
    payload, exponent, unit, memory, mixture, inverse = call(
        functools.partial(row_forward, res_count),
        [
            ((seq_count, n_seq + 1, block, 2 * C), F32),
            ((n_seq, n_keys, H * n_rows), F32),
            ((res_count, n_seq, n_rows, C), F32),
            ((res_count, n_seq, n_rows, 2 * C), F32),
            ((n_seq, n_rows, C), F32),
            ((n_seq, n_rows, C), F32),
        ],
        sent, *[shift_residues(sent, away, res_count) for away in away_range],
        alignment, cotangent, norm_gains, row_project, row_output, own_unit, query_gate, query_heads, own_memory, pair_bias,
        present,
        scratch=[pltpu.VMEM((res_count, n_rows, C), F32)],
        name="row_forward",
    )
    arrived = swap_blocks(payload)
    (returned,) = call(
        functools.partial(column_step, n_seq=n_seq),
        [((seq_count, 3, block, 2 * C), F32)],
        arrived, norm_gains, column_project, column_output,
        scratch=[pltpu.VMEM((seq_count, group, 2 * C), F32), pltpu.VMEM((seq_count, group, C), F32)],
        name="column_step",
    )
    returned = swap_blocks(returned)
    part = -(-5 * C // (2 * ROWS * res_count)) * ROWS
    keys_each = n_keys // seq_count
    tiles = H * n_rows // LANES
    left = seq_count // 2 * tiles
    bias_grad, middle_grad, *sums = call(
        functools.partial(row_backward, res_count),
        [((n_keys, H * n_rows), F32), ((n_seq, n_rows, C), F32)]
        + [((part + ROWS + n_rows, LANES), F32)] * res_count,
        returned, exponent, unit, memory, query_gate, query_heads, mixture, inverse, own_unit, row_project, row_output,
        scratch=[pltpu.VMEM((res_count, part + ROWS + n_rows, LANES), F32)],
        name="row_backward",
    )
    sums = sums[:1] + [shift_residues(sums[away], -away, res_count) for away in away_range]
    state, send = call(
        split_blocks, [((left, keys_each, LANES), F32)] * 2, bias_grad, name="split_blocks"
    )
    part_tiles = part // ROWS
    send, normed = call(
        add_shares,
        [((left + part_tiles + 1, ROWS, LANES), F32), ((n_rows, LANES), F32)],
        send, *sums,
        name="add_shares",
    )
    grad_alignment, done = call(
        finish_alignment,
        [(alignment.shape, alignment.dtype), ((ROWS, LANES), F32)],
        alignment, middle_grad, norm_gains, normed,
        name="finish_alignment",
    )
    steps = seq_count.bit_length() - 1
    for at in range(steps):
        arrived = cross(send, at, seq_count, res_count)
        if at < steps - 1:
            left //= 2
            state, send = call(
                functools.partial(step, part_tiles, at == 0),
                [((left, ROWS, LANES), F32), ((left + part_tiles + (1 << at), ROWS, LANES), F32)],
                state, send, arrived,
                name="step",
            )
    (shared,) = call(
        functools.partial(last_step, part_tiles),
        [((part_tiles + seq_count // 2, ROWS, LANES), F32)],
        send, arrived, done,
        unread=1,
        name="last_step",
    )
    (bias_grad,) = call(bias_last, [((H, keys_each, n_rows), F32)], state, arrived, name="bias_last")
    grads = call(
        functools.partial(unpack, res_count, part_tiles),
        [((2, C), F32), ((C, 4 * C), F32), ((C, C), F32), ((C, 2 * C + 2 * DH), F32), ((C, C), F32)],
        shared, *[shift_residues(shared, away, res_count) for away in away_range],
        norm_gains, row_project, column_project,
        scratch=[
            pltpu.VMEM((res_count, part_tiles + seq_count // 2, ROWS, LANES), F32),
            pltpu.VMEM((2, C, LANES), F32),
        ],
        name="unpack",
    )
    return (grad_alignment, jnp.transpose(bias_grad, (0, 2, 1)), *grads)


def solution(mesh):
    placed = (
        P("seq", "res", None),
        P("seq", "res", None),
        P(None, "res", None),
        P(),
        P(),
        P(),
        P(),
        P(),
        P("res"),
        P("seq"),
    )
    return jax.shard_map(
        functools.partial(local, seq_count=mesh.shape["seq"], res_count=mesh.shape["res"]),
        mesh=mesh,
        in_specs=placed,
        out_specs=(P("seq", "res", None), P(None, "res", "seq"), P(), P(), P(), P(), P()),
        check_vma=False,
    )
```
